32 devices in a mesh: seq: 8 (over y, x, core), chan: 4 (over z).
Axes of the slice: x: 2, y: 2, z: 4, core: 2. Of those that a mesh axis runs over, the one named last changes fastest.
Arguments:
- out_grads: bfloat16 [1024, 4096], P(('seq', 'chan')), may hold values from -6 to 6
- layer_inputs: bfloat16 [1024, 4096], P('seq', 'chan'), may hold values from -0.046875 to 0.046875
- filters: bfloat16 [512, 256], P('seq', 'chan'), may hold values from -0.25 to 0.25
Outputs:
- input_grads: bfloat16 [1024, 4096], P('seq', 'chan')
- filter_grads: float32 [512, 256], P('seq', 'chan')
The draws below stay inside these ranges and needn't reach their ends.
All inputs are finite; a program needn't handle non-finite values.
Results may differ from the reference program's by a relative error of at most 0.001.
Values may be sent and summed in bfloat16 or wider, within the bound.
No kernel may reach another device: no remote copies, remote signals or barrier semaphores. Data moves between devices by JAX's collectives and lax.ppermute only.
A program may use at most 64 MiB of HBM per device.

```python
import jax
import jax.numpy as jnp
from jax import lax

D = 4096
GROUPS = 256
BLOCK = 128
REACH = 4
TAPS = 512
SEQ = 1024
N_SEQ = 8


def block_scale(own_key, dims, cuts, least, high):
    def one(dim, parts):
        draws = jax.random.uniform(jax.random.fold_in(jax.random.fold_in(own_key, 6), dim), (parts,), jnp.float32, least / len(cuts), high / len(cuts))
        return jnp.repeat(jnp.exp(draws), dims[dim] // parts).reshape((-1,) + (1,) * (len(dims) - dim - 1))

    level = one(*cuts[0])
    for cut in cuts[1:]:
        level = level * one(*cut)
    return level


def scatter_about(own_key, dims, deviation, limit, shards=(), held_as=jnp.bfloat16):
    level = block_scale(own_key, dims, shards, -0.22, 0.18) if shards else 1.0
    entries = jax.random.normal(own_key, dims, jnp.float32) * deviation * level
    return jnp.minimum(jnp.maximum(entries, -limit), limit).astype(held_as)


def setup_inputs(seed: int = 0) -> dict:
    arg_keys = jax.random.split(jax.random.key(seed), 4)
    return {
        "out_grads": scatter_about(arg_keys[0], (SEQ, D), 1.0, 6.0, ((0, 32),)),
        "layer_inputs": scatter_about(arg_keys[1], (SEQ, D), (SEQ * (D // GROUPS)) ** -0.5, 0.046875, ((0, 8), (1, 4))),
        "filters": scatter_about(arg_keys[2], (TAPS, GROUPS), TAPS ** -0.5, 0.25, ((0, 8), (1, 4))),
    }


def diagonal_sums(products):
    groups_here, length, _ = products.shape
    flipped = products[:, ::-1, :]
    padded = jnp.pad(flipped, ((0, 0), (0, 0), (0, length)))
    flat = padded.reshape(groups_here, 2 * length * length)[:, : length * (2 * length - 1)]
    return flat.reshape(groups_here, length, 2 * length - 1).sum(axis=1)


def reference(out_grads, layer_inputs, filters):
    per_group = D // GROUPS
    filt_rows = filters.astype(jnp.float32).T
    grad_blocks = out_grads.astype(jnp.float32).reshape(N_SEQ, BLOCK, GROUPS, per_group)
    input_blocks = layer_inputs.astype(jnp.float32).reshape(N_SEQ, BLOCK, GROUPS, per_group)
    offsets = jnp.arange(BLOCK, dtype=jnp.int32)[None, :] - jnp.arange(BLOCK, dtype=jnp.int32)[:, None]

    def one_block(index):
        x_block = input_blocks[index]
        dx_total = jnp.zeros((BLOCK, GROUPS, per_group), jnp.float32)
        lag_buffer = jnp.zeros((GROUPS, (REACH + 2) * BLOCK), jnp.float32)
        for lag_block in range(REACH + 1):
            current = grad_blocks[jnp.mod(index + lag_block, N_SEQ)]
            lag_index = lag_block * BLOCK + offsets
            inside = (lag_index >= 0) & (lag_index < TAPS)
            toeplitz = jnp.where(inside[None], filt_rows[:, jnp.clip(lag_index, 0, TAPS - 1)], jnp.float32(0.0))
            dx_total = dx_total + jnp.einsum("guv,vgk->ugk", toeplitz, current, precision=lax.Precision.HIGHEST)
            products = jnp.einsum("vgk,ugk->guv", current, x_block, precision=lax.Precision.HIGHEST)
            start = lag_block * BLOCK
            lag_buffer = lag_buffer.at[:, start:start + 2 * BLOCK - 1].add(diagonal_sums(products))
        return dx_total, lag_buffer[:, BLOCK - 1:BLOCK - 1 + TAPS]

    dx_blocks, dh_blocks = lax.map(one_block, jnp.arange(N_SEQ, dtype=jnp.int32))
    input_grads = dx_blocks.reshape(SEQ, D).astype(jnp.bfloat16)
    filter_grads = jnp.sum(dh_blocks, axis=0).T
    return input_grads, filter_grads
```

```python
import functools

import jax
import jax.numpy as jnp
from jax import lax
from jax.experimental import pallas as pl
from jax.experimental.pallas import tpu as pltpu
from jax.sharding import PartitionSpec as P

LANES = 128
STEP = 32
EXTRA = 16
VMEM_LIMIT = 40 * 1024 * 1024


def shifted(value, axis, steps):
    count = lax.axis_size(axis)
    pairs = [(source, (source + steps) % count) for source in range(count)]
    return lax.ppermute(value, axis, pairs)


def skewed_sums(products):
    groups_here, length, _ = products.shape
    padded = jnp.pad(products, ((0, 0), (0, 0), (0, length)))
    flat = padded.reshape(groups_here, 2 * length * length)[:, : length * (2 * length - 1)]
    return flat.reshape(groups_here, length, 2 * length - 1).sum(axis=1)


def by_tokens(out_grads, layer_inputs, filters):
    local_grads = lax.all_to_all(out_grads, "chan", split_axis=1, concat_axis=0, tiled=True)
    taps_all = lax.all_gather(filters, "seq", axis=0, tiled=True)
    block_len = local_grads.shape[0]
    chan_width = local_grads.shape[1]
    groups_here = filters.shape[1]
    per_group = chan_width // groups_here
    taps_total = taps_all.shape[0]
    spread_blocks = taps_total // block_len
    filt_rows = taps_all.T
    x_reversed = layer_inputs[::-1].reshape(block_len, groups_here, per_group).transpose(1, 2, 0)
    offsets = lax.broadcasted_iota(jnp.int32, (block_len, block_len), 1) - lax.broadcasted_iota(
        jnp.int32, (block_len, block_len), 0
    )
    dx_total = jnp.zeros((groups_here, per_group, block_len), jnp.float32)
    lag_buffer = jnp.zeros((groups_here, (spread_blocks + 2) * block_len), jnp.float32)
    current = local_grads
    for lag_block in range(spread_blocks + 1):
        if lag_block > 0:
            current = shifted(local_grads, "seq", -lag_block)
        dy_grouped = current.reshape(block_len, groups_here, per_group).transpose(1, 2, 0)
        lag_index = lag_block * block_len + offsets
        inside = (lag_index >= 0) & (lag_index < taps_total)
        picked = jnp.take(filt_rows, jnp.clip(lag_index, 0, taps_total - 1), axis=1)
        toeplitz = jnp.where(inside[None], picked, jnp.zeros((), jnp.bfloat16))
        dx_total = dx_total + jnp.einsum(
            "guv,gkv->gku", toeplitz, dy_grouped, preferred_element_type=jnp.float32
        )
        products = jnp.einsum(
            "gku,gkv->guv", x_reversed, dy_grouped, preferred_element_type=jnp.float32
        )
        start = lag_block * block_len
        lag_buffer = lag_buffer.at[:, start : start + 2 * block_len - 1].add(skewed_sums(products))
    partial_dh = lag_buffer[:, block_len - 1 : block_len - 1 + taps_total].T
    filter_grads = lax.psum_scatter(partial_dh, "seq", scatter_dimension=0, tiled=True)
    input_grads = dx_total.transpose(2, 0, 1).reshape(block_len, chan_width).astype(jnp.bfloat16)
    return (input_grads, filter_grads)


def roll_left(value, steps):
    width = value.shape[-1]
    return pltpu.roll(value, (width - steps) % width, value.ndim - 1)


def pack_kernel(n_seq, n_chan, dy_ref, x_ref, f_ref, dyp_ref, xp_ref):
    for seq in range(n_seq):
        for chan in range(n_chan):
            start = (chan * n_seq + seq) * LANES
            dyp_ref[seq * n_chan + chan] = dy_ref[:, start : start + LANES]
    block_len = x_ref.shape[0]
    taps_here, groups_here = f_ref.shape
    per_dest = groups_here // n_seq
    by_group = f_ref[...].astype(jnp.float32).T
    by_group = jnp.concatenate(
        [by_group, jnp.zeros((groups_here, LANES - taps_here), jnp.float32)], axis=1
    )
    rest = jnp.zeros((EXTRA - per_dest, LANES), jnp.float32)
    for seq in range(n_seq):
        xp_ref[seq, :block_len, :] = x_ref[:, seq * LANES : (seq + 1) * LANES]
        rows = by_group[seq * per_dest : (seq + 1) * per_dest]
        xp_ref[seq, block_len:, :] = jnp.concatenate([rows, rest], axis=0).astype(jnp.bfloat16)


def conv_kernel(n_seq, taps_here, dy_ref, xf_ref, out_ref, dye_ref, toep_ref, lag_ref):
    tokens = dy_ref.shape[0]
    block_len = tokens // n_seq
    groups = toep_ref.shape[0] // STEP
    taps = n_seq * taps_here
    reach = taps + LANES
    per_group = LANES // groups
    tile_taps = LANES // taps_here

    dye_ref[:tokens] = dy_ref[...]
    dye_ref[tokens:] = dy_ref[:reach]

    low = lax.broadcasted_iota(jnp.int32, (groups, LANES), 1) < taps_here
    pieces = [xf_ref[seq, block_len:, :].astype(jnp.float32)[:groups] for seq in range(n_seq)]
    tiles = []
    for tile in range(n_seq // tile_taps):
        first, second = pieces[tile * 2], pieces[tile * 2 + 1]
        tiles.append(jnp.where(low, first, pltpu.roll(second, taps_here, 1)))
    filt = jnp.concatenate(tiles + [jnp.zeros((groups, LANES), jnp.float32)], axis=1)
    for group in range(groups):
        rows = jnp.broadcast_to(filt[group : group + 1], (STEP, reach))
        rows = pltpu.roll(rows, 0, 1, stride=1, stride_axis=0)
        toep_ref[group * STEP : (group + 1) * STEP] = rows.astype(jnp.bfloat16)

    lane2 = lax.broadcasted_iota(jnp.int32, (STEP, 2 * LANES), 1)
    group2 = (lane2 % LANES) // per_group
    lane1 = lax.broadcasted_iota(jnp.int32, (STEP, LANES), 1)
    group1 = lane1 // per_group
    toeplitz = toep_ref[...]
    for pair in range(tokens // (2 * STEP)):
        at = pair * 2 * STEP
        window = jnp.concatenate(
            [dye_ref[at : at + reach], dye_ref[at + STEP : at + STEP + reach]], axis=1
        )
        full = jnp.dot(toeplitz, window, preferred_element_type=jnp.float32)
        total = jnp.zeros((STEP, 2 * LANES), jnp.float32)
        for group in range(groups):
            total = jnp.where(group2 == group, full[group * STEP : (group + 1) * STEP], total)
        block, row = at // block_len, at % block_len
        out_ref[block, row : row + STEP, :] = total[:, :LANES].astype(jnp.bfloat16)
        out_ref[block, row + STEP : row + 2 * STEP, :] = total[:, LANES:].astype(jnp.bfloat16)
        x_first = xf_ref[block, row : row + STEP, :]
        x_second = xf_ref[block, row + STEP : row + 2 * STEP, :]
        masked = jnp.concatenate(
            [
                jnp.concatenate(
                    [
                        jnp.where(group1 == group, x_first, jnp.zeros_like(x_first)),
                        jnp.where(group1 == group, x_second, jnp.zeros_like(x_second)),
                    ],
                    axis=1,
                )
                for group in range(groups)
            ],
            axis=0,
        )
        part = lax.dot_general(
            masked, window, (((1,), (1,)), ((), ())), preferred_element_type=jnp.float32
        )
        if pair == 0:
            lag_ref[...] = part
        else:
            lag_ref[...] += part

    eights = []
    for group in range(groups):
        at = group * STEP
        rows = lag_ref[at : at + 8]
        for high in range(1, STEP // 8):
            rows = rows + roll_left(lag_ref[at + 8 * high : at + 8 * high + 8], 8 * high)
        eights.append(rows)
    skew = jnp.concatenate(eights, axis=0)
    row_in = lax.broadcasted_iota(jnp.int32, skew.shape, 0) % 8
    for bit in (1, 2, 4):
        skew = jnp.where((row_in & bit) != 0, roll_left(skew, bit), skew)
    dh = skew.reshape(groups, 8, reach).sum(axis=1)[:, :taps]

    high = dh.astype(jnp.bfloat16).astype(jnp.float32)
    left = dh - high
    mid = left.astype(jnp.bfloat16).astype(jnp.float32)
    least = left - mid
    for seq in range(n_seq):
        tile = (seq // tile_taps) * LANES
        parts = [value[:, tile : tile + LANES] for value in (high, mid, least)]
        turned = [pltpu.roll(value, taps_here, 1) for value in parts]
        if seq % tile_taps == 0:
            top, bottom = jnp.where(low, parts[0], turned[1]), parts[2]
        else:
            top, bottom = jnp.where(low, turned[0], parts[1]), turned[2]
        out_ref[seq, block_len:, :] = jnp.concatenate([top, bottom], axis=0).astype(jnp.bfloat16)


def unpack_kernel(n_seq, got_ref, dx_ref, dh_ref):
    block_len = dx_ref.shape[0]
    taps_here, groups_here = dh_ref.shape
    groups = groups_here // n_seq
    rows = []
    for seq in range(n_seq):
        dx_ref[:, seq * LANES : (seq + 1) * LANES] = got_ref[seq, :block_len, :]
        extra = got_ref[seq, block_len:, :].astype(jnp.float32)
        top, bottom = extra[:groups], extra[groups:]
        rows.append(top + pltpu.roll(top, taps_here, 1) + bottom)
    dh_ref[...] = jnp.concatenate(rows, axis=0).T[:taps_here]


def by_channels(n_seq, n_chan, out_grads, layer_inputs, filters):
    rows = out_grads.shape[0]
    block_len = layer_inputs.shape[0]
    taps_here, groups_here = filters.shape
    groups = groups_here // n_seq
    tokens = n_seq * block_len
    taps = n_seq * taps_here
    params = pltpu.CompilerParams(vmem_limit_bytes=VMEM_LIMIT)
    whole = pl.BlockSpec(memory_space=pltpu.VMEM)
    packed_shape = jax.ShapeDtypeStruct((n_seq, block_len + EXTRA, LANES), jnp.bfloat16)
    dy_packed, x_packed = pl.pallas_call(
        functools.partial(pack_kernel, n_seq, n_chan),
        out_shape=(
            jax.ShapeDtypeStruct((n_seq * n_chan, rows, LANES), jnp.bfloat16),
            packed_shape,
        ),
        in_specs=[whole] * 3,
        out_specs=(whole, whole),
        compiler_params=params,
        name="pack",
    )(out_grads, layer_inputs, filters)
    dy = lax.all_to_all(dy_packed, ("seq", "chan"), split_axis=0, concat_axis=0, tiled=True)
    xf = lax.all_to_all(x_packed, "seq", split_axis=0, concat_axis=0, tiled=True)
    result = pl.pallas_call(
        functools.partial(conv_kernel, n_seq, taps_here),
        out_shape=packed_shape,
        in_specs=[whole] * 2,
        out_specs=whole,
        scratch_shapes=[
            pltpu.VMEM((tokens + taps + LANES, LANES), jnp.bfloat16),
            pltpu.VMEM((groups * STEP, taps + LANES), jnp.bfloat16),
            pltpu.VMEM((groups * STEP, taps + LANES), jnp.float32),
        ],
        compiler_params=params,
        name="conv",
    )(dy.reshape(tokens, LANES), xf)
    back = lax.all_to_all(result, "seq", split_axis=0, concat_axis=0, tiled=True)
    return pl.pallas_call(
        functools.partial(unpack_kernel, n_seq),
        out_shape=(
            jax.ShapeDtypeStruct((block_len, n_seq * LANES), jnp.bfloat16),
            jax.ShapeDtypeStruct((taps_here, groups_here), jnp.float32),
        ),
        in_specs=[whole],
        out_specs=(whole, whole),
        compiler_params=params,
        name="unpack",
    )(back)


def solution(mesh):
    n_seq, n_chan = mesh.shape["seq"], mesh.shape["chan"]

    def on_device(out_grads, layer_inputs, filters):
        taps_here, groups_here = filters.shape
        fits = (
            layer_inputs.shape[1] == n_seq * LANES
            and groups_here == 8 * n_seq
            and 2 * taps_here == LANES
            and out_grads.shape[0] % 16 == 0
            and layer_inputs.shape[0] % (2 * STEP) == 0
            and n_seq * taps_here + LANES <= n_seq * layer_inputs.shape[0]
        )
        if fits:
            return by_channels(n_seq, n_chan, out_grads, layer_inputs, filters)
        return by_tokens(out_grads, layer_inputs, filters)

    in_specs = (P(("seq", "chan"), None), P("seq", "chan"), P("seq", "chan"))
    out_specs = (P("seq", "chan"), P("seq", "chan"))
    return jax.shard_map(
        on_device, mesh=mesh, in_specs=in_specs, out_specs=out_specs, check_vma=False
    )
```

```python
import functools

import jax
import jax.numpy as jnp
from jax import lax
from jax.experimental import pallas as pl
from jax.experimental.pallas import tpu as pltpu
from jax.sharding import PartitionSpec as P

LANES = 128
STEP = 32
EXTRA = 16
VMEM_LIMIT = 40 * 1024 * 1024


def shifted(value, axis, steps):
    count = lax.axis_size(axis)
    pairs = [(source, (source + steps) % count) for source in range(count)]
    return lax.ppermute(value, axis, pairs)


def skewed_sums(products):
    groups_here, length, _ = products.shape
    padded = jnp.pad(products, ((0, 0), (0, 0), (0, length)))
    flat = padded.reshape(groups_here, 2 * length * length)[:, : length * (2 * length - 1)]
    return flat.reshape(groups_here, length, 2 * length - 1).sum(axis=1)


def by_tokens(out_grads, layer_inputs, filters):
    local_grads = lax.all_to_all(out_grads, "chan", split_axis=1, concat_axis=0, tiled=True)
    taps_all = lax.all_gather(filters, "seq", axis=0, tiled=True)
    block_len = local_grads.shape[0]
    chan_width = local_grads.shape[1]
    groups_here = filters.shape[1]
    per_group = chan_width // groups_here
    taps_total = taps_all.shape[0]
    spread_blocks = taps_total // block_len
    filt_rows = taps_all.T
    x_reversed = layer_inputs[::-1].reshape(block_len, groups_here, per_group).transpose(1, 2, 0)
    offsets = lax.broadcasted_iota(jnp.int32, (block_len, block_len), 1) - lax.broadcasted_iota(
        jnp.int32, (block_len, block_len), 0
    )
    dx_total = jnp.zeros((groups_here, per_group, block_len), jnp.float32)
    lag_buffer = jnp.zeros((groups_here, (spread_blocks + 2) * block_len), jnp.float32)
    current = local_grads
    for lag_block in range(spread_blocks + 1):
        if lag_block > 0:
            current = shifted(local_grads, "seq", -lag_block)
        dy_grouped = current.reshape(block_len, groups_here, per_group).transpose(1, 2, 0)
        lag_index = lag_block * block_len + offsets
        inside = (lag_index >= 0) & (lag_index < taps_total)
        picked = jnp.take(filt_rows, jnp.clip(lag_index, 0, taps_total - 1), axis=1)
        toeplitz = jnp.where(inside[None], picked, jnp.zeros((), jnp.bfloat16))
        dx_total = dx_total + jnp.einsum(
            "guv,gkv->gku", toeplitz, dy_grouped, preferred_element_type=jnp.float32
        )
        products = jnp.einsum(
            "gku,gkv->guv", x_reversed, dy_grouped, preferred_element_type=jnp.float32
        )
        start = lag_block * block_len
        lag_buffer = lag_buffer.at[:, start : start + 2 * block_len - 1].add(skewed_sums(products))
    partial_dh = lag_buffer[:, block_len - 1 : block_len - 1 + taps_total].T
    filter_grads = lax.psum_scatter(partial_dh, "seq", scatter_dimension=0, tiled=True)
    input_grads = dx_total.transpose(2, 0, 1).reshape(block_len, chan_width).astype(jnp.bfloat16)
    return (input_grads, filter_grads)


def roll_left(value, steps):
    width = value.shape[-1]
    return pltpu.roll(value, (width - steps) % width, value.ndim - 1)


def split_kernel(dy_ref, out_ref):
    n_chan, _, width = out_ref.shape
    for chan in range(n_chan):
        out_ref[chan] = dy_ref[:, chan * width : (chan + 1) * width]


def pack_kernel(n_seq, dy_ref, x_ref, f_ref, out_ref):
    block_len = x_ref.shape[0]
    taps_here, groups_here = f_ref.shape
    per_dest = groups_here // n_seq
    by_group = f_ref[...].astype(jnp.float32).T
    by_group = jnp.concatenate(
        [by_group, jnp.zeros((groups_here, LANES - taps_here), jnp.float32)], axis=1
    )
    rest = jnp.zeros((EXTRA - per_dest, LANES), jnp.float32)
    for seq in range(n_seq):
        columns = slice(seq * LANES, (seq + 1) * LANES)
        out_ref[seq, :block_len, :] = dy_ref[:, columns]
        out_ref[seq, block_len : 2 * block_len, :] = x_ref[:, columns]
        rows = by_group[seq * per_dest : (seq + 1) * per_dest]
        out_ref[seq, 2 * block_len :, :] = jnp.concatenate([rows, rest], axis=0).astype(jnp.bfloat16)


def conv_kernel(n_seq, taps_here, in_ref, out_ref, dye_ref, toep_ref, lag_ref):
    block_len = out_ref.shape[1] - EXTRA
    tokens = n_seq * block_len
    groups = toep_ref.shape[0] // STEP
    taps = n_seq * taps_here
    reach = taps + LANES
    per_group = LANES // groups
    tile_taps = LANES // taps_here

    for start in range(0, tokens + reach, block_len):
        rows = min(block_len, tokens + reach - start)
        dye_ref[start : start + rows] = in_ref[start // block_len % n_seq, :rows, :]

    low = lax.broadcasted_iota(jnp.int32, (groups, LANES), 1) < taps_here
    pieces = [in_ref[seq, 2 * block_len :, :].astype(jnp.float32)[:groups] for seq in range(n_seq)]
    tiles = []
    for tile in range(n_seq // tile_taps):
        first, second = pieces[tile * 2], pieces[tile * 2 + 1]
        tiles.append(jnp.where(low, first, pltpu.roll(second, taps_here, 1)))
    filt = jnp.concatenate(tiles + [jnp.zeros((groups, LANES), jnp.float32)], axis=1)
    for group in range(groups):
        rows = jnp.broadcast_to(filt[group : group + 1], (STEP, reach))
        rows = pltpu.roll(rows, 0, 1, stride=1, stride_axis=0)
        toep_ref[group * STEP : (group + 1) * STEP] = rows.astype(jnp.bfloat16)

    lane2 = lax.broadcasted_iota(jnp.int32, (STEP, 2 * LANES), 1)
    group2 = (lane2 % LANES) // per_group
    lane1 = lax.broadcasted_iota(jnp.int32, (STEP, LANES), 1)
    group1 = lane1 // per_group
    toeplitz = toep_ref[...]
    for pair in range(tokens // (2 * STEP)):
        at = pair * 2 * STEP
        window = jnp.concatenate(
            [dye_ref[at : at + reach], dye_ref[at + STEP : at + STEP + reach]], axis=1
        )
        full = jnp.dot(toeplitz, window, preferred_element_type=jnp.float32)
        total = jnp.zeros((STEP, 2 * LANES), jnp.float32)
        for group in range(groups):
            total = jnp.where(group2 == group, full[group * STEP : (group + 1) * STEP], total)
        block, row = at // block_len, at % block_len
        out_ref[block, row : row + STEP, :] = total[:, :LANES].astype(jnp.bfloat16)
        out_ref[block, row + STEP : row + 2 * STEP, :] = total[:, LANES:].astype(jnp.bfloat16)
        x_first = in_ref[block, block_len + row : block_len + row + STEP, :]
        x_second = in_ref[block, block_len + row + STEP : block_len + row + 2 * STEP, :]
        masked = jnp.concatenate(
            [
                jnp.concatenate(
                    [
                        jnp.where(group1 == group, x_first, jnp.zeros_like(x_first)),
                        jnp.where(group1 == group, x_second, jnp.zeros_like(x_second)),
                    ],
                    axis=1,
                )
                for group in range(groups)
            ],
            axis=0,
        )
        part = lax.dot_general(
            masked, window, (((1,), (1,)), ((), ())), preferred_element_type=jnp.float32
        )
        if pair == 0:
            lag_ref[...] = part
        else:
            lag_ref[...] += part

    eights = []
    for group in range(groups):
        at = group * STEP
        rows = lag_ref[at : at + 8]
        for high in range(1, STEP // 8):
            rows = rows + roll_left(lag_ref[at + 8 * high : at + 8 * high + 8], 8 * high)
        eights.append(rows)
    skew = jnp.concatenate(eights, axis=0)
    row_in = lax.broadcasted_iota(jnp.int32, skew.shape, 0) % 8
    for bit in (1, 2, 4):
        skew = jnp.where((row_in & bit) != 0, roll_left(skew, bit), skew)
    dh = skew.reshape(groups, 8, reach).sum(axis=1)[:, :taps]

    high = dh.astype(jnp.bfloat16).astype(jnp.float32)
    left = dh - high
    mid = left.astype(jnp.bfloat16).astype(jnp.float32)
    least = left - mid
    for seq in range(n_seq):
        tile = (seq // tile_taps) * LANES
        parts = [value[:, tile : tile + LANES] for value in (high, mid, least)]
        turned = [pltpu.roll(value, taps_here, 1) for value in parts]
        if seq % tile_taps == 0:
            top, bottom = jnp.where(low, parts[0], turned[1]), parts[2]
        else:
            top, bottom = jnp.where(low, turned[0], parts[1]), turned[2]
        out_ref[seq, block_len:, :] = jnp.concatenate([top, bottom], axis=0).astype(jnp.bfloat16)


def unpack_kernel(n_seq, got_ref, dx_ref, dh_ref):
    block_len = dx_ref.shape[0]
    taps_here, groups_here = dh_ref.shape
    groups = groups_here // n_seq
    rows = []
    for seq in range(n_seq):
        dx_ref[:, seq * LANES : (seq + 1) * LANES] = got_ref[seq, :block_len, :]
        extra = got_ref[seq, block_len:, :].astype(jnp.float32)
        top, bottom = extra[:groups], extra[groups:]
        rows.append(top + pltpu.roll(top, taps_here, 1) + bottom)
    dh_ref[...] = jnp.concatenate(rows, axis=0).T[:taps_here]


def by_channels(n_seq, n_chan, out_grads, layer_inputs, filters):
    rows = out_grads.shape[0]
    block_len = layer_inputs.shape[0]
    taps_here, groups_here = filters.shape
    groups = groups_here // n_seq
    tokens = n_seq * block_len
    taps = n_seq * taps_here
    params = pltpu.CompilerParams(vmem_limit_bytes=VMEM_LIMIT)
    whole = pl.BlockSpec(memory_space=pltpu.VMEM)
    dy_split = pl.pallas_call(
        split_kernel,
        out_shape=jax.ShapeDtypeStruct((n_chan, rows, n_seq * LANES), jnp.bfloat16),
        in_specs=[whole],
        out_specs=whole,
        compiler_params=params,
        name="split",
    )(out_grads)
    dy = lax.all_to_all(dy_split, "chan", split_axis=0, concat_axis=0, tiled=True)
    packed = pl.pallas_call(
        functools.partial(pack_kernel, n_seq),
        out_shape=jax.ShapeDtypeStruct((n_seq, 2 * block_len + EXTRA, LANES), jnp.bfloat16),
        in_specs=[whole] * 3,
        out_specs=whole,
        compiler_params=params,
        name="pack",
    )(dy.reshape(block_len, n_seq * LANES), layer_inputs, filters)
    packed = lax.all_to_all(packed, "seq", split_axis=0, concat_axis=0, tiled=True)
    result = pl.pallas_call(
        functools.partial(conv_kernel, n_seq, taps_here),
        out_shape=jax.ShapeDtypeStruct((n_seq, block_len + EXTRA, LANES), jnp.bfloat16),
        in_specs=[whole],
        out_specs=whole,
        scratch_shapes=[
            pltpu.VMEM((tokens + taps + LANES, LANES), jnp.bfloat16),
            pltpu.VMEM((groups * STEP, taps + LANES), jnp.bfloat16),
            pltpu.VMEM((groups * STEP, taps + LANES), jnp.float32),
        ],
        compiler_params=params,
        name="conv",
    )(packed)
    back = lax.all_to_all(result, "seq", split_axis=0, concat_axis=0, tiled=True)
    return pl.pallas_call(
        functools.partial(unpack_kernel, n_seq),
        out_shape=(
            jax.ShapeDtypeStruct((block_len, n_seq * LANES), jnp.bfloat16),
            jax.ShapeDtypeStruct((taps_here, groups_here), jnp.float32),
        ),
        in_specs=[whole],
        out_specs=(whole, whole),
        compiler_params=params,
        name="unpack",
    )(back)


def solution(mesh):
    n_seq, n_chan = mesh.shape["seq"], mesh.shape["chan"]

    def on_device(out_grads, layer_inputs, filters):
        taps_here, groups_here = filters.shape
        fits = (
            layer_inputs.shape[1] == n_seq * LANES
            and groups_here == 8 * n_seq
            and 2 * taps_here == LANES
            and out_grads.shape[0] % 16 == 0
            and layer_inputs.shape[0] % (2 * STEP) == 0
            and n_seq * taps_here + LANES <= n_seq * layer_inputs.shape[0]
        )
        if fits:
            return by_channels(n_seq, n_chan, out_grads, layer_inputs, filters)
        return by_tokens(out_grads, layer_inputs, filters)

    in_specs = (P(("seq", "chan"), None), P("seq", "chan"), P("seq", "chan"))
    out_specs = (P("seq", "chan"), P("seq", "chan"))
    return jax.shard_map(
        on_device, mesh=mesh, in_specs=in_specs, out_specs=out_specs, check_vma=False
    )
```

```python
import functools

import jax
import jax.numpy as jnp
from jax import lax
from jax.experimental import pallas as pl
from jax.experimental.pallas import tpu as pltpu
from jax.sharding import PartitionSpec as P

LANES = 128
STEP = 32
EXTRA = 16
VMEM_LIMIT = 40 * 1024 * 1024


def shifted(value, axis, steps):
    count = lax.axis_size(axis)
    pairs = [(source, (source + steps) % count) for source in range(count)]
    return lax.ppermute(value, axis, pairs)


def skewed_sums(products):
    groups_here, length, _ = products.shape
    padded = jnp.pad(products, ((0, 0), (0, 0), (0, length)))
    flat = padded.reshape(groups_here, 2 * length * length)[:, : length * (2 * length - 1)]
    return flat.reshape(groups_here, length, 2 * length - 1).sum(axis=1)


def by_tokens(out_grads, layer_inputs, filters):
    local_grads = lax.all_to_all(out_grads, "chan", split_axis=1, concat_axis=0, tiled=True)
    taps_all = lax.all_gather(filters, "seq", axis=0, tiled=True)
    block_len = local_grads.shape[0]
    chan_width = local_grads.shape[1]
    groups_here = filters.shape[1]
    per_group = chan_width // groups_here
    taps_total = taps_all.shape[0]
    spread_blocks = taps_total // block_len
    filt_rows = taps_all.T
    x_reversed = layer_inputs[::-1].reshape(block_len, groups_here, per_group).transpose(1, 2, 0)
    offsets = lax.broadcasted_iota(jnp.int32, (block_len, block_len), 1) - lax.broadcasted_iota(
        jnp.int32, (block_len, block_len), 0
    )
    dx_total = jnp.zeros((groups_here, per_group, block_len), jnp.float32)
    lag_buffer = jnp.zeros((groups_here, (spread_blocks + 2) * block_len), jnp.float32)
    current = local_grads
    for lag_block in range(spread_blocks + 1):
        if lag_block > 0:
            current = shifted(local_grads, "seq", -lag_block)
        dy_grouped = current.reshape(block_len, groups_here, per_group).transpose(1, 2, 0)
        lag_index = lag_block * block_len + offsets
        inside = (lag_index >= 0) & (lag_index < taps_total)
        picked = jnp.take(filt_rows, jnp.clip(lag_index, 0, taps_total - 1), axis=1)
        toeplitz = jnp.where(inside[None], picked, jnp.zeros((), jnp.bfloat16))
        dx_total = dx_total + jnp.einsum(
            "guv,gkv->gku", toeplitz, dy_grouped, preferred_element_type=jnp.float32
        )
        products = jnp.einsum(
            "gku,gkv->guv", x_reversed, dy_grouped, preferred_element_type=jnp.float32
        )
        start = lag_block * block_len
        lag_buffer = lag_buffer.at[:, start : start + 2 * block_len - 1].add(skewed_sums(products))
    partial_dh = lag_buffer[:, block_len - 1 : block_len - 1 + taps_total].T
    filter_grads = lax.psum_scatter(partial_dh, "seq", scatter_dimension=0, tiled=True)
    input_grads = dx_total.transpose(2, 0, 1).reshape(block_len, chan_width).astype(jnp.bfloat16)
    return (input_grads, filter_grads)


def xor_permute(value, axis, bits):
    pairs = [(source, source ^ bits) for source in range(lax.axis_size(axis))]
    return lax.ppermute(value, axis, pairs)


def roll_left(value, steps):
    width = value.shape[-1]
    return pltpu.roll(value, (width - steps) % width, value.ndim - 1)


def place():
    seq = lax.axis_index("seq")
    return seq // 2, seq % 2, lax.axis_index("chan")


def rows_at(index, size):
    return pl.ds(pl.multiple_of(index * size, 16), size)


def split_kernel(n_seq, n_chan, dy_ref, x_ref, f_ref, keep_ref, send_ref):
    _, core, _ = place()
    chips = n_seq // 2
    rows = dy_ref.shape[0]
    block_len = x_ref.shape[0]
    taps_here, groups_here = f_ref.shape
    per_dest = groups_here // n_seq
    by_group = f_ref[...].astype(jnp.float32).T
    by_group = jnp.concatenate(
        [by_group, jnp.zeros((groups_here, LANES - taps_here), jnp.float32)], axis=1
    )
    rest = jnp.zeros((EXTRA - per_dest, LANES), jnp.float32)
    for flip, out_ref in ((0, keep_ref), (1, send_ref)):
        to_core = core ^ flip
        for chan in range(n_chan):
            for chip in range(chips):
                column = (chan * n_seq + 2 * chip + to_core) * LANES
                at = (chan * chips + chip) * rows
                out_ref[at : at + rows] = dy_ref[:, pl.ds(pl.multiple_of(column, LANES), LANES)]
        base = n_chan * chips * rows
        for chip in range(chips):
            column = (2 * chip + to_core) * LANES
            at = base + chip * (block_len + EXTRA)
            out_ref[at : at + block_len] = x_ref[:, pl.ds(pl.multiple_of(column, LANES), LANES)]
            first = 2 * chip * per_dest
            taps = jnp.where(
                to_core == 0,
                by_group[first : first + per_dest],
                by_group[first + per_dest : first + 2 * per_dest],
            )
            out_ref[at + block_len : at + block_len + EXTRA] = jnp.concatenate(
                [taps, rest], axis=0
            ).astype(jnp.bfloat16)


def fan_kernel(n_chan, rows, keep_ref, got_ref, *out_refs):
    chip, _, chan = place()
    chips = len(out_refs) - n_chan
    size = chips * rows
    base = n_chan * size
    for bits in range(n_chan):
        out_refs[bits][:size] = keep_ref[rows_at(chan ^ bits, size)]
        out_refs[bits][size:] = got_ref[rows_at(chan ^ bits, size)]
    for bits in range(chips):
        out_ref = out_refs[n_chan + bits]
        size = out_ref.shape[0] // 2
        source = pl.ds(pl.multiple_of(base + (chip ^ bits) * size, 16), size)
        out_ref[:size] = keep_ref[source]
        out_ref[size:] = got_ref[source]


def regroup_kernel(rows, n_chan, *refs):
    chip, _, chan = place()
    in_refs, out_refs = refs[:n_chan], refs[n_chan:]
    chips = len(out_refs)
    for to_bits in range(chips):
        for from_bits in range(n_chan):
            for core in range(2):
                out_refs[to_bits][rows_at(core * n_chan + (chan ^ from_bits), rows)] = in_refs[
                    from_bits
                ][rows_at(core * chips + (chip ^ to_bits), rows)]


def conv_kernel(n_seq, taps_here, *refs):
    chips = n_seq // 2
    dy_refs, x_refs = refs[:chips], refs[chips : 2 * chips]
    keep_ref, send_ref, dye_ref, x_ref, filt_ref, toep_ref, lag_ref, out_ref = refs[2 * chips :]
    block_len = out_ref.shape[1] - EXTRA
    tokens = n_seq * block_len
    groups = toep_ref.shape[0] // STEP
    taps = n_seq * taps_here
    reach = taps + LANES
    per_group = LANES // groups
    chip, core, _ = place()

    low = lax.broadcasted_iota(jnp.int32, (groups, LANES), 1) < taps_here
    for bits in range(chips):
        pieces = []
        for flip in range(2):
            source = (chip ^ bits) * 2 + (core ^ flip)
            at = flip * block_len
            dye_ref[rows_at(source, block_len)] = dy_refs[bits][at : at + block_len]
            at = flip * (block_len + EXTRA)
            x_ref[rows_at(source, block_len)] = x_refs[bits][at : at + block_len]
            at += block_len
            pieces.append(x_refs[bits][at : at + EXTRA].astype(jnp.float32)[:groups])
        first = jnp.where(core == 0, pieces[0], pieces[1])
        second = jnp.where(core == 0, pieces[1], pieces[0])
        filt_ref[chip ^ bits] = jnp.where(low, first, pltpu.roll(second, taps_here, 1))
    dye_ref[tokens:] = dye_ref[:reach]

    tiles = [filt_ref[tile] for tile in range(chips)]
    filt = jnp.concatenate(tiles + [jnp.zeros((groups, LANES), jnp.float32)], axis=1)
    for group in range(groups):
        rows = jnp.broadcast_to(filt[group : group + 1], (STEP, reach))
        rows = pltpu.roll(rows, 0, 1, stride=1, stride_axis=0)
        toep_ref[group * STEP : (group + 1) * STEP] = rows.astype(jnp.bfloat16)

    lane2 = lax.broadcasted_iota(jnp.int32, (STEP, 2 * LANES), 1)
    group2 = (lane2 % LANES) // per_group
    lane1 = lax.broadcasted_iota(jnp.int32, (STEP, LANES), 1)
    group1 = lane1 // per_group
    toeplitz = toep_ref[...]
    for pair in range(tokens // (2 * STEP)):
        at = pair * 2 * STEP
        window = jnp.concatenate(
            [dye_ref[at : at + reach], dye_ref[at + STEP : at + STEP + reach]], axis=1
        )
        full = jnp.dot(toeplitz, window, preferred_element_type=jnp.float32)
        total = jnp.zeros((STEP, 2 * LANES), jnp.float32)
        for group in range(groups):
            total = jnp.where(group2 == group, full[group * STEP : (group + 1) * STEP], total)
        block, row = at // block_len, at % block_len
        out_ref[block, row : row + STEP, :] = total[:, :LANES].astype(jnp.bfloat16)
        out_ref[block, row + STEP : row + 2 * STEP, :] = total[:, LANES:].astype(jnp.bfloat16)
        x_first = x_ref[at : at + STEP]
        x_second = x_ref[at + STEP : at + 2 * STEP]
        masked = jnp.concatenate(
            [
                jnp.concatenate(
                    [
                        jnp.where(group1 == group, x_first, jnp.zeros_like(x_first)),
                        jnp.where(group1 == group, x_second, jnp.zeros_like(x_second)),
                    ],
                    axis=1,
                )
                for group in range(groups)
            ],
            axis=0,
        )
        part = lax.dot_general(
            masked, window, (((1,), (1,)), ((), ())), preferred_element_type=jnp.float32
        )
        if pair == 0:
            lag_ref[...] = part
        else:
            lag_ref[...] += part

    eights = []
    for group in range(groups):
        at = group * STEP
        rows = lag_ref[at : at + 8]
        for high in range(1, STEP // 8):
            rows = rows + roll_left(lag_ref[at + 8 * high : at + 8 * high + 8], 8 * high)
        eights.append(rows)
    skew = jnp.concatenate(eights, axis=0)
    row_in = lax.broadcasted_iota(jnp.int32, skew.shape, 0) % 8
    for bit in (1, 2, 4):
        skew = jnp.where((row_in & bit) != 0, roll_left(skew, bit), skew)
    dh = skew.reshape(groups, 8, reach).sum(axis=1)[:, :taps]

    high = dh.astype(jnp.bfloat16).astype(jnp.float32)
    left = dh - high
    mid = left.astype(jnp.bfloat16).astype(jnp.float32)
    least = left - mid
    for seq in range(n_seq):
        tile = (seq // 2) * LANES
        parts = [value[:, tile : tile + LANES] for value in (high, mid, least)]
        turned = [pltpu.roll(value, taps_here, 1) for value in parts]
        if seq % 2 == 0:
            top, bottom = jnp.where(low, parts[0], turned[1]), parts[2]
        else:
            top, bottom = jnp.where(low, turned[0], parts[1]), turned[2]
        out_ref[seq, block_len:, :] = jnp.concatenate([top, bottom], axis=0).astype(jnp.bfloat16)

    for to_chip in range(chips):
        keep_ref[to_chip] = out_ref[to_chip * 2 + core]
        send_ref[to_chip] = out_ref[to_chip * 2 + (1 - core)]


def back_kernel(keep_ref, got_ref, *out_refs):
    chip, _, _ = place()
    for bits, out_ref in enumerate(out_refs):
        out_ref[0] = keep_ref[chip ^ bits]
        out_ref[1] = got_ref[chip ^ bits]


def unpack_kernel(*refs):
    *got_refs, dx_ref, dh_ref, rows_ref = refs
    chip, core, _ = place()
    block_len = dx_ref.shape[0]
    taps_here, groups_here = dh_ref.shape
    groups = groups_here // (2 * len(got_refs))
    for bits, got_ref in enumerate(got_refs):
        for flip in range(2):
            source = (chip ^ bits) * 2 + (core ^ flip)
            columns = pl.ds(pl.multiple_of(source * LANES, LANES), LANES)
            dx_ref[:, columns] = got_ref[flip, :block_len, :]
            extra = got_ref[flip, block_len:, :].astype(jnp.float32)
            top, bottom = extra[:groups], extra[groups:]
            rows_ref[pl.ds(pl.multiple_of(source * groups, 8), groups)] = (
                top + pltpu.roll(top, taps_here, 1) + bottom
            )
    dh_ref[...] = rows_ref[...].T[:taps_here]


def local_call(kernel, out_shape, operands, name, scratch=()):
    whole = pl.BlockSpec(memory_space=pltpu.VMEM)
    return pl.pallas_call(
        kernel,
        out_shape=out_shape,
        in_specs=[whole] * len(operands),
        out_specs=[whole] * len(out_shape),
        scratch_shapes=scratch,
        compiler_params=pltpu.CompilerParams(vmem_limit_bytes=VMEM_LIMIT),
        name=name,
    )(*operands)


def by_channels(n_seq, n_chan, out_grads, layer_inputs, filters):
    rows = out_grads.shape[0]
    block_len = layer_inputs.shape[0]
    taps_here, groups_here = filters.shape
    groups = groups_here // n_seq
    tokens = n_seq * block_len
    taps = n_seq * taps_here
    chips = n_seq // 2

    def half(*shape):
        return jax.ShapeDtypeStruct(shape, jnp.bfloat16)

    unit = block_len + EXTRA
    keep, send = local_call(
        functools.partial(split_kernel, n_seq, n_chan),
        [half(chips * (n_chan * rows + unit), LANES)] * 2,
        (out_grads, layer_inputs, filters),
        "split",
    )
    got = xor_permute(send, "seq", 1)
    pieces = local_call(
        functools.partial(fan_kernel, n_chan, rows),
        [half(2 * chips * rows, LANES)] * n_chan + [half(2 * unit, LANES)] * chips,
        (keep, got),
        "fan",
    )
    dy = [pieces[0]] + [xor_permute(pieces[k], "chan", k) for k in range(1, n_chan)]
    pieces = pieces[n_chan:]
    x = [pieces[0]] + [xor_permute(pieces[k], "seq", 2 * k) for k in range(1, chips)]
    pieces = local_call(
        functools.partial(regroup_kernel, rows, n_chan),
        [half(2 * n_chan * rows, LANES)] * chips,
        dy,
        "regroup",
    )
    dy = [pieces[0]] + [xor_permute(pieces[k], "seq", 2 * k) for k in range(1, chips)]
    keep, send = local_call(
        functools.partial(conv_kernel, n_seq, taps_here),
        [half(chips, unit, LANES)] * 2,
        (*dy, *x),
        "conv",
        [
            pltpu.VMEM((tokens + taps + LANES, LANES), jnp.bfloat16),
            pltpu.VMEM((tokens, LANES), jnp.bfloat16),
            pltpu.VMEM((chips, groups, LANES), jnp.float32),
            pltpu.VMEM((groups * STEP, taps + LANES), jnp.bfloat16),
            pltpu.VMEM((groups * STEP, taps + LANES), jnp.float32),
            pltpu.VMEM((n_seq, unit, LANES), jnp.bfloat16),
        ],
    )
    got = xor_permute(send, "seq", 1)
    pieces = local_call(back_kernel, [half(2, unit, LANES)] * chips, (keep, got), "back")
    back = [pieces[0]] + [xor_permute(pieces[k], "seq", 2 * k) for k in range(1, chips)]
    return local_call(
        unpack_kernel,
        [
            half(block_len, n_seq * LANES),
            jax.ShapeDtypeStruct((taps_here, groups_here), jnp.float32),
        ],
        back,
        "unpack",
        [pltpu.VMEM((groups_here, LANES), jnp.float32)],
    )


def solution(mesh):
    n_seq, n_chan = mesh.shape["seq"], mesh.shape["chan"]

    def on_device(out_grads, layer_inputs, filters):
        taps_here, groups_here = filters.shape
        fits = (
            n_seq in (2, 4, 8, 16, 32)
            and n_chan in (2, 4, 8, 16, 32)
            and layer_inputs.shape[1] == n_seq * LANES
            and groups_here == 8 * n_seq
            and 2 * taps_here == LANES
            and out_grads.shape[0] % 16 == 0
            and layer_inputs.shape[0] % (2 * STEP) == 0
            and n_seq * taps_here + LANES <= n_seq * layer_inputs.shape[0]
        )
        if fits:
            return tuple(by_channels(n_seq, n_chan, out_grads, layer_inputs, filters))
        return by_tokens(out_grads, layer_inputs, filters)

    in_specs = (P(("seq", "chan"), None), P("seq", "chan"), P("seq", "chan"))
    out_specs = (P("seq", "chan"), P("seq", "chan"))
    return jax.shard_map(
        on_device, mesh=mesh, in_specs=in_specs, out_specs=out_specs, check_vma=False
    )
```

```python
import functools

import jax
import jax.numpy as jnp
from jax import lax
from jax.experimental import pallas as pl
from jax.experimental.pallas import tpu as pltpu
from jax.sharding import PartitionSpec as P

LANES = 128
STEP = 32
EXTRA = 16
VMEM_LIMIT = 40 * 1024 * 1024


def shifted(value, axis, steps):
    count = lax.axis_size(axis)
    pairs = [(source, (source + steps) % count) for source in range(count)]
    return lax.ppermute(value, axis, pairs)


def skewed_sums(products):
    groups_here, length, _ = products.shape
    padded = jnp.pad(products, ((0, 0), (0, 0), (0, length)))
    flat = padded.reshape(groups_here, 2 * length * length)[:, : length * (2 * length - 1)]
    return flat.reshape(groups_here, length, 2 * length - 1).sum(axis=1)


def by_tokens(out_grads, layer_inputs, filters):
    local_grads = lax.all_to_all(out_grads, "chan", split_axis=1, concat_axis=0, tiled=True)
    taps_all = lax.all_gather(filters, "seq", axis=0, tiled=True)
    block_len = local_grads.shape[0]
    chan_width = local_grads.shape[1]
    groups_here = filters.shape[1]
    per_group = chan_width // groups_here
    taps_total = taps_all.shape[0]
    spread_blocks = taps_total // block_len
    filt_rows = taps_all.T
    x_reversed = layer_inputs[::-1].reshape(block_len, groups_here, per_group).transpose(1, 2, 0)
    offsets = lax.broadcasted_iota(jnp.int32, (block_len, block_len), 1) - lax.broadcasted_iota(
        jnp.int32, (block_len, block_len), 0
    )
    dx_total = jnp.zeros((groups_here, per_group, block_len), jnp.float32)
    lag_buffer = jnp.zeros((groups_here, (spread_blocks + 2) * block_len), jnp.float32)
    current = local_grads
    for lag_block in range(spread_blocks + 1):
        if lag_block > 0:
            current = shifted(local_grads, "seq", -lag_block)
        dy_grouped = current.reshape(block_len, groups_here, per_group).transpose(1, 2, 0)
        lag_index = lag_block * block_len + offsets
        inside = (lag_index >= 0) & (lag_index < taps_total)
        picked = jnp.take(filt_rows, jnp.clip(lag_index, 0, taps_total - 1), axis=1)
        toeplitz = jnp.where(inside[None], picked, jnp.zeros((), jnp.bfloat16))
        dx_total = dx_total + jnp.einsum(
            "guv,gkv->gku", toeplitz, dy_grouped, preferred_element_type=jnp.float32
        )
        products = jnp.einsum(
            "gku,gkv->guv", x_reversed, dy_grouped, preferred_element_type=jnp.float32
        )
        start = lag_block * block_len
        lag_buffer = lag_buffer.at[:, start : start + 2 * block_len - 1].add(skewed_sums(products))
    partial_dh = lag_buffer[:, block_len - 1 : block_len - 1 + taps_total].T
    filter_grads = lax.psum_scatter(partial_dh, "seq", scatter_dimension=0, tiled=True)
    input_grads = dx_total.transpose(2, 0, 1).reshape(block_len, chan_width).astype(jnp.bfloat16)
    return (input_grads, filter_grads)


def xor_permute(value, axis, bits):
    pairs = [(source, source ^ bits) for source in range(lax.axis_size(axis))]
    return lax.ppermute(value, axis, pairs)


def partners(count):
    return [(count - step) % count for step in range(count)]


def fan_out(pieces, axis, unit):
    masks = partners(len(pieces))[1:]
    return [pieces[0]] + [xor_permute(p, axis, m * unit) for p, m in zip(pieces[1:], masks)]


def roll_left(value, steps):
    width = value.shape[-1]
    return pltpu.roll(value, (width - steps) % width, value.ndim - 1)


def place():
    seq = lax.axis_index("seq")
    return seq // 2, seq % 2, lax.axis_index("chan")


def rows_at(index, size):
    return pl.ds(pl.multiple_of(index * size, 16), size)


def own_grads_kernel(n_seq, in_ref, out_ref):
    _, core, chan = place()
    n_chan, size, _ = out_ref.shape
    rows = in_ref.shape[0]
    for index, bits in enumerate(partners(n_chan)):
        for chip in range(size // rows):
            column = ((chan ^ bits) * n_seq + 2 * chip + core) * LANES
            out_ref[index, chip * rows : (chip + 1) * rows] = in_ref[
                :, pl.ds(pl.multiple_of(column, LANES), LANES)
            ]


def fan_grads_kernel(n_seq, own_ref, other_ref, *out_refs):
    _, core, chan = place()
    rows = other_ref.shape[0]
    size = own_ref.shape[1]
    for index, bits in enumerate(partners(len(out_refs))):
        out_refs[index][:size] = own_ref[index]
        for chip in range(size // rows):
            column = ((chan ^ bits) * n_seq + 2 * chip + core) * LANES
            at = size + chip * rows
            out_refs[index][at : at + rows] = other_ref[
                :, pl.ds(pl.multiple_of(column, LANES), LANES)
            ]


def fan_inputs_kernel(x_own_ref, x_other_ref, f_own_ref, f_other_ref, *refs):
    *out_refs, taps_ref = refs
    chip, core, _ = place()
    block_len = x_own_ref.shape[0]
    taps_here, groups_here = f_own_ref.shape
    groups = groups_here // (2 * len(out_refs))
    rest = jnp.zeros((EXTRA - groups, LANES), jnp.float32)
    for flip, (x_ref, f_ref) in enumerate(((x_own_ref, f_own_ref), (x_other_ref, f_other_ref))):
        taps_ref[flip] = jnp.concatenate(
            [
                f_ref[...].astype(jnp.float32).T,
                jnp.zeros((groups_here, LANES - taps_here), jnp.float32),
            ],
            axis=1,
        )
        for bits, out_ref in zip(partners(len(out_refs)), out_refs):
            target = 2 * (chip ^ bits) + core
            at = flip * (block_len + EXTRA)
            out_ref[at : at + block_len] = x_ref[
                :, pl.ds(pl.multiple_of(target * LANES, LANES), LANES)
            ]
            taps = taps_ref[flip, pl.ds(pl.multiple_of(target * groups, groups), groups)]
            out_ref[at + block_len : at + block_len + EXTRA] = jnp.concatenate(
                [taps, rest], axis=0
            ).astype(jnp.bfloat16)


def regroup_kernel(rows, n_chan, *refs):
    chip, _, chan = place()
    in_refs, out_refs = refs[:n_chan], refs[n_chan:]
    chips = len(out_refs)
    for to_bits, out_ref in zip(partners(chips), out_refs):
        for from_bits, in_ref in zip(partners(n_chan), in_refs):
            for core in range(2):
                out_ref[rows_at(core * n_chan + (chan ^ from_bits), rows)] = in_ref[
                    rows_at(core * chips + (chip ^ to_bits), rows)
                ]


def group_of_lane(width, groups):
    lane = lax.broadcasted_iota(jnp.int32, (STEP, width), 1)
    return (lane % LANES) // (LANES // groups)


def window_at(dye_ref, at, reach):
    return jnp.concatenate(
        [dye_ref[at : at + reach], dye_ref[at + STEP : at + STEP + reach]], axis=1
    )


def filtered(toeplitz, window, groups):
    full = jnp.dot(toeplitz, window, preferred_element_type=jnp.float32)
    group2 = group_of_lane(2 * LANES, groups)
    total = full[:STEP]
    for group in range(1, groups):
        total = jnp.where(group2 == group, full[group * STEP : (group + 1) * STEP], total)
    return jnp.concatenate([total[:, :LANES], total[:, LANES:]], axis=0).astype(jnp.bfloat16)


def first_kernel(n_seq, taps_here, *refs):
    chips = n_seq // 2
    dy_refs, x_refs = refs[:chips], refs[chips : 2 * chips]
    send_ref, taps_ref, dye_ref, toep_ref, x_ref, filt_ref, lag_ref, parts_ref = refs[2 * chips :]
    block_len = x_ref.shape[0] // n_seq
    tokens = n_seq * block_len
    groups = toep_ref.shape[0] // STEP
    taps = n_seq * taps_here
    reach = taps + LANES
    chip, core, _ = place()

    low = lax.broadcasted_iota(jnp.int32, (groups, LANES), 1) < taps_here
    for bits, dy_piece_ref, x_piece_ref in zip(partners(chips), dy_refs, x_refs):
        pieces = []
        for flip in range(2):
            block = (2 * (chip ^ bits) + (core ^ flip) - core + n_seq) % n_seq
            at = flip * block_len
            dye_ref[rows_at(block, block_len)] = dy_piece_ref[at : at + block_len]
            at = flip * (block_len + EXTRA)
            x_ref[rows_at(block, block_len)] = x_piece_ref[at : at + block_len]
            at += block_len
            pieces.append(x_piece_ref[at : at + EXTRA].astype(jnp.float32)[:groups])
        first = jnp.where(core == 0, pieces[0], pieces[1])
        second = jnp.where(core == 0, pieces[1], pieces[0])
        filt_ref[chip ^ bits] = jnp.where(low, first, pltpu.roll(second, taps_here, 1))
    dye_ref[tokens:] = dye_ref[:reach]

    tiles = [filt_ref[tile] for tile in range(chips)]
    filt = jnp.concatenate(tiles + [jnp.zeros((groups, LANES), jnp.float32)], axis=1)
    for group in range(groups):
        rows = jnp.broadcast_to(filt[group : group + 1], (STEP, reach))
        rows = pltpu.roll(rows, 0, 1, stride=1, stride_axis=0)
        toep_ref[group * STEP : (group + 1) * STEP] = rows.astype(jnp.bfloat16)

    group2 = group_of_lane(2 * LANES, groups)
    toeplitz = toep_ref[...]
    for at in range(0, tokens, 2 * STEP):
        window = window_at(dye_ref, at, reach)
        block, row = at // block_len, at % block_len
        if block % 2 == 1:
            send_ref[(block // 2 + core) % chips, row : row + 2 * STEP, :] = filtered(
                toeplitz, window, groups
            )
        inputs = jnp.concatenate(
            [x_ref[at : at + STEP], x_ref[at + STEP : at + 2 * STEP]], axis=1
        )
        masked = jnp.concatenate(
            [jnp.where(group2 == group, inputs, jnp.zeros_like(inputs)) for group in range(groups)],
            axis=0,
        )
        part = lax.dot_general(
            masked, window, (((1,), (1,)), ((), ())), preferred_element_type=jnp.float32
        )
        if at == 0:
            lag_ref[...] = part
        else:
            lag_ref[...] += part

    eights = []
    for group in range(groups):
        at = group * STEP
        rows = lag_ref[at : at + 8]
        for high in range(1, STEP // 8):
            rows = rows + roll_left(lag_ref[at + 8 * high : at + 8 * high + 8], 8 * high)
        eights.append(rows)
    skew = jnp.concatenate(eights, axis=0)
    row_in = lax.broadcasted_iota(jnp.int32, skew.shape, 0) % 8
    for bit in (1, 2, 4):
        skew = jnp.where((row_in & bit) != 0, roll_left(skew, bit), skew)
    dh = skew.reshape(groups, 8, reach).sum(axis=1)[:, :taps]

    high = dh.astype(jnp.bfloat16).astype(jnp.float32)
    left = dh - high
    mid = left.astype(jnp.bfloat16).astype(jnp.float32)
    least = left - mid
    for seq in range(n_seq):
        tile = (seq // 2) * LANES
        parts = [value[:, tile : tile + LANES] for value in (high, mid, least)]
        turned = [pltpu.roll(value, taps_here, 1) for value in parts]
        if seq % 2 == 0:
            top, bottom = jnp.where(low, parts[0], turned[1]), parts[2]
        else:
            top, bottom = jnp.where(low, turned[0], parts[1]), turned[2]
        parts_ref[seq] = jnp.concatenate([top, bottom], axis=0).astype(jnp.bfloat16)
    for to_chip in range(chips):
        taps_ref[to_chip] = parts_ref[2 * to_chip + core]
        send_ref[to_chip, block_len:, :] = parts_ref[2 * to_chip + 1 - core]


def second_kernel(dye_ref, toep_ref, out_ref):
    chips, block_len, _ = out_ref.shape
    groups = toep_ref.shape[0] // STEP
    reach = toep_ref.shape[1]
    toeplitz = toep_ref[...]
    for to_chip in range(chips):
        for row in range(0, block_len, 2 * STEP):
            window = window_at(dye_ref, 2 * to_chip * block_len + row, reach)
            out_ref[to_chip, row : row + 2 * STEP, :] = filtered(toeplitz, window, groups)


def back_kernel(keep_ref, taps_ref, got_ref, *out_refs):
    chip, _, _ = place()
    block_len = keep_ref.shape[1]
    for bits, out_ref in zip(partners(len(out_refs)), out_refs):
        out_ref[0, :block_len, :] = keep_ref[chip ^ bits]
        out_ref[0, block_len:, :] = taps_ref[chip ^ bits]
        out_ref[1] = got_ref[chip ^ bits]


def unpack_kernel(*refs):
    *got_refs, dx_ref, dh_ref, rows_ref = refs
    chip, core, _ = place()
    block_len = dx_ref.shape[0]
    taps_here, groups_here = dh_ref.shape
    groups = groups_here // (2 * len(got_refs))
    for bits, got_ref in zip(partners(len(got_refs)), got_refs):
        for flip in range(2):
            source = (chip ^ bits) * 2 + (core ^ flip)
            columns = pl.ds(pl.multiple_of(source * LANES, LANES), LANES)
            dx_ref[:, columns] = got_ref[flip, :block_len, :]
            extra = got_ref[flip, block_len:, :].astype(jnp.float32)
            top, bottom = extra[:groups], extra[groups:]
            rows_ref[pl.ds(pl.multiple_of(source * groups, 8), groups)] = (
                top + pltpu.roll(top, taps_here, 1) + bottom
            )
    dh_ref[...] = rows_ref[...].T[:taps_here]


def local_call(kernel, out_shape, operands, name, scratch=()):
    whole = pl.BlockSpec(memory_space=pltpu.VMEM)
    return pl.pallas_call(
        kernel,
        out_shape=out_shape,
        in_specs=[whole] * len(operands),
        out_specs=[whole] * len(out_shape),
        scratch_shapes=scratch,
        compiler_params=pltpu.CompilerParams(vmem_limit_bytes=VMEM_LIMIT),
        name=name,
    )(*operands)


def by_channels(n_seq, n_chan, out_grads, layer_inputs, filters):
    rows = out_grads.shape[0]
    block_len = layer_inputs.shape[0]
    taps_here, groups_here = filters.shape
    groups = groups_here // n_seq
    tokens = n_seq * block_len
    taps = n_seq * taps_here
    chips = n_seq // 2

    def half(*shape):
        return jax.ShapeDtypeStruct(shape, jnp.bfloat16)

    unit = block_len + EXTRA
    dy_other = xor_permute(out_grads, "seq", 1)
    x_other = xor_permute(layer_inputs, "seq", 1)
    f_other = xor_permute(filters, "seq", 1)
    (own,) = local_call(
        functools.partial(own_grads_kernel, n_seq),
        [half(n_chan, chips * rows, LANES)],
        (out_grads,),
        "own_grads",
    )
    pieces = local_call(
        functools.partial(fan_grads_kernel, n_seq),
        [half(2 * chips * rows, LANES)] * n_chan,
        (own, dy_other),
        "fan_grads",
    )
    dy = fan_out(pieces, "chan", 1)
    pieces = local_call(
        fan_inputs_kernel,
        [half(2 * unit, LANES)] * chips,
        (layer_inputs, x_other, filters, f_other),
        "fan_inputs",
        [pltpu.VMEM((2, groups_here, LANES), jnp.float32)],
    )
    x = fan_out(pieces, "seq", 2)
    pieces = local_call(
        functools.partial(regroup_kernel, rows, n_chan),
        [half(2 * n_chan * rows, LANES)] * chips,
        dy,
        "regroup",
    )
    dy = fan_out(pieces, "seq", 2)
    send, tap_parts, dye, toeplitz = local_call(
        functools.partial(first_kernel, n_seq, taps_here),
        [
            half(chips, unit, LANES),
            half(chips, EXTRA, LANES),
            half(tokens + taps + LANES, LANES),
            half(groups * STEP, taps + LANES),
        ],
        (*dy, *x),
        "first",
        [
            pltpu.VMEM((tokens, LANES), jnp.bfloat16),
            pltpu.VMEM((chips, groups, LANES), jnp.float32),
            pltpu.VMEM((groups * STEP, taps + LANES), jnp.float32),
            pltpu.VMEM((n_seq, EXTRA, LANES), jnp.bfloat16),
        ],
    )
    got = xor_permute(send, "seq", 1)
    (keep,) = local_call(
        second_kernel, [half(chips, block_len, LANES)], (dye, toeplitz), "second"
    )
    pieces = local_call(
        back_kernel, [half(2, unit, LANES)] * chips, (keep, tap_parts, got), "back"
    )
    return local_call(
        unpack_kernel,
        [
            half(block_len, n_seq * LANES),
            jax.ShapeDtypeStruct((taps_here, groups_here), jnp.float32),
        ],
        fan_out(pieces, "seq", 2),
        "unpack",
        [pltpu.VMEM((groups_here, LANES), jnp.float32)],
    )


def solution(mesh):
    n_seq, n_chan = mesh.shape["seq"], mesh.shape["chan"]

    def on_device(out_grads, layer_inputs, filters):
        taps_here, groups_here = filters.shape
        fits = (
            n_seq in (2, 4, 8, 16, 32)
            and n_chan in (2, 4, 8, 16, 32)
            and layer_inputs.shape[1] == n_seq * LANES
            and groups_here == 8 * n_seq
            and 2 * taps_here == LANES
            and out_grads.shape[0] % 16 == 0
            and layer_inputs.shape[0] % (2 * STEP) == 0
            and n_seq * taps_here + LANES <= n_seq * layer_inputs.shape[0]
        )
        if fits:
            return tuple(by_channels(n_seq, n_chan, out_grads, layer_inputs, filters))
        return by_tokens(out_grads, layer_inputs, filters)

    in_specs = (P(("seq", "chan"), None), P("seq", "chan"), P("seq", "chan"))
    out_specs = (P("seq", "chan"), P("seq", "chan"))
    return jax.shard_map(
        on_device, mesh=mesh, in_specs=in_specs, out_specs=out_specs, check_vma=False
    )
```

```python
import functools

import jax
import jax.numpy as jnp
from jax import lax
from jax.experimental import pallas as pl
from jax.experimental.pallas import tpu as pltpu
from jax.sharding import PartitionSpec as P

LANES = 128
STEP = 32
EXTRA = 16
VMEM_LIMIT = 40 * 1024 * 1024


def shifted(value, axis, steps):
    count = lax.axis_size(axis)
    pairs = [(source, (source + steps) % count) for source in range(count)]
    return lax.ppermute(value, axis, pairs)


def skewed_sums(products):
    groups_here, length, _ = products.shape
    padded = jnp.pad(products, ((0, 0), (0, 0), (0, length)))
    flat = padded.reshape(groups_here, 2 * length * length)[:, : length * (2 * length - 1)]
    return flat.reshape(groups_here, length, 2 * length - 1).sum(axis=1)


def by_tokens(out_grads, layer_inputs, filters):
    local_grads = lax.all_to_all(out_grads, "chan", split_axis=1, concat_axis=0, tiled=True)
    taps_all = lax.all_gather(filters, "seq", axis=0, tiled=True)
    block_len = local_grads.shape[0]
    chan_width = local_grads.shape[1]
    groups_here = filters.shape[1]
    per_group = chan_width // groups_here
    taps_total = taps_all.shape[0]
    spread_blocks = taps_total // block_len
    filt_rows = taps_all.T
    x_reversed = layer_inputs[::-1].reshape(block_len, groups_here, per_group).transpose(1, 2, 0)
    offsets = lax.broadcasted_iota(jnp.int32, (block_len, block_len), 1) - lax.broadcasted_iota(
        jnp.int32, (block_len, block_len), 0
    )
    dx_total = jnp.zeros((groups_here, per_group, block_len), jnp.float32)
    lag_buffer = jnp.zeros((groups_here, (spread_blocks + 2) * block_len), jnp.float32)
    current = local_grads
    for lag_block in range(spread_blocks + 1):
        if lag_block > 0:
            current = shifted(local_grads, "seq", -lag_block)
        dy_grouped = current.reshape(block_len, groups_here, per_group).transpose(1, 2, 0)
        lag_index = lag_block * block_len + offsets
        inside = (lag_index >= 0) & (lag_index < taps_total)
        picked = jnp.take(filt_rows, jnp.clip(lag_index, 0, taps_total - 1), axis=1)
        toeplitz = jnp.where(inside[None], picked, jnp.zeros((), jnp.bfloat16))
        dx_total = dx_total + jnp.einsum(
            "guv,gkv->gku", toeplitz, dy_grouped, preferred_element_type=jnp.float32
        )
        products = jnp.einsum(
            "gku,gkv->guv", x_reversed, dy_grouped, preferred_element_type=jnp.float32
        )
        start = lag_block * block_len
        lag_buffer = lag_buffer.at[:, start : start + 2 * block_len - 1].add(skewed_sums(products))
    partial_dh = lag_buffer[:, block_len - 1 : block_len - 1 + taps_total].T
    filter_grads = lax.psum_scatter(partial_dh, "seq", scatter_dimension=0, tiled=True)
    input_grads = dx_total.transpose(2, 0, 1).reshape(block_len, chan_width).astype(jnp.bfloat16)
    return (input_grads, filter_grads)


def xor_permute(value, axis, bits):
    pairs = [(source, source ^ bits) for source in range(lax.axis_size(axis))]
    return lax.ppermute(value, axis, pairs)


def partners(count):
    return [(count - step) % count for step in range(count)]


def fan_out(pieces, axis, unit):
    masks = partners(len(pieces))[1:]
    return [pieces[0]] + [xor_permute(p, axis, m * unit) for p, m in zip(pieces[1:], masks)]


def roll_left(value, steps):
    width = value.shape[-1]
    return pltpu.roll(value, (width - steps) % width, value.ndim - 1)


def place():
    seq = lax.axis_index("seq")
    return seq // 2, seq % 2, lax.axis_index("chan")


def rows_at(index, size):
    return pl.ds(pl.multiple_of(index * size, 16), size)


def fan_grads_kernel(n_seq, in_ref, out_ref):
    n_chan = out_ref.shape[0] // n_seq
    for seq in range(n_seq):
        for chan in range(n_chan):
            start = (chan * n_seq + seq) * LANES
            out_ref[seq * n_chan + chan] = in_ref[:, start : start + LANES]


def fan_inputs_kernel(x_own_ref, x_other_ref, f_own_ref, f_other_ref, *refs):
    *out_refs, taps_ref = refs
    chip, core, _ = place()
    block_len = x_own_ref.shape[0]
    taps_here, groups_here = f_own_ref.shape
    groups = groups_here // (2 * len(out_refs))
    rest = jnp.zeros((EXTRA - groups, LANES), jnp.float32)
    for flip, (x_ref, f_ref) in enumerate(((x_own_ref, f_own_ref), (x_other_ref, f_other_ref))):
        taps_ref[flip] = jnp.concatenate(
            [
                f_ref[...].astype(jnp.float32).T,
                jnp.zeros((groups_here, LANES - taps_here), jnp.float32),
            ],
            axis=1,
        )
        for bits, out_ref in zip(partners(len(out_refs)), out_refs):
            target = 2 * (chip ^ bits) + core
            at = flip * (block_len + EXTRA)
            out_ref[at : at + block_len] = x_ref[
                :, pl.ds(pl.multiple_of(target * LANES, LANES), LANES)
            ]
            taps = taps_ref[flip, pl.ds(pl.multiple_of(target * groups, groups), groups)]
            out_ref[at + block_len : at + block_len + EXTRA] = jnp.concatenate(
                [taps, rest], axis=0
            ).astype(jnp.bfloat16)


def toeplitz_kernel(n_seq, taps_here, *refs):
    chips = n_seq // 2
    in_refs = refs[:chips]
    toep_ref, x_ref, filt_ref = refs[chips:]
    block_len = x_ref.shape[0] // n_seq
    groups = toep_ref.shape[0] // STEP
    reach = toep_ref.shape[1]
    chip, core, _ = place()
    low = lax.broadcasted_iota(jnp.int32, (groups, LANES), 1) < taps_here
    for bits, in_ref in zip(partners(chips), in_refs):
        pieces = []
        for flip in range(2):
            block = (2 * (chip ^ bits) + (core ^ flip) - core + n_seq) % n_seq
            at = flip * (block_len + EXTRA)
            x_ref[rows_at(block, block_len)] = in_ref[at : at + block_len]
            at += block_len
            pieces.append(in_ref[at : at + EXTRA].astype(jnp.float32)[:groups])
        first = jnp.where(core == 0, pieces[0], pieces[1])
        second = jnp.where(core == 0, pieces[1], pieces[0])
        filt_ref[chip ^ bits] = jnp.where(low, first, pltpu.roll(second, taps_here, 1))
    tiles = [filt_ref[tile] for tile in range(chips)]
    filt = jnp.concatenate(tiles + [jnp.zeros((groups, LANES), jnp.float32)], axis=1)
    for group in range(groups):
        rows = jnp.broadcast_to(filt[group : group + 1], (STEP, reach))
        rows = pltpu.roll(rows, 0, 1, stride=1, stride_axis=0)
        toep_ref[group * STEP : (group + 1) * STEP] = rows.astype(jnp.bfloat16)


def group_of_lane(width, groups):
    lane = lax.broadcasted_iota(jnp.int32, (STEP, width), 1)
    return (lane % LANES) // (LANES // groups)


def window_at(dye_ref, at, reach):
    return jnp.concatenate(
        [dye_ref[at : at + reach], dye_ref[at + STEP : at + STEP + reach]], axis=1
    )


def filtered(toeplitz, window, groups):
    full = jnp.dot(toeplitz, window, preferred_element_type=jnp.float32)
    group2 = group_of_lane(2 * LANES, groups)
    total = full[:STEP]
    for group in range(1, groups):
        total = jnp.where(group2 == group, full[group * STEP : (group + 1) * STEP], total)
    return jnp.concatenate([total[:, :LANES], total[:, LANES:]], axis=0).astype(jnp.bfloat16)


def first_kernel(
    n_seq, taps_here, dy_ref, x_ref, toep_ref, send_ref, taps_ref, dye_ref, lag_ref, parts_ref
):
    chips = n_seq // 2
    tokens = dy_ref.shape[0]
    block_len = tokens // n_seq
    groups = toep_ref.shape[0] // STEP
    taps = n_seq * taps_here
    reach = taps + LANES
    _, core, _ = place()
    low = lax.broadcasted_iota(jnp.int32, (groups, LANES), 1) < taps_here

    for block in range(n_seq):
        dye_ref[block * block_len : (block + 1) * block_len] = dy_ref[
            rows_at((block + core) % n_seq, block_len)
        ]
    dye_ref[tokens:] = dye_ref[:reach]

    group2 = group_of_lane(2 * LANES, groups)
    toeplitz = toep_ref[...]
    for at in range(0, tokens, 2 * STEP):
        window = window_at(dye_ref, at, reach)
        block, row = at // block_len, at % block_len
        if block % 2 == 1:
            send_ref[(block // 2 + core) % chips, row : row + 2 * STEP, :] = filtered(
                toeplitz, window, groups
            )
        inputs = jnp.concatenate(
            [x_ref[at : at + STEP], x_ref[at + STEP : at + 2 * STEP]], axis=1
        )
        masked = jnp.concatenate(
            [jnp.where(group2 == group, inputs, jnp.zeros_like(inputs)) for group in range(groups)],
            axis=0,
        )
        part = lax.dot_general(
            masked, window, (((1,), (1,)), ((), ())), preferred_element_type=jnp.float32
        )
        if at == 0:
            lag_ref[...] = part
        else:
            lag_ref[...] += part

    eights = []
    for group in range(groups):
        at = group * STEP
        rows = lag_ref[at : at + 8]
        for high in range(1, STEP // 8):
            rows = rows + roll_left(lag_ref[at + 8 * high : at + 8 * high + 8], 8 * high)
        eights.append(rows)
    skew = jnp.concatenate(eights, axis=0)
    row_in = lax.broadcasted_iota(jnp.int32, skew.shape, 0) % 8
    for bit in (1, 2, 4):
        skew = jnp.where((row_in & bit) != 0, roll_left(skew, bit), skew)
    dh = skew.reshape(groups, 8, reach).sum(axis=1)[:, :taps]

    high = dh.astype(jnp.bfloat16).astype(jnp.float32)
    left = dh - high
    mid = left.astype(jnp.bfloat16).astype(jnp.float32)
    least = left - mid
    for seq in range(n_seq):
        tile = (seq // 2) * LANES
        parts = [value[:, tile : tile + LANES] for value in (high, mid, least)]
        turned = [pltpu.roll(value, taps_here, 1) for value in parts]
        if seq % 2 == 0:
            top, bottom = jnp.where(low, parts[0], turned[1]), parts[2]
        else:
            top, bottom = jnp.where(low, turned[0], parts[1]), turned[2]
        parts_ref[seq] = jnp.concatenate([top, bottom], axis=0).astype(jnp.bfloat16)
    for to_chip in range(chips):
        taps_ref[to_chip] = parts_ref[2 * to_chip + core]
        send_ref[to_chip, block_len:, :] = parts_ref[2 * to_chip + 1 - core]


def second_kernel(dye_ref, toep_ref, out_ref):
    chips, block_len, _ = out_ref.shape
    groups = toep_ref.shape[0] // STEP
    reach = toep_ref.shape[1]
    toeplitz = toep_ref[...]
    for to_chip in range(chips):
        for row in range(0, block_len, 2 * STEP):
            window = window_at(dye_ref, 2 * to_chip * block_len + row, reach)
            out_ref[to_chip, row : row + 2 * STEP, :] = filtered(toeplitz, window, groups)


def back_kernel(keep_ref, taps_ref, got_ref, *out_refs):
    chip, _, _ = place()
    block_len = keep_ref.shape[1]
    for bits, out_ref in zip(partners(len(out_refs)), out_refs):
        out_ref[0, :block_len, :] = keep_ref[chip ^ bits]
        out_ref[0, block_len:, :] = taps_ref[chip ^ bits]
        out_ref[1] = got_ref[chip ^ bits]


def unpack_kernel(*refs):
    *got_refs, dx_ref, dh_ref, rows_ref = refs
    chip, core, _ = place()
    block_len = dx_ref.shape[0]
    taps_here, groups_here = dh_ref.shape
    groups = groups_here // (2 * len(got_refs))
    for bits, got_ref in zip(partners(len(got_refs)), got_refs):
        for flip in range(2):
            source = (chip ^ bits) * 2 + (core ^ flip)
            columns = pl.ds(pl.multiple_of(source * LANES, LANES), LANES)
            dx_ref[:, columns] = got_ref[flip, :block_len, :]
            extra = got_ref[flip, block_len:, :].astype(jnp.float32)
            top, bottom = extra[:groups], extra[groups:]
            rows_ref[pl.ds(pl.multiple_of(source * groups, 8), groups)] = (
                top + pltpu.roll(top, taps_here, 1) + bottom
            )
    dh_ref[...] = rows_ref[...].T[:taps_here]


def local_call(kernel, out_shape, operands, name, scratch=()):
    whole = pl.BlockSpec(memory_space=pltpu.VMEM)
    return pl.pallas_call(
        kernel,
        out_shape=out_shape,
        in_specs=[whole] * len(operands),
        out_specs=[whole] * len(out_shape),
        scratch_shapes=scratch,
        compiler_params=pltpu.CompilerParams(vmem_limit_bytes=VMEM_LIMIT),
        name=name,
    )(*operands)


def by_channels(n_seq, n_chan, out_grads, layer_inputs, filters):
    rows = out_grads.shape[0]
    block_len = layer_inputs.shape[0]
    taps_here, groups_here = filters.shape
    groups = groups_here // n_seq
    tokens = n_seq * block_len
    taps = n_seq * taps_here
    chips = n_seq // 2

    def half(*shape):
        return jax.ShapeDtypeStruct(shape, jnp.bfloat16)

    unit = block_len + EXTRA
    x_other = xor_permute(layer_inputs, "seq", 1)
    f_other = xor_permute(filters, "seq", 1)
    (dy,) = local_call(
        functools.partial(fan_grads_kernel, n_seq),
        [half(n_seq * n_chan, rows, LANES)],
        (out_grads,),
        "fan_grads",
    )
    dy = lax.all_to_all(dy, ("seq", "chan"), split_axis=0, concat_axis=0, tiled=True)
    pieces = local_call(
        fan_inputs_kernel,
        [half(2 * unit, LANES)] * chips,
        (layer_inputs, x_other, filters, f_other),
        "fan_inputs",
        [pltpu.VMEM((2, groups_here, LANES), jnp.float32)],
    )
    toeplitz, x = local_call(
        functools.partial(toeplitz_kernel, n_seq, taps_here),
        [half(groups * STEP, taps + LANES), half(tokens, LANES)],
        fan_out(pieces, "seq", 2),
        "toeplitz",
        [pltpu.VMEM((chips, groups, LANES), jnp.float32)],
    )
    send, tap_parts, dye = local_call(
        functools.partial(first_kernel, n_seq, taps_here),
        [
            half(chips, unit, LANES),
            half(chips, EXTRA, LANES),
            half(tokens + taps + LANES, LANES),
        ],
        (dy.reshape(tokens, LANES), x, toeplitz),
        "first",
        [
            pltpu.VMEM((groups * STEP, taps + LANES), jnp.float32),
            pltpu.VMEM((n_seq, EXTRA, LANES), jnp.bfloat16),
        ],
    )
    got = xor_permute(send, "seq", 1)
    (keep,) = local_call(
        second_kernel, [half(chips, block_len, LANES)], (dye, toeplitz), "second"
    )
    pieces = local_call(
        back_kernel, [half(2, unit, LANES)] * chips, (keep, tap_parts, got), "back"
    )
    return local_call(
        unpack_kernel,
        [
            half(block_len, n_seq * LANES),
            jax.ShapeDtypeStruct((taps_here, groups_here), jnp.float32),
        ],
        fan_out(pieces, "seq", 2),
        "unpack",
        [pltpu.VMEM((groups_here, LANES), jnp.float32)],
    )


def solution(mesh):
    n_seq, n_chan = mesh.shape["seq"], mesh.shape["chan"]

    def on_device(out_grads, layer_inputs, filters):
        taps_here, groups_here = filters.shape
        fits = (
            n_seq in (2, 4, 8, 16, 32)
            and n_chan in (2, 4, 8, 16, 32)
            and layer_inputs.shape[1] == n_seq * LANES
            and groups_here == 8 * n_seq
            and 2 * taps_here == LANES
            and out_grads.shape[0] % 16 == 0
            and layer_inputs.shape[0] % (2 * STEP) == 0
            and n_seq * taps_here + LANES <= n_seq * layer_inputs.shape[0]
        )
        if fits:
            return tuple(by_channels(n_seq, n_chan, out_grads, layer_inputs, filters))
        return by_tokens(out_grads, layer_inputs, filters)

    in_specs = (P(("seq", "chan"), None), P("seq", "chan"), P("seq", "chan"))
    out_specs = (P("seq", "chan"), P("seq", "chan"))
    return jax.shard_map(
        on_device, mesh=mesh, in_specs=in_specs, out_specs=out_specs, check_vma=False
    )
```

```python
import functools

import jax
import jax.numpy as jnp
from jax import lax
from jax.experimental import pallas as pl
from jax.experimental.pallas import tpu as pltpu
from jax.sharding import PartitionSpec as P

LANES = 128
STEP = 32
EXTRA = 16
DEPTH = 1024
VMEM_LIMIT = 40 * 1024 * 1024


def shifted(value, axis, steps):
    count = lax.axis_size(axis)
    pairs = [(source, (source + steps) % count) for source in range(count)]
    return lax.ppermute(value, axis, pairs)


def skewed_sums(products):
    groups_here, length, _ = products.shape
    padded = jnp.pad(products, ((0, 0), (0, 0), (0, length)))
    flat = padded.reshape(groups_here, 2 * length * length)[:, : length * (2 * length - 1)]
    return flat.reshape(groups_here, length, 2 * length - 1).sum(axis=1)


def by_tokens(out_grads, layer_inputs, filters):
    local_grads = lax.all_to_all(out_grads, "chan", split_axis=1, concat_axis=0, tiled=True)
    taps_all = lax.all_gather(filters, "seq", axis=0, tiled=True)
    block_len = local_grads.shape[0]
    chan_width = local_grads.shape[1]
    groups_here = filters.shape[1]
    per_group = chan_width // groups_here
    taps_total = taps_all.shape[0]
    spread_blocks = taps_total // block_len
    filt_rows = taps_all.T
    x_reversed = layer_inputs[::-1].reshape(block_len, groups_here, per_group).transpose(1, 2, 0)
    offsets = lax.broadcasted_iota(jnp.int32, (block_len, block_len), 1) - lax.broadcasted_iota(
        jnp.int32, (block_len, block_len), 0
    )
    dx_total = jnp.zeros((groups_here, per_group, block_len), jnp.float32)
    lag_buffer = jnp.zeros((groups_here, (spread_blocks + 2) * block_len), jnp.float32)
    current = local_grads
    for lag_block in range(spread_blocks + 1):
        if lag_block > 0:
            current = shifted(local_grads, "seq", -lag_block)
        dy_grouped = current.reshape(block_len, groups_here, per_group).transpose(1, 2, 0)
        lag_index = lag_block * block_len + offsets
        inside = (lag_index >= 0) & (lag_index < taps_total)
        picked = jnp.take(filt_rows, jnp.clip(lag_index, 0, taps_total - 1), axis=1)
        toeplitz = jnp.where(inside[None], picked, jnp.zeros((), jnp.bfloat16))
        dx_total = dx_total + jnp.einsum(
            "guv,gkv->gku", toeplitz, dy_grouped, preferred_element_type=jnp.float32
        )
        products = jnp.einsum(
            "gku,gkv->guv", x_reversed, dy_grouped, preferred_element_type=jnp.float32
        )
        start = lag_block * block_len
        lag_buffer = lag_buffer.at[:, start : start + 2 * block_len - 1].add(skewed_sums(products))
    partial_dh = lag_buffer[:, block_len - 1 : block_len - 1 + taps_total].T
    filter_grads = lax.psum_scatter(partial_dh, "seq", scatter_dimension=0, tiled=True)
    input_grads = dx_total.transpose(2, 0, 1).reshape(block_len, chan_width).astype(jnp.bfloat16)
    return (input_grads, filter_grads)


def xor_permute(value, axis, bits):
    pairs = [(source, source ^ bits) for source in range(lax.axis_size(axis))]
    return lax.ppermute(value, axis, pairs)


def partners(count):
    return [(count - step) % count for step in range(count)]


def fan_out(pieces, axis, unit):
    masks = partners(len(pieces))[1:]
    return [pieces[0]] + [xor_permute(p, axis, m * unit) for p, m in zip(pieces[1:], masks)]


def roll_left(value, steps):
    width = value.shape[-1]
    return pltpu.roll(value, (width - steps) % width, value.ndim - 1)


def place():
    seq = lax.axis_index("seq")
    return seq // 2, seq % 2, lax.axis_index("chan")


def rows_at(index, size):
    return pl.ds(pl.multiple_of(index * size, 16), size)


def fan_grads_kernel(n_seq, in_ref, out_ref, sems):
    n_chan = out_ref.shape[0] // n_seq
    copies = []
    for chan in reversed(range(n_chan)):
        for seq in range(n_seq):
            start = (chan * n_seq + seq) * LANES
            to = seq * n_chan + chan
            copies.append(
                pltpu.make_async_copy(
                    in_ref.at[:, start : start + LANES], out_ref.at[to], sems.at[to]
                )
            )
    for copy in copies:
        copy.start()
    for copy in copies:
        copy.wait()


def fan_inputs_kernel(x_own_ref, x_other_ref, f_own_ref, f_other_ref, *refs):
    *out_refs, taps_ref = refs
    chip, core, _ = place()
    block_len = x_own_ref.shape[0]
    taps_here, groups_here = f_own_ref.shape
    groups = groups_here // (2 * len(out_refs))
    rest = jnp.zeros((groups_here, LANES - taps_here), jnp.float32)
    for flip, f_ref in enumerate((f_own_ref, f_other_ref)):
        taps_ref[flip] = jnp.concatenate([f_ref[...].astype(jnp.float32).T, rest], axis=1)
    for bits, out_ref in zip(partners(len(out_refs)), out_refs):
        target = 2 * (chip ^ bits) + core
        columns = pl.ds(pl.multiple_of(target * LANES, LANES), LANES)
        out_ref[:block_len] = x_own_ref[:, columns]
        out_ref[block_len : 2 * block_len] = x_other_ref[:, columns]
        rows = pl.ds(pl.multiple_of(target * groups, groups), groups)
        taps = jnp.concatenate([taps_ref[0, rows], taps_ref[1, rows]], axis=0)
        out_ref[2 * block_len :] = taps.astype(jnp.bfloat16)


def toeplitz_kernel(n_seq, taps_here, *refs):
    chips = n_seq // 2
    in_refs = refs[:chips]
    toep_ref, x_ref, filt_ref = refs[chips:]
    block_len = x_ref.shape[0] // n_seq
    groups = toep_ref.shape[0] // STEP
    reach = toep_ref.shape[1]
    chip, core, _ = place()
    low = lax.broadcasted_iota(jnp.int32, (groups, LANES), 1) < taps_here
    for bits, in_ref in zip(partners(chips), in_refs):
        for flip in range(2):
            block = 2 * (chip ^ bits) + (core ^ flip)
            x_ref[rows_at(block, block_len)] = in_ref[flip * block_len : (flip + 1) * block_len]
        taps = in_ref[2 * block_len :].astype(jnp.float32)
        first = jnp.where(core == 0, taps[:groups], taps[groups:])
        second = jnp.where(core == 0, taps[groups:], taps[:groups])
        filt_ref[chip ^ bits] = jnp.where(low, first, pltpu.roll(second, taps_here, 1))
    tiles = [filt_ref[tile] for tile in range(chips)]
    filt = jnp.concatenate(tiles + [jnp.zeros((groups, LANES), jnp.float32)], axis=1)
    for group in range(groups):
        rows = jnp.broadcast_to(filt[group : group + 1], (STEP, reach))
        rows = pltpu.roll(rows, 0, 1, stride=1, stride_axis=0)
        toep_ref[group * STEP : (group + 1) * STEP] = rows.astype(jnp.bfloat16)


def group_of_lane(rows, width, groups):
    lane = lax.broadcasted_iota(jnp.int32, (rows, width), 1)
    return (lane % LANES) // (LANES // groups)


def filtered(dye_ref, start, toeplitz, groups):
    reach = toeplitz.shape[1]
    window = jnp.concatenate(
        [
            dye_ref[pl.ds(pl.multiple_of(start, STEP), reach)],
            dye_ref[pl.ds(pl.multiple_of(start + STEP, STEP), reach)],
        ],
        axis=1,
    )
    full = jnp.dot(toeplitz, window, preferred_element_type=jnp.float32)
    group2 = group_of_lane(STEP, 2 * LANES, groups)
    total = full[:STEP]
    for group in range(1, groups):
        total = jnp.where(group2 == group, full[group * STEP : (group + 1) * STEP], total)
    return jnp.concatenate([total[:, :LANES], total[:, LANES:]], axis=0).astype(jnp.bfloat16)


def results_for(to_chip, core, dye_ref, toep_ref, taps_ref, out_ref):
    block_len = (out_ref.shape[0] - taps_ref.shape[1]) // 2
    toeplitz = toep_ref[...]
    groups = toeplitz.shape[0] // STEP
    for flip in range(2):
        start = (2 * to_chip + (core ^ flip)) * block_len
        for row in range(0, block_len, 2 * STEP):
            at = flip * block_len + row
            out_ref[at : at + 2 * STEP] = filtered(dye_ref, start + row, toeplitz, groups)
    out_ref[2 * block_len :] = taps_ref[to_chip]


def first_kernel(
    n_seq, taps_here, far, dy_ref, x_ref, toep_ref, dye_ref, taps_ref, out_ref, lag_ref
):
    chips = n_seq // 2
    tokens = dy_ref.shape[0]
    groups = toep_ref.shape[0] // STEP
    taps = n_seq * taps_here
    reach = taps + LANES
    chip, core, _ = place()

    dye_ref[:tokens] = dy_ref[...]
    dye_ref[tokens:] = dy_ref[:reach]

    deep = DEPTH // LANES
    group_in = group_of_lane(STEP, DEPTH, groups)
    for at in range(0, tokens, STEP * deep):
        starts = range(at, at + STEP * deep, STEP)
        windows = jnp.concatenate([dye_ref[row : row + reach] for row in starts], axis=1)
        inputs = jnp.concatenate([x_ref[row : row + STEP] for row in starts], axis=1)
        masked = jnp.concatenate(
            [jnp.where(group_in == group, inputs, jnp.zeros_like(inputs)) for group in range(groups)],
            axis=0,
        )
        part = lax.dot_general(
            masked, windows, (((1,), (1,)), ((), ())), preferred_element_type=jnp.float32
        )
        if at == 0:
            lag_ref[...] = part
        else:
            lag_ref[...] += part

    eights = []
    for group in range(groups):
        at = group * STEP
        rows = lag_ref[at : at + 8]
        for high in range(1, STEP // 8):
            rows = rows + roll_left(lag_ref[at + 8 * high : at + 8 * high + 8], 8 * high)
        eights.append(rows)
    skew = jnp.concatenate(eights, axis=0)
    row_in = lax.broadcasted_iota(jnp.int32, skew.shape, 0) % 8
    for bit in (1, 2, 4):
        skew = jnp.where((row_in & bit) != 0, roll_left(skew, bit), skew)
    dh = skew.reshape(groups, 8, reach).sum(axis=1)[:, :taps]

    high = dh.astype(jnp.bfloat16).astype(jnp.float32)
    rest = dh - high
    low = lax.broadcasted_iota(jnp.int32, (groups, LANES), 1) < taps_here
    for to_chip in range(chips):
        columns = slice(to_chip * LANES, (to_chip + 1) * LANES)
        top, bottom = high[:, columns], rest[:, columns]
        even = jnp.where(low, top, pltpu.roll(bottom, taps_here, 1))
        odd = jnp.where(low, pltpu.roll(top, taps_here, 1), bottom)
        mine = jnp.where(core == 0, even, odd)
        other = jnp.where(core == 0, odd, even)
        taps_ref[to_chip] = jnp.concatenate([mine, other], axis=0).astype(jnp.bfloat16)

    results_for(chip ^ far, core, dye_ref, toep_ref, taps_ref, out_ref)


def more_kernel(masks, dye_ref, toep_ref, taps_ref, *out_refs):
    chip, core, _ = place()
    for bits, out_ref in zip(masks, out_refs):
        results_for(chip ^ bits, core, dye_ref, toep_ref, taps_ref, out_ref)


def swap_kernel(*refs):
    *got_refs, out_ref = refs
    groups = EXTRA // 2
    block_len = (got_refs[0].shape[0] - EXTRA) // 2
    taps = []
    for index, got_ref in enumerate(got_refs):
        out_ref[index * block_len : (index + 1) * block_len] = got_ref[block_len : 2 * block_len]
        taps.append(got_ref[2 * block_len :].astype(jnp.float32)[groups:])
    out_ref[len(got_refs) * block_len :] = jnp.concatenate(taps, axis=0).astype(jnp.bfloat16)


def unpack_kernel(*refs):
    *got_refs, swapped_ref, dx_ref, dh_ref, rows_ref = refs
    chips = len(got_refs)
    chip, core, _ = place()
    block_len = dx_ref.shape[0]
    taps_here, groups_here = dh_ref.shape
    groups = groups_here // (2 * chips)
    other_taps = swapped_ref[chips * block_len :].astype(jnp.float32)
    for index, (bits, got_ref) in enumerate(zip(partners(chips), got_refs)):
        mine_taps = got_ref[2 * block_len :].astype(jnp.float32)[:groups]
        for flip, tokens, taps in (
            (0, got_ref[:block_len], mine_taps),
            (
                1,
                swapped_ref[index * block_len : (index + 1) * block_len],
                other_taps[index * groups : (index + 1) * groups],
            ),
        ):
            source = (chip ^ bits) * 2 + (core ^ flip)
            dx_ref[:, pl.ds(pl.multiple_of(source * LANES, LANES), LANES)] = tokens
            rows_ref[pl.ds(pl.multiple_of(source * groups, groups), groups)] = taps + pltpu.roll(
                taps, taps_here, 1
            )
    dh_ref[...] = rows_ref[...].T[:taps_here]


def local_call(kernel, out_shape, operands, name, scratch=()):
    whole = pl.BlockSpec(memory_space=pltpu.VMEM)
    return pl.pallas_call(
        kernel,
        out_shape=out_shape,
        in_specs=[whole] * len(operands),
        out_specs=[whole] * len(out_shape),
        scratch_shapes=scratch,
        compiler_params=pltpu.CompilerParams(vmem_limit_bytes=VMEM_LIMIT),
        name=name,
    )(*operands)


def by_channels(n_seq, n_chan, out_grads, layer_inputs, filters):
    rows = out_grads.shape[0]
    block_len = layer_inputs.shape[0]
    taps_here, groups_here = filters.shape
    groups = groups_here // n_seq
    tokens = n_seq * block_len
    taps = n_seq * taps_here
    chips = n_seq // 2
    masks = partners(chips)

    def half(*shape):
        return jax.ShapeDtypeStruct(shape, jnp.bfloat16)

    unit = half(2 * block_len + EXTRA, LANES)
    x_other = xor_permute(layer_inputs, "seq", 1)
    f_other = xor_permute(filters, "seq", 1)
    dy = pl.pallas_call(
        functools.partial(fan_grads_kernel, n_seq),
        out_shape=half(n_seq * n_chan, rows, LANES),
        in_specs=[pl.BlockSpec(memory_space=pltpu.HBM)],
        out_specs=pl.BlockSpec(memory_space=pltpu.HBM),
        scratch_shapes=[pltpu.SemaphoreType.DMA((n_seq * n_chan,))],
        name="fan_grads",
    )(out_grads)
    dy, x_other, f_other = lax.optimization_barrier((dy, x_other, f_other))
    dy = lax.all_to_all(dy, ("seq", "chan"), split_axis=0, concat_axis=0, tiled=True)
    pieces = local_call(
        fan_inputs_kernel,
        [unit] * chips,
        (layer_inputs, x_other, filters, f_other),
        "fan_inputs",
        [pltpu.VMEM((2, groups_here, LANES), jnp.float32)],
    )
    toeplitz, x = local_call(
        functools.partial(toeplitz_kernel, n_seq, taps_here),
        [half(groups * STEP, taps + LANES), half(tokens, LANES)],
        fan_out(pieces, "seq", 2),
        "toeplitz",
        [pltpu.VMEM((chips, groups, LANES), jnp.float32)],
    )
    dye, tap_parts, far = local_call(
        functools.partial(first_kernel, n_seq, taps_here, masks[1]),
        [half(tokens + taps + LANES, LANES), half(chips, EXTRA, LANES), unit],
        (dy.reshape(tokens, LANES), x, toeplitz),
        "first",
        [pltpu.VMEM((groups * STEP, taps + LANES), jnp.float32)],
    )
    results = [xor_permute(far, "seq", 2 * masks[1])]
    if masks[2:]:
        near = local_call(
            functools.partial(more_kernel, masks[2:]),
            [unit] * len(masks[2:]),
            (dye, toeplitz, tap_parts),
            "near",
        )
        results += [xor_permute(p, "seq", 2 * m) for p, m in zip(near, masks[2:])]
    results[0], tap_parts = lax.optimization_barrier((results[0], tap_parts))
    (own,) = local_call(
        functools.partial(more_kernel, masks[:1]), [unit], (dye, toeplitz, tap_parts), "own"
    )
    results = [own] + results
    (send,) = local_call(
        swap_kernel, [half(chips * (block_len + EXTRA // 2), LANES)], results, "swap"
    )
    return local_call(
        unpack_kernel,
        [
            half(block_len, n_seq * LANES),
            jax.ShapeDtypeStruct((taps_here, groups_here), jnp.float32),
        ],
        (*results, xor_permute(send, "seq", 1)),
        "unpack",
        [pltpu.VMEM((groups_here, LANES), jnp.float32)],
    )


def solution(mesh):
    n_seq, n_chan = mesh.shape["seq"], mesh.shape["chan"]

    def on_device(out_grads, layer_inputs, filters):
        taps_here, groups_here = filters.shape
        fits = (
            n_seq in (4, 8, 16, 32)
            and n_chan in (2, 4, 8, 16, 32)
            and layer_inputs.shape[1] == n_seq * LANES
            and groups_here == 8 * n_seq
            and 2 * taps_here == LANES
            and out_grads.shape[0] % 16 == 0
            and layer_inputs.shape[0] % (2 * STEP) == 0
            and n_seq * layer_inputs.shape[0] % (STEP * DEPTH // LANES) == 0
            and n_seq * taps_here + LANES <= n_seq * layer_inputs.shape[0]
        )
        if fits:
            return tuple(by_channels(n_seq, n_chan, out_grads, layer_inputs, filters))
        return by_tokens(out_grads, layer_inputs, filters)

    in_specs = (P(("seq", "chan"), None), P("seq", "chan"), P("seq", "chan"))
    out_specs = (P("seq", "chan"), P("seq", "chan"))
    return jax.shard_map(
        on_device, mesh=mesh, in_specs=in_specs, out_specs=out_specs, check_vma=False
    )
```

```python
import functools

import jax
import jax.numpy as jnp
from jax import lax
from jax.experimental import pallas as pl
from jax.experimental.pallas import tpu as pltpu
from jax.sharding import PartitionSpec as P

LANES = 128
STEP = 32
EXTRA = 16
DEPTH = 1024
VMEM_LIMIT = 40 * 1024 * 1024


def shifted(value, axis, steps):
    count = lax.axis_size(axis)
    pairs = [(source, (source + steps) % count) for source in range(count)]
    return lax.ppermute(value, axis, pairs)


def skewed_sums(products):
    groups_here, length, _ = products.shape
    padded = jnp.pad(products, ((0, 0), (0, 0), (0, length)))
    flat = padded.reshape(groups_here, 2 * length * length)[:, : length * (2 * length - 1)]
    return flat.reshape(groups_here, length, 2 * length - 1).sum(axis=1)


def by_tokens(out_grads, layer_inputs, filters):
    local_grads = lax.all_to_all(out_grads, "chan", split_axis=1, concat_axis=0, tiled=True)
    taps_all = lax.all_gather(filters, "seq", axis=0, tiled=True)
    block_len = local_grads.shape[0]
    chan_width = local_grads.shape[1]
    groups_here = filters.shape[1]
    per_group = chan_width // groups_here
    taps_total = taps_all.shape[0]
    spread_blocks = taps_total // block_len
    filt_rows = taps_all.T
    x_reversed = layer_inputs[::-1].reshape(block_len, groups_here, per_group).transpose(1, 2, 0)
    offsets = lax.broadcasted_iota(jnp.int32, (block_len, block_len), 1) - lax.broadcasted_iota(
        jnp.int32, (block_len, block_len), 0
    )
    dx_total = jnp.zeros((groups_here, per_group, block_len), jnp.float32)
    lag_buffer = jnp.zeros((groups_here, (spread_blocks + 2) * block_len), jnp.float32)
    current = local_grads
    for lag_block in range(spread_blocks + 1):
        if lag_block > 0:
            current = shifted(local_grads, "seq", -lag_block)
        dy_grouped = current.reshape(block_len, groups_here, per_group).transpose(1, 2, 0)
        lag_index = lag_block * block_len + offsets
        inside = (lag_index >= 0) & (lag_index < taps_total)
        picked = jnp.take(filt_rows, jnp.clip(lag_index, 0, taps_total - 1), axis=1)
        toeplitz = jnp.where(inside[None], picked, jnp.zeros((), jnp.bfloat16))
        dx_total = dx_total + jnp.einsum(
            "guv,gkv->gku", toeplitz, dy_grouped, preferred_element_type=jnp.float32
        )
        products = jnp.einsum(
            "gku,gkv->guv", x_reversed, dy_grouped, preferred_element_type=jnp.float32
        )
        start = lag_block * block_len
        lag_buffer = lag_buffer.at[:, start : start + 2 * block_len - 1].add(skewed_sums(products))
    partial_dh = lag_buffer[:, block_len - 1 : block_len - 1 + taps_total].T
    filter_grads = lax.psum_scatter(partial_dh, "seq", scatter_dimension=0, tiled=True)
    input_grads = dx_total.transpose(2, 0, 1).reshape(block_len, chan_width).astype(jnp.bfloat16)
    return (input_grads, filter_grads)


def xor_permute(value, axis, bits):
    pairs = [(source, source ^ bits) for source in range(lax.axis_size(axis))]
    return lax.ppermute(value, axis, pairs)


def turned_permute(value, axis, masks):
    pairs = [(source, source ^ masks[source % 2]) for source in range(lax.axis_size(axis))]
    return lax.ppermute(value, axis, pairs)


def partners(count):
    return [(count - step) % count for step in range(count)]


def fan_out(pieces, axis, unit):
    masks = partners(len(pieces))[1:]
    return [pieces[0]] + [xor_permute(p, axis, m * unit) for p, m in zip(pieces[1:], masks)]


def roll_left(value, steps):
    width = value.shape[-1]
    return pltpu.roll(value, (width - steps) % width, value.ndim - 1)


def place():
    seq = lax.axis_index("seq")
    return seq // 2, seq % 2, lax.axis_index("chan")


def rows_at(index, size):
    return pl.ds(pl.multiple_of(index * size, 16), size)


def fan_grads_kernel(n_seq, in_ref, out_ref):
    n_chan = out_ref.shape[0] // n_seq
    for seq in range(n_seq):
        for chan in range(n_chan):
            start = (chan * n_seq + seq) * LANES
            out_ref[seq * n_chan + chan] = in_ref[:, start : start + LANES]


def fan_inputs_kernel(x_own_ref, x_other_ref, f_own_ref, f_other_ref, *refs):
    *out_refs, taps_ref = refs
    chip, core, _ = place()
    block_len = x_own_ref.shape[0]
    taps_here, groups_here = f_own_ref.shape
    groups = groups_here // (2 * len(out_refs))
    rest = jnp.zeros((groups_here, LANES - taps_here), jnp.float32)
    for flip, f_ref in enumerate((f_own_ref, f_other_ref)):
        taps_ref[flip] = jnp.concatenate([f_ref[...].astype(jnp.float32).T, rest], axis=1)
    for bits, out_ref in zip(partners(len(out_refs)), out_refs):
        target = 2 * (chip ^ bits) + core
        columns = pl.ds(pl.multiple_of(target * LANES, LANES), LANES)
        out_ref[:block_len] = x_own_ref[:, columns]
        out_ref[block_len : 2 * block_len] = x_other_ref[:, columns]
        rows = pl.ds(pl.multiple_of(target * groups, groups), groups)
        taps = jnp.concatenate([taps_ref[0, rows], taps_ref[1, rows]], axis=0)
        out_ref[2 * block_len :] = taps.astype(jnp.bfloat16)


def toeplitz_kernel(n_seq, taps_here, *refs):
    chips = n_seq // 2
    in_refs = refs[:chips]
    toep_ref, x_ref, filt_ref = refs[chips:]
    block_len = x_ref.shape[0] // n_seq
    groups = toep_ref.shape[0] // STEP
    reach = toep_ref.shape[1]
    chip, core, _ = place()
    low = lax.broadcasted_iota(jnp.int32, (groups, LANES), 1) < taps_here
    for bits, in_ref in zip(partners(chips), in_refs):
        for flip in range(2):
            block = 2 * (chip ^ bits) + (core ^ flip)
            x_ref[rows_at(block, block_len)] = in_ref[flip * block_len : (flip + 1) * block_len]
        taps = in_ref[2 * block_len :].astype(jnp.float32)
        first = jnp.where(core == 0, taps[:groups], taps[groups:])
        second = jnp.where(core == 0, taps[groups:], taps[:groups])
        filt_ref[chip ^ bits] = jnp.where(low, first, pltpu.roll(second, taps_here, 1))
    tiles = [filt_ref[tile] for tile in range(chips)]
    filt = jnp.concatenate(tiles + [jnp.zeros((groups, LANES), jnp.float32)], axis=1)
    for group in range(groups):
        rows = jnp.broadcast_to(filt[group : group + 1], (STEP, reach))
        rows = pltpu.roll(rows, 0, 1, stride=1, stride_axis=0)
        toep_ref[group * STEP : (group + 1) * STEP] = rows.astype(jnp.bfloat16)


def group_of_lane(rows, width, groups):
    lane = lax.broadcasted_iota(jnp.int32, (rows, width), 1)
    return (lane % LANES) // (LANES // groups)


def filtered(dye_ref, start, toeplitz, groups):
    reach = toeplitz.shape[1]
    window = jnp.concatenate(
        [
            dye_ref[pl.ds(pl.multiple_of(start, STEP), reach)],
            dye_ref[pl.ds(pl.multiple_of(start + STEP, STEP), reach)],
        ],
        axis=1,
    )
    full = jnp.dot(toeplitz, window, preferred_element_type=jnp.float32)
    group2 = group_of_lane(STEP, 2 * LANES, groups)
    total = full[:STEP]
    for group in range(1, groups):
        total = jnp.where(group2 == group, full[group * STEP : (group + 1) * STEP], total)
    return jnp.concatenate([total[:, :LANES], total[:, LANES:]], axis=0).astype(jnp.bfloat16)


def tokens_of(seq, dye_ref, toep_ref, out_ref, at, block_len):
    toeplitz = toep_ref[...]
    groups = toeplitz.shape[0] // STEP
    for row in range(0, block_len, 2 * STEP):
        out_ref[at + row : at + row + 2 * STEP] = filtered(
            dye_ref, seq * block_len + row, toeplitz, groups
        )


def first_kernel(
    n_seq, taps_here, far, dy_ref, x_ref, toep_ref, dye_ref, taps_ref, out_ref, lag_ref
):
    chips = n_seq // 2
    tokens = dy_ref.shape[0]
    groups = toep_ref.shape[0] // STEP
    taps = n_seq * taps_here
    reach = taps + LANES
    chip, core, _ = place()

    dye_ref[:tokens] = dy_ref[...]
    dye_ref[tokens:] = dy_ref[:reach]

    deep = DEPTH // LANES
    group_in = group_of_lane(STEP, DEPTH, groups)
    for at in range(0, tokens, STEP * deep):
        starts = range(at, at + STEP * deep, STEP)
        windows = jnp.concatenate([dye_ref[row : row + reach] for row in starts], axis=1)
        inputs = jnp.concatenate([x_ref[row : row + STEP] for row in starts], axis=1)
        masked = jnp.concatenate(
            [jnp.where(group_in == group, inputs, jnp.zeros_like(inputs)) for group in range(groups)],
            axis=0,
        )
        part = lax.dot_general(
            masked, windows, (((1,), (1,)), ((), ())), preferred_element_type=jnp.float32
        )
        if at == 0:
            lag_ref[...] = part
        else:
            lag_ref[...] += part

    eights = []
    for group in range(groups):
        at = group * STEP
        rows = lag_ref[at : at + 8]
        for high in range(1, STEP // 8):
            rows = rows + roll_left(lag_ref[at + 8 * high : at + 8 * high + 8], 8 * high)
        eights.append(rows)
    skew = jnp.concatenate(eights, axis=0)
    row_in = lax.broadcasted_iota(jnp.int32, skew.shape, 0) % 8
    for bit in (1, 2, 4):
        skew = jnp.where((row_in & bit) != 0, roll_left(skew, bit), skew)
    dh = skew.reshape(groups, 8, reach).sum(axis=1)[:, :taps]

    high = dh.astype(jnp.bfloat16).astype(jnp.float32)
    rest = dh - high
    low = lax.broadcasted_iota(jnp.int32, (groups, LANES), 1) < taps_here
    for to_chip in range(chips):
        columns = slice(to_chip * LANES, (to_chip + 1) * LANES)
        top, bottom = high[:, columns], rest[:, columns]
        even = jnp.where(low, top, pltpu.roll(bottom, taps_here, 1))
        odd = jnp.where(low, pltpu.roll(top, taps_here, 1), bottom)
        mine = jnp.where(core == 0, even, odd)
        other = jnp.where(core == 0, odd, even)
        taps_ref[to_chip] = jnp.concatenate([mine, other], axis=0).astype(jnp.bfloat16)

    block_len = (out_ref.shape[0] - EXTRA) // 2
    for flip in range(2):
        seq = 2 * (chip ^ far) + (core ^ flip)
        tokens_of(seq, dye_ref, toep_ref, out_ref, flip * block_len, block_len)
    out_ref[2 * block_len :] = taps_ref[chip ^ far]


def half_of(taps, flip):
    groups = EXTRA // 2
    return taps.astype(jnp.float32)[flip * groups : (flip + 1) * groups]


def stacked(rows):
    return jnp.concatenate(rows, axis=0).astype(jnp.bfloat16)


def near_kernel(masks, flip, dye_ref, toep_ref, taps_ref, out_ref):
    chip, core, _ = place()
    block_len = (out_ref.shape[0] - len(masks) * EXTRA // 2) // len(masks)
    for index, bits in enumerate(masks):
        seq = 2 * (chip ^ bits) + (core ^ flip)
        tokens_of(seq, dye_ref, toep_ref, out_ref, index * block_len, block_len)
    out_ref[len(masks) * block_len :] = stacked(
        [half_of(taps_ref[chip ^ bits], flip) for bits in masks]
    )


def near_pieces_kernel(keep_ref, got_ref, *out_refs):
    _, core, _ = place()
    count = len(out_refs)
    block_len = (out_refs[0].shape[0] - EXTRA) // 2
    groups = EXTRA // 2
    keep_taps = keep_ref[count * block_len :].astype(jnp.float32)
    got_taps = got_ref[count * block_len :].astype(jnp.float32)
    taps = [
        stacked(
            [value[index * groups : (index + 1) * groups] for value in (keep_taps, got_taps)]
        )
        for index in range(count)
    ]
    for index, out_ref in enumerate(out_refs):
        other = (index + 1) % count
        out_ref[:block_len] = keep_ref[rows_at((index + core) % count, block_len)]
        out_ref[block_len : 2 * block_len] = got_ref[rows_at((index + core) % count, block_len)]
        out_ref[2 * block_len :] = jnp.where(core == 0, taps[index], taps[other])


def own_kernel(dye_ref, toep_ref, taps_ref, out_ref):
    chip, core, _ = place()
    block_len = (out_ref.shape[0] - EXTRA) // 2
    for flip in range(2):
        seq = 2 * chip + (core ^ flip)
        tokens_of(seq, dye_ref, toep_ref, out_ref, flip * block_len, block_len)
    out_ref[2 * block_len :] = taps_ref[chip]


def swap_kernel(*refs):
    *in_refs, out_ref = refs
    block_len = (in_refs[0].shape[0] - EXTRA) // 2
    for index, in_ref in enumerate(in_refs):
        out_ref[index * block_len : (index + 1) * block_len] = in_ref[block_len : 2 * block_len]
    out_ref[len(in_refs) * block_len :] = stacked(
        [half_of(in_ref[2 * block_len :], 1) for in_ref in in_refs]
    )


def unpack_kernel(masks, *refs):
    own_ref, far_ref, swapped_ref, *near_refs, dx_ref, dh_ref, rows_ref = refs
    chip, core, _ = place()
    block_len = dx_ref.shape[0]
    taps_here, groups_here = dh_ref.shape
    groups = EXTRA // 2

    def put(from_chip, flip, tokens, taps):
        source = 2 * from_chip + (core ^ flip)
        dx_ref[:, pl.ds(pl.multiple_of(source * LANES, LANES), LANES)] = tokens
        rows_ref[pl.ds(pl.multiple_of(source * groups, groups), groups)] = taps + pltpu.roll(
            taps, taps_here, 1
        )

    swapped_taps = swapped_ref[2 * block_len :]
    for index, ref in enumerate((own_ref, far_ref)):
        put(chip ^ masks[index], 0, ref[:block_len], half_of(ref[2 * block_len :], 0))
        rows = swapped_ref[index * block_len : (index + 1) * block_len]
        put(chip ^ masks[index], 1, rows, half_of(swapped_taps, index))
    near = masks[2:]
    for index, ref in enumerate(near_refs):
        bits = jnp.where(core == 0, near[index], near[(index + 1) % len(near)])
        for flip in range(2):
            rows = ref[flip * block_len : (flip + 1) * block_len]
            put(chip ^ bits, flip, rows, half_of(ref[2 * block_len :], flip))
    dh_ref[...] = rows_ref[...].T[:taps_here]


def local_call(kernel, out_shape, operands, name, scratch=()):
    whole = pl.BlockSpec(memory_space=pltpu.VMEM)
    return pl.pallas_call(
        kernel,
        out_shape=out_shape,
        in_specs=[whole] * len(operands),
        out_specs=[whole] * len(out_shape),
        scratch_shapes=scratch,
        compiler_params=pltpu.CompilerParams(vmem_limit_bytes=VMEM_LIMIT),
        name=name,
    )(*operands)


def by_channels(n_seq, n_chan, out_grads, layer_inputs, filters):
    rows = out_grads.shape[0]
    block_len = layer_inputs.shape[0]
    taps_here, groups_here = filters.shape
    groups = groups_here // n_seq
    tokens = n_seq * block_len
    taps = n_seq * taps_here
    chips = n_seq // 2
    masks = partners(chips)

    def half(*shape):
        return jax.ShapeDtypeStruct(shape, jnp.bfloat16)

    unit = half(2 * block_len + EXTRA, LANES)
    x_other = xor_permute(layer_inputs, "seq", 1)
    f_other = xor_permute(filters, "seq", 1)
    (dy,) = local_call(
        functools.partial(fan_grads_kernel, n_seq),
        [half(n_seq * n_chan, rows, LANES)],
        (out_grads,),
        "fan_grads",
    )
    dy = lax.all_to_all(dy, ("seq", "chan"), split_axis=0, concat_axis=0, tiled=True)
    pieces = local_call(
        fan_inputs_kernel,
        [unit] * chips,
        (layer_inputs, x_other, filters, f_other),
        "fan_inputs",
        [pltpu.VMEM((2, groups_here, LANES), jnp.float32)],
    )
    toeplitz, x = local_call(
        functools.partial(toeplitz_kernel, n_seq, taps_here),
        [half(groups * STEP, taps + LANES), half(tokens, LANES)],
        fan_out(pieces, "seq", 2),
        "toeplitz",
        [pltpu.VMEM((chips, groups, LANES), jnp.float32)],
    )
    dye, tap_parts, far = local_call(
        functools.partial(first_kernel, n_seq, taps_here, masks[1]),
        [half(tokens + taps + LANES, LANES), half(chips, EXTRA, LANES), unit],
        (dy.reshape(tokens, LANES), x, toeplitz),
        "first",
        [pltpu.VMEM((groups * STEP, taps + LANES), jnp.float32)],
    )
    far = xor_permute(far, "seq", 2 * masks[1])
    near = masks[2:]
    near_shape = half(len(near) * (block_len + EXTRA // 2), LANES)
    (send,) = local_call(
        functools.partial(near_kernel, near, 1), [near_shape], (dye, toeplitz, tap_parts), "near_swap"
    )
    got = xor_permute(send, "seq", 1)
    (keep,) = local_call(
        functools.partial(near_kernel, near, 0), [near_shape], (dye, toeplitz, tap_parts), "near_keep"
    )
    pieces = local_call(near_pieces_kernel, [unit] * len(near), (keep, got), "near_pieces")
    pieces = [
        turned_permute(piece, "seq", [2 * bits for bits in near[index:] + near[:index]])
        for index, piece in enumerate(pieces)
    ]
    far, tap_parts = lax.optimization_barrier((far, tap_parts))
    (own,) = local_call(own_kernel, [unit], (dye, toeplitz, tap_parts), "own")
    (send,) = local_call(
        swap_kernel, [half(2 * block_len + EXTRA, LANES)], (own, far), "swap"
    )
    return local_call(
        functools.partial(unpack_kernel, masks),
        [
            half(block_len, n_seq * LANES),
            jax.ShapeDtypeStruct((taps_here, groups_here), jnp.float32),
        ],
        (own, far, xor_permute(send, "seq", 1), *pieces),
        "unpack",
        [pltpu.VMEM((groups_here, LANES), jnp.float32)],
    )


def solution(mesh):
    n_seq, n_chan = mesh.shape["seq"], mesh.shape["chan"]

    def on_device(out_grads, layer_inputs, filters):
        taps_here, groups_here = filters.shape
        fits = (
            n_seq == 8
            and n_chan in (2, 4, 8)
            and layer_inputs.shape[1] == n_seq * LANES
            and groups_here == 8 * n_seq
            and 2 * taps_here == LANES
            and out_grads.shape[0] % 16 == 0
            and layer_inputs.shape[0] % (2 * STEP) == 0
            and n_seq * layer_inputs.shape[0] % (STEP * DEPTH // LANES) == 0
            and n_seq * taps_here + LANES <= n_seq * layer_inputs.shape[0]
        )
        if fits:
            return tuple(by_channels(n_seq, n_chan, out_grads, layer_inputs, filters))
        return by_tokens(out_grads, layer_inputs, filters)

    in_specs = (P(("seq", "chan"), None), P("seq", "chan"), P("seq", "chan"))
    out_specs = (P("seq", "chan"), P("seq", "chan"))
    return jax.shard_map(
        on_device, mesh=mesh, in_specs=in_specs, out_specs=out_specs, check_vma=False
    )
```

```python
import functools

import jax
import jax.numpy as jnp
from jax import lax
from jax.experimental import pallas as pl
from jax.experimental.pallas import tpu as pltpu
from jax.sharding import PartitionSpec as P

LANES = 128
STEP = 32
SLAB = 64
EXTRA = 16
DEPTH = 1024
VMEM_LIMIT = 40 * 1024 * 1024


def shifted(value, axis, steps):
    count = lax.axis_size(axis)
    pairs = [(source, (source + steps) % count) for source in range(count)]
    return lax.ppermute(value, axis, pairs)


def skewed_sums(products):
    groups_here, length, _ = products.shape
    padded = jnp.pad(products, ((0, 0), (0, 0), (0, length)))
    flat = padded.reshape(groups_here, 2 * length * length)[:, : length * (2 * length - 1)]
    return flat.reshape(groups_here, length, 2 * length - 1).sum(axis=1)


def by_tokens(out_grads, layer_inputs, filters):
    local_grads = lax.all_to_all(out_grads, "chan", split_axis=1, concat_axis=0, tiled=True)
    taps_all = lax.all_gather(filters, "seq", axis=0, tiled=True)
    block_len = local_grads.shape[0]
    chan_width = local_grads.shape[1]
    groups_here = filters.shape[1]
    per_group = chan_width // groups_here
    taps_total = taps_all.shape[0]
    spread_blocks = taps_total // block_len
    filt_rows = taps_all.T
    x_reversed = layer_inputs[::-1].reshape(block_len, groups_here, per_group).transpose(1, 2, 0)
    offsets = lax.broadcasted_iota(jnp.int32, (block_len, block_len), 1) - lax.broadcasted_iota(
        jnp.int32, (block_len, block_len), 0
    )
    dx_total = jnp.zeros((groups_here, per_group, block_len), jnp.float32)
    lag_buffer = jnp.zeros((groups_here, (spread_blocks + 2) * block_len), jnp.float32)
    current = local_grads
    for lag_block in range(spread_blocks + 1):
        if lag_block > 0:
            current = shifted(local_grads, "seq", -lag_block)
        dy_grouped = current.reshape(block_len, groups_here, per_group).transpose(1, 2, 0)
        lag_index = lag_block * block_len + offsets
        inside = (lag_index >= 0) & (lag_index < taps_total)
        picked = jnp.take(filt_rows, jnp.clip(lag_index, 0, taps_total - 1), axis=1)
        toeplitz = jnp.where(inside[None], picked, jnp.zeros((), jnp.bfloat16))
        dx_total = dx_total + jnp.einsum(
            "guv,gkv->gku", toeplitz, dy_grouped, preferred_element_type=jnp.float32
        )
        products = jnp.einsum(
            "gku,gkv->guv", x_reversed, dy_grouped, preferred_element_type=jnp.float32
        )
        start = lag_block * block_len
        lag_buffer = lag_buffer.at[:, start : start + 2 * block_len - 1].add(skewed_sums(products))
    partial_dh = lag_buffer[:, block_len - 1 : block_len - 1 + taps_total].T
    filter_grads = lax.psum_scatter(partial_dh, "seq", scatter_dimension=0, tiled=True)
    input_grads = dx_total.transpose(2, 0, 1).reshape(block_len, chan_width).astype(jnp.bfloat16)
    return (input_grads, filter_grads)


def xor_permute(value, axis, bits):
    pairs = [(source, source ^ bits) for source in range(lax.axis_size(axis))]
    return lax.ppermute(value, axis, pairs)


def turned_permute(value, axis, masks):
    pairs = [(source, source ^ masks[source % 2]) for source in range(lax.axis_size(axis))]
    return lax.ppermute(value, axis, pairs)


def partners(count):
    return [(count - step) % count for step in range(count)]


def fan_out(pieces, axis, unit):
    masks = partners(len(pieces))[1:]
    return [pieces[0]] + [xor_permute(p, axis, m * unit) for p, m in zip(pieces[1:], masks)]


def roll_left(value, steps):
    width = value.shape[-1]
    return pltpu.roll(value, (width - steps) % width, value.ndim - 1)


def place():
    seq = lax.axis_index("seq")
    return seq // 2, seq % 2, lax.axis_index("chan")


def rows_at(index, size):
    return pl.ds(pl.multiple_of(index * size, 16), size)


def fan_grads_kernel(n_seq, in_ref, out_ref):
    n_chan = out_ref.shape[0] // n_seq
    for seq in range(n_seq):
        for chan in range(n_chan):
            start = (chan * n_seq + seq) * LANES
            out_ref[seq * n_chan + chan] = in_ref[:, start : start + LANES]


def fan_inputs_kernel(x_own_ref, x_other_ref, f_own_ref, f_other_ref, *refs):
    *out_refs, taps_ref = refs
    chip, core, _ = place()
    block_len = x_own_ref.shape[0]
    taps_here, groups_here = f_own_ref.shape
    groups = groups_here // (2 * len(out_refs))
    rest = jnp.zeros((groups_here, LANES - taps_here), jnp.float32)
    for flip, f_ref in enumerate((f_own_ref, f_other_ref)):
        taps_ref[flip] = jnp.concatenate([f_ref[...].astype(jnp.float32).T, rest], axis=1)
    for bits, out_ref in zip(partners(len(out_refs)), out_refs):
        target = 2 * (chip ^ bits) + core
        columns = pl.ds(pl.multiple_of(target * LANES, LANES), LANES)
        out_ref[:block_len] = x_own_ref[:, columns]
        out_ref[block_len : 2 * block_len] = x_other_ref[:, columns]
        rows = pl.ds(pl.multiple_of(target * groups, groups), groups)
        taps = jnp.concatenate([taps_ref[0, rows], taps_ref[1, rows]], axis=0)
        out_ref[2 * block_len :] = taps.astype(jnp.bfloat16)


def toeplitz_kernel(n_seq, taps_here, *refs):
    chips = n_seq // 2
    in_refs = refs[:chips]
    toep_ref, x_ref, filt_ref = refs[chips:]
    block_len = x_ref.shape[0] // n_seq
    groups = toep_ref.shape[0] // SLAB
    reach = toep_ref.shape[1]
    chip, core, _ = place()
    low = lax.broadcasted_iota(jnp.int32, (groups, LANES), 1) < taps_here
    for bits, in_ref in zip(partners(chips), in_refs):
        for flip in range(2):
            block = 2 * (chip ^ bits) + (core ^ flip)
            x_ref[rows_at(block, block_len)] = in_ref[flip * block_len : (flip + 1) * block_len]
        taps = in_ref[2 * block_len :].astype(jnp.float32)
        first = jnp.where(core == 0, taps[:groups], taps[groups:])
        second = jnp.where(core == 0, taps[groups:], taps[:groups])
        filt_ref[chip ^ bits] = jnp.where(low, first, pltpu.roll(second, taps_here, 1))
    tiles = [filt_ref[tile] for tile in range(chips)]
    filt = jnp.concatenate(tiles + [jnp.zeros((groups, LANES), jnp.float32)], axis=1)
    for group in range(groups):
        rows = jnp.broadcast_to(filt[group : group + 1], (SLAB, reach))
        rows = pltpu.roll(rows, 0, 1, stride=1, stride_axis=0)
        toep_ref[group * SLAB : (group + 1) * SLAB] = rows.astype(jnp.bfloat16)


def group_of_lane(rows, width, groups):
    lane = lax.broadcasted_iota(jnp.int32, (rows, width), 1)
    return (lane % LANES) // (LANES // groups)


def filtered(dye_ref, start, toeplitz, groups):
    reach = toeplitz.shape[1]
    window = jnp.concatenate(
        [
            dye_ref[pl.ds(pl.multiple_of(start, SLAB), reach)],
            dye_ref[pl.ds(pl.multiple_of(start + SLAB, SLAB), reach)],
        ],
        axis=1,
    )
    full = jnp.dot(toeplitz, window, preferred_element_type=jnp.float32)
    group2 = group_of_lane(SLAB, 2 * LANES, groups)
    total = full[:SLAB]
    for group in range(1, groups):
        total = jnp.where(group2 == group, full[group * SLAB : (group + 1) * SLAB], total)
    return jnp.concatenate([total[:, :LANES], total[:, LANES:]], axis=0).astype(jnp.bfloat16)


def tokens_of(seq, dye_ref, toep_ref, out_ref, at, block_len):
    toeplitz = toep_ref[...]
    groups = toeplitz.shape[0] // SLAB
    for row in range(0, block_len, 2 * SLAB):
        out_ref[at + row : at + row + 2 * SLAB] = filtered(
            dye_ref, seq * block_len + row, toeplitz, groups
        )


def first_kernel(
    n_seq, taps_here, far, dy_ref, x_ref, toep_ref, dye_ref, taps_ref, out_ref, lag_ref
):
    chips = n_seq // 2
    tokens = dy_ref.shape[0]
    groups = toep_ref.shape[0] // SLAB
    taps = n_seq * taps_here
    reach = taps + LANES
    chip, core, _ = place()

    dye_ref[:tokens] = dy_ref[...]
    dye_ref[tokens:] = dy_ref[:reach]

    deep = DEPTH // LANES
    group_in = group_of_lane(STEP, DEPTH, groups)
    for at in range(0, tokens, STEP * deep):
        starts = range(at, at + STEP * deep, STEP)
        windows = jnp.concatenate([dye_ref[row : row + reach] for row in starts], axis=1)
        inputs = jnp.concatenate([x_ref[row : row + STEP] for row in starts], axis=1)
        masked = jnp.concatenate(
            [jnp.where(group_in == group, inputs, jnp.zeros_like(inputs)) for group in range(groups)],
            axis=0,
        )
        part = lax.dot_general(
            windows, masked, (((1,), (1,)), ((), ())), preferred_element_type=jnp.float32
        )
        if at == 0:
            lag_ref[...] = part
        else:
            lag_ref[...] += part

    lags = lag_ref[...].T
    eights = []
    for group in range(groups):
        at = group * STEP
        rows = lags[at : at + 8]
        for high in range(1, STEP // 8):
            rows = rows + roll_left(lags[at + 8 * high : at + 8 * high + 8], 8 * high)
        eights.append(rows)
    skew = jnp.concatenate(eights, axis=0)
    row_in = lax.broadcasted_iota(jnp.int32, skew.shape, 0) % 8
    for bit in (1, 2, 4):
        skew = jnp.where((row_in & bit) != 0, roll_left(skew, bit), skew)
    dh = skew.reshape(groups, 8, reach).sum(axis=1)[:, :taps]

    high = dh.astype(jnp.bfloat16).astype(jnp.float32)
    rest = dh - high
    low = lax.broadcasted_iota(jnp.int32, (groups, LANES), 1) < taps_here
    for to_chip in range(chips):
        columns = slice(to_chip * LANES, (to_chip + 1) * LANES)
        top, bottom = high[:, columns], rest[:, columns]
        even = jnp.where(low, top, pltpu.roll(bottom, taps_here, 1))
        odd = jnp.where(low, pltpu.roll(top, taps_here, 1), bottom)
        mine = jnp.where(core == 0, even, odd)
        other = jnp.where(core == 0, odd, even)
        taps_ref[to_chip] = jnp.concatenate([mine, other], axis=0).astype(jnp.bfloat16)

    block_len = (out_ref.shape[0] - EXTRA) // 2
    for flip in range(2):
        seq = 2 * (chip ^ far) + (core ^ flip)
        tokens_of(seq, dye_ref, toep_ref, out_ref, flip * block_len, block_len)
    out_ref[2 * block_len :] = taps_ref[chip ^ far]


def half_of(taps, flip):
    groups = EXTRA // 2
    return taps.astype(jnp.float32)[flip * groups : (flip + 1) * groups]


def stacked(rows):
    return jnp.concatenate(rows, axis=0).astype(jnp.bfloat16)


def near_kernel(masks, flip, dye_ref, toep_ref, taps_ref, out_ref):
    chip, core, _ = place()
    block_len = (out_ref.shape[0] - len(masks) * EXTRA // 2) // len(masks)
    for index, bits in enumerate(masks):
        seq = 2 * (chip ^ bits) + (core ^ flip)
        tokens_of(seq, dye_ref, toep_ref, out_ref, index * block_len, block_len)
    out_ref[len(masks) * block_len :] = stacked(
        [half_of(taps_ref[chip ^ bits], flip) for bits in masks]
    )


def near_pieces_kernel(keep_ref, got_ref, *out_refs):
    _, core, _ = place()
    count = len(out_refs)
    block_len = (out_refs[0].shape[0] - EXTRA) // 2
    groups = EXTRA // 2
    keep_taps = keep_ref[count * block_len :].astype(jnp.float32)
    got_taps = got_ref[count * block_len :].astype(jnp.float32)
    taps = [
        stacked(
            [value[index * groups : (index + 1) * groups] for value in (keep_taps, got_taps)]
        )
        for index in range(count)
    ]
    for index, out_ref in enumerate(out_refs):
        other = (index + 1) % count
        out_ref[:block_len] = keep_ref[rows_at((index + core) % count, block_len)]
        out_ref[block_len : 2 * block_len] = got_ref[rows_at((index + core) % count, block_len)]
        out_ref[2 * block_len :] = jnp.where(core == 0, taps[index], taps[other])


def own_kernel(dye_ref, toep_ref, taps_ref, out_ref):
    chip, core, _ = place()
    block_len = (out_ref.shape[0] - EXTRA) // 2
    for flip in range(2):
        seq = 2 * chip + (core ^ flip)
        tokens_of(seq, dye_ref, toep_ref, out_ref, flip * block_len, block_len)
    out_ref[2 * block_len :] = taps_ref[chip]


def swap_kernel(*refs):
    *in_refs, out_ref = refs
    block_len = (in_refs[0].shape[0] - EXTRA) // 2
    for index, in_ref in enumerate(in_refs):
        out_ref[index * block_len : (index + 1) * block_len] = in_ref[block_len : 2 * block_len]
    out_ref[len(in_refs) * block_len :] = stacked(
        [half_of(in_ref[2 * block_len :], 1) for in_ref in in_refs]
    )


def unpack_kernel(masks, *refs):
    own_ref, far_ref, swapped_ref, *near_refs, dx_ref, dh_ref, rows_ref = refs
    chip, core, _ = place()
    block_len = dx_ref.shape[0]
    taps_here, groups_here = dh_ref.shape
    groups = EXTRA // 2

    def put(from_chip, flip, tokens, taps):
        source = 2 * from_chip + (core ^ flip)
        dx_ref[:, pl.ds(pl.multiple_of(source * LANES, LANES), LANES)] = tokens
        rows_ref[pl.ds(pl.multiple_of(source * groups, groups), groups)] = taps + pltpu.roll(
            taps, taps_here, 1
        )

    swapped_taps = swapped_ref[2 * block_len :]
    for index, ref in enumerate((own_ref, far_ref)):
        put(chip ^ masks[index], 0, ref[:block_len], half_of(ref[2 * block_len :], 0))
        rows = swapped_ref[index * block_len : (index + 1) * block_len]
        put(chip ^ masks[index], 1, rows, half_of(swapped_taps, index))
    near = masks[2:]
    for index, ref in enumerate(near_refs):
        bits = jnp.where(core == 0, near[index], near[(index + 1) % len(near)])
        for flip in range(2):
            rows = ref[flip * block_len : (flip + 1) * block_len]
            put(chip ^ bits, flip, rows, half_of(ref[2 * block_len :], flip))
    dh_ref[...] = rows_ref[...].T[:taps_here]


def local_call(kernel, out_shape, operands, name, scratch=()):
    whole = pl.BlockSpec(memory_space=pltpu.VMEM)
    return pl.pallas_call(
        kernel,
        out_shape=out_shape,
        in_specs=[whole] * len(operands),
        out_specs=[whole] * len(out_shape),
        scratch_shapes=scratch,
        compiler_params=pltpu.CompilerParams(vmem_limit_bytes=VMEM_LIMIT),
        name=name,
    )(*operands)


def by_channels(n_seq, n_chan, out_grads, layer_inputs, filters):
    rows = out_grads.shape[0]
    block_len = layer_inputs.shape[0]
    taps_here, groups_here = filters.shape
    groups = groups_here // n_seq
    tokens = n_seq * block_len
    taps = n_seq * taps_here
    chips = n_seq // 2
    masks = partners(chips)

    def half(*shape):
        return jax.ShapeDtypeStruct(shape, jnp.bfloat16)

    unit = half(2 * block_len + EXTRA, LANES)
    x_other = xor_permute(layer_inputs, "seq", 1)
    f_other = xor_permute(filters, "seq", 1)
    (dy,) = local_call(
        functools.partial(fan_grads_kernel, n_seq),
        [half(n_seq * n_chan, rows, LANES)],
        (out_grads,),
        "fan_grads",
    )
    dy = lax.all_to_all(dy, ("seq", "chan"), split_axis=0, concat_axis=0, tiled=True)
    pieces = local_call(
        fan_inputs_kernel,
        [unit] * chips,
        (layer_inputs, x_other, filters, f_other),
        "fan_inputs",
        [pltpu.VMEM((2, groups_here, LANES), jnp.float32)],
    )
    toeplitz, x = local_call(
        functools.partial(toeplitz_kernel, n_seq, taps_here),
        [half(groups * SLAB, taps + LANES), half(tokens, LANES)],
        fan_out(pieces, "seq", 2),
        "toeplitz",
        [pltpu.VMEM((chips, groups, LANES), jnp.float32)],
    )
    dye, tap_parts, far = local_call(
        functools.partial(first_kernel, n_seq, taps_here, masks[1]),
        [half(tokens + taps + LANES, LANES), half(chips, EXTRA, LANES), unit],
        (dy.reshape(tokens, LANES), x, toeplitz),
        "first",
        [pltpu.VMEM((taps + LANES, groups * STEP), jnp.float32)],
    )
    far = xor_permute(far, "seq", 2 * masks[1])
    near = masks[2:]
    near_shape = half(len(near) * (block_len + EXTRA // 2), LANES)
    (send,) = local_call(
        functools.partial(near_kernel, near, 1), [near_shape], (dye, toeplitz, tap_parts), "near_swap"
    )
    got = xor_permute(send, "seq", 1)
    (keep,) = local_call(
        functools.partial(near_kernel, near, 0), [near_shape], (dye, toeplitz, tap_parts), "near_keep"
    )
    pieces = local_call(near_pieces_kernel, [unit] * len(near), (keep, got), "near_pieces")
    pieces = [
        turned_permute(piece, "seq", [2 * bits for bits in near[index:] + near[:index]])
        for index, piece in enumerate(pieces)
    ]
    far, tap_parts = lax.optimization_barrier((far, tap_parts))
    (own,) = local_call(own_kernel, [unit], (dye, toeplitz, tap_parts), "own")
    (send,) = local_call(
        swap_kernel, [half(2 * block_len + EXTRA, LANES)], (own, far), "swap"
    )
    return local_call(
        functools.partial(unpack_kernel, masks),
        [
            half(block_len, n_seq * LANES),
            jax.ShapeDtypeStruct((taps_here, groups_here), jnp.float32),
        ],
        (own, far, xor_permute(send, "seq", 1), *pieces),
        "unpack",
        [pltpu.VMEM((groups_here, LANES), jnp.float32)],
    )


def solution(mesh):
    n_seq, n_chan = mesh.shape["seq"], mesh.shape["chan"]

    def on_device(out_grads, layer_inputs, filters):
        taps_here, groups_here = filters.shape
        fits = (
            n_seq == 8
            and n_chan in (2, 4, 8)
            and layer_inputs.shape[1] == n_seq * LANES
            and groups_here == 8 * n_seq
            and 2 * taps_here == LANES
            and out_grads.shape[0] % 16 == 0
            and layer_inputs.shape[0] % (2 * SLAB) == 0
            and n_seq * layer_inputs.shape[0] % (STEP * DEPTH // LANES) == 0
            and n_seq * taps_here + LANES <= n_seq * layer_inputs.shape[0]
        )
        if fits:
            return tuple(by_channels(n_seq, n_chan, out_grads, layer_inputs, filters))
        return by_tokens(out_grads, layer_inputs, filters)

    in_specs = (P(("seq", "chan"), None), P("seq", "chan"), P("seq", "chan"))
    out_specs = (P("seq", "chan"), P("seq", "chan"))
    return jax.shard_map(
        on_device, mesh=mesh, in_specs=in_specs, out_specs=out_specs, check_vma=False
    )
```

```python
import functools

import jax
import jax.numpy as jnp
from jax import lax
from jax.experimental import pallas as pl
from jax.experimental.pallas import tpu as pltpu
from jax.sharding import PartitionSpec as P

LANES = 128
STEP = 32
SLAB = 64
EXTRA = 16
DEPTH = 1024
VMEM_LIMIT = 40 * 1024 * 1024


def shifted(value, axis, steps):
    count = lax.axis_size(axis)
    pairs = [(source, (source + steps) % count) for source in range(count)]
    return lax.ppermute(value, axis, pairs)


def skewed_sums(products):
    groups_here, length, _ = products.shape
    padded = jnp.pad(products, ((0, 0), (0, 0), (0, length)))
    flat = padded.reshape(groups_here, 2 * length * length)[:, : length * (2 * length - 1)]
    return flat.reshape(groups_here, length, 2 * length - 1).sum(axis=1)


def by_tokens(out_grads, layer_inputs, filters):
    local_grads = lax.all_to_all(out_grads, "chan", split_axis=1, concat_axis=0, tiled=True)
    taps_all = lax.all_gather(filters, "seq", axis=0, tiled=True)
    block_len = local_grads.shape[0]
    chan_width = local_grads.shape[1]
    groups_here = filters.shape[1]
    per_group = chan_width // groups_here
    taps_total = taps_all.shape[0]
    spread_blocks = taps_total // block_len
    filt_rows = taps_all.T
    x_reversed = layer_inputs[::-1].reshape(block_len, groups_here, per_group).transpose(1, 2, 0)
    offsets = lax.broadcasted_iota(jnp.int32, (block_len, block_len), 1) - lax.broadcasted_iota(
        jnp.int32, (block_len, block_len), 0
    )
    dx_total = jnp.zeros((groups_here, per_group, block_len), jnp.float32)
    lag_buffer = jnp.zeros((groups_here, (spread_blocks + 2) * block_len), jnp.float32)
    current = local_grads
    for lag_block in range(spread_blocks + 1):
        if lag_block > 0:
            current = shifted(local_grads, "seq", -lag_block)
        dy_grouped = current.reshape(block_len, groups_here, per_group).transpose(1, 2, 0)
        lag_index = lag_block * block_len + offsets
        inside = (lag_index >= 0) & (lag_index < taps_total)
        picked = jnp.take(filt_rows, jnp.clip(lag_index, 0, taps_total - 1), axis=1)
        toeplitz = jnp.where(inside[None], picked, jnp.zeros((), jnp.bfloat16))
        dx_total = dx_total + jnp.einsum(
            "guv,gkv->gku", toeplitz, dy_grouped, preferred_element_type=jnp.float32
        )
        products = jnp.einsum(
            "gku,gkv->guv", x_reversed, dy_grouped, preferred_element_type=jnp.float32
        )
        start = lag_block * block_len
        lag_buffer = lag_buffer.at[:, start : start + 2 * block_len - 1].add(skewed_sums(products))
    partial_dh = lag_buffer[:, block_len - 1 : block_len - 1 + taps_total].T
    filter_grads = lax.psum_scatter(partial_dh, "seq", scatter_dimension=0, tiled=True)
    input_grads = dx_total.transpose(2, 0, 1).reshape(block_len, chan_width).astype(jnp.bfloat16)
    return (input_grads, filter_grads)


def xor_permute(value, axis, bits):
    pairs = [(source, source ^ bits) for source in range(lax.axis_size(axis))]
    return lax.ppermute(value, axis, pairs)


def turned_permute(value, axis, masks):
    pairs = [(source, source ^ masks[source % 2]) for source in range(lax.axis_size(axis))]
    return lax.ppermute(value, axis, pairs)


def partners(count):
    return [(count - step) % count for step in range(count)]


def fan_out(pieces, axis, unit):
    masks = partners(len(pieces))[1:]
    return [pieces[0]] + [xor_permute(p, axis, m * unit) for p, m in zip(pieces[1:], masks)]


def roll_left(value, steps):
    width = value.shape[-1]
    return pltpu.roll(value, (width - steps) % width, value.ndim - 1)


def place():
    seq = lax.axis_index("seq")
    return seq // 2, seq % 2, lax.axis_index("chan")


def rows_at(index, size):
    return pl.ds(pl.multiple_of(index * size, 16), size)


def fan_grads_kernel(n_seq, in_ref, out_ref):
    n_chan = out_ref.shape[0] // n_seq
    for seq in range(n_seq):
        for chan in range(n_chan):
            start = (chan * n_seq + seq) * LANES
            out_ref[seq * n_chan + chan] = in_ref[:, start : start + LANES]


def fan_inputs_kernel(x_own_ref, x_other_ref, f_own_ref, f_other_ref, *refs):
    *out_refs, taps_ref = refs
    chip, core, _ = place()
    block_len = x_own_ref.shape[0]
    taps_here, groups_here = f_own_ref.shape
    groups = groups_here // (2 * len(out_refs))
    rest = jnp.zeros((groups_here, LANES - taps_here), jnp.float32)
    for flip, f_ref in enumerate((f_own_ref, f_other_ref)):
        taps_ref[flip] = jnp.concatenate([f_ref[...].astype(jnp.float32).T, rest], axis=1)
    for bits, out_ref in zip(partners(len(out_refs)), out_refs):
        target = 2 * (chip ^ bits) + core
        columns = pl.ds(pl.multiple_of(target * LANES, LANES), LANES)
        out_ref[:block_len] = x_own_ref[:, columns]
        out_ref[block_len : 2 * block_len] = x_other_ref[:, columns]
        rows = pl.ds(pl.multiple_of(target * groups, groups), groups)
        taps = jnp.concatenate([taps_ref[0, rows], taps_ref[1, rows]], axis=0)
        out_ref[2 * block_len :] = taps.astype(jnp.bfloat16)


def place_inputs(in_refs, taps_here, x_ref, filt_ref):
    block_len = (in_refs[0].shape[0] - EXTRA) // 2
    groups = EXTRA // 2
    chip, core, _ = place()
    low = lax.broadcasted_iota(jnp.int32, (groups, LANES), 1) < taps_here
    for bits, in_ref in zip(partners(len(in_refs)), in_refs):
        for flip in range(2):
            block = 2 * (chip ^ bits) + (core ^ flip)
            x_ref[rows_at(block, block_len)] = in_ref[flip * block_len : (flip + 1) * block_len]
        taps = in_ref[2 * block_len :].astype(jnp.float32)
        first = jnp.where(core == 0, taps[:groups], taps[groups:])
        second = jnp.where(core == 0, taps[groups:], taps[:groups])
        filt_ref[chip ^ bits] = jnp.where(low, first, pltpu.roll(second, taps_here, 1))


def toeplitz_rows(filt_ref, toep_ref):
    chips, groups, _ = filt_ref.shape
    reach = toep_ref.shape[1]
    tiles = [filt_ref[tile] for tile in range(chips)]
    filt = jnp.concatenate(tiles + [jnp.zeros((groups, LANES), jnp.float32)], axis=1)
    for group in range(groups):
        rows = jnp.broadcast_to(filt[group : group + 1], (SLAB, reach))
        rows = pltpu.roll(rows, 0, 1, stride=1, stride_axis=0)
        toep_ref[group * SLAB : (group + 1) * SLAB] = rows.astype(jnp.bfloat16)


def group_of_lane(rows, width, groups):
    lane = lax.broadcasted_iota(jnp.int32, (rows, width), 1)
    return (lane % LANES) // (LANES // groups)


def filtered(dye_ref, start, toeplitz, groups):
    reach = toeplitz.shape[1]
    window = jnp.concatenate(
        [
            dye_ref[pl.ds(pl.multiple_of(start, SLAB), reach)],
            dye_ref[pl.ds(pl.multiple_of(start + SLAB, SLAB), reach)],
        ],
        axis=1,
    )
    full = jnp.dot(toeplitz, window, preferred_element_type=jnp.float32)
    group2 = group_of_lane(SLAB, 2 * LANES, groups)
    total = full[:SLAB]
    for group in range(1, groups):
        total = jnp.where(group2 == group, full[group * SLAB : (group + 1) * SLAB], total)
    return jnp.concatenate([total[:, :LANES], total[:, LANES:]], axis=0).astype(jnp.bfloat16)


def tokens_of(seq, dye_ref, toep_ref, out_ref, at, block_len):
    toeplitz = toep_ref[...]
    groups = toeplitz.shape[0] // SLAB
    for row in range(0, block_len, 2 * SLAB):
        out_ref[at + row : at + row + 2 * SLAB] = filtered(
            dye_ref, seq * block_len + row, toeplitz, groups
        )


def first_kernel(n_seq, taps_here, far, dy_ref, *refs):
    chips = n_seq // 2
    in_refs = refs[:chips]
    dye_ref, taps_ref, toep_ref, out_ref, x_ref, filt_ref, lag_ref = refs[chips:]
    tokens = dy_ref.shape[0]
    groups = EXTRA // 2
    taps = n_seq * taps_here
    reach = taps + LANES
    chip, core, _ = place()

    place_inputs(in_refs, taps_here, x_ref, filt_ref)
    dye_ref[:tokens] = dy_ref[...]
    dye_ref[tokens:] = dy_ref[:reach]

    rows = taps + STEP
    deep = DEPTH // LANES
    group_in = group_of_lane(STEP, DEPTH, groups)
    lag_ref[rows:] = jnp.zeros((reach - rows, groups * STEP), jnp.float32)
    for at in range(0, tokens, STEP * deep):
        starts = range(at, at + STEP * deep, STEP)
        windows = jnp.concatenate([dye_ref[row : row + rows] for row in starts], axis=1)
        inputs = jnp.concatenate([x_ref[row : row + STEP] for row in starts], axis=1)
        masked = jnp.concatenate(
            [jnp.where(group_in == group, inputs, jnp.zeros_like(inputs)) for group in range(groups)],
            axis=0,
        )
        part = lax.dot_general(
            windows, masked, (((1,), (1,)), ((), ())), preferred_element_type=jnp.float32
        )
        if at == 0:
            lag_ref[:rows] = part
        else:
            lag_ref[:rows] += part
        if at == 0:
            toeplitz_rows(filt_ref, toep_ref)

    lags = lag_ref[...].T
    eights = []
    for group in range(groups):
        at = group * STEP
        rows = lags[at : at + 8]
        for high in range(1, STEP // 8):
            rows = rows + roll_left(lags[at + 8 * high : at + 8 * high + 8], 8 * high)
        eights.append(rows)
    skew = jnp.concatenate(eights, axis=0)
    row_in = lax.broadcasted_iota(jnp.int32, skew.shape, 0) % 8
    for bit in (1, 2, 4):
        skew = jnp.where((row_in & bit) != 0, roll_left(skew, bit), skew)
    dh = skew.reshape(groups, 8, reach).sum(axis=1)[:, :taps]

    high = dh.astype(jnp.bfloat16).astype(jnp.float32)
    rest = dh - high
    low = lax.broadcasted_iota(jnp.int32, (groups, LANES), 1) < taps_here
    for to_chip in range(chips):
        columns = slice(to_chip * LANES, (to_chip + 1) * LANES)
        top, bottom = high[:, columns], rest[:, columns]
        even = jnp.where(low, top, pltpu.roll(bottom, taps_here, 1))
        odd = jnp.where(low, pltpu.roll(top, taps_here, 1), bottom)
        mine = jnp.where(core == 0, even, odd)
        other = jnp.where(core == 0, odd, even)
        taps_ref[to_chip] = jnp.concatenate([mine, other], axis=0).astype(jnp.bfloat16)

    block_len = (out_ref.shape[0] - EXTRA) // 2
    for flip in range(2):
        seq = 2 * (chip ^ far) + (core ^ flip)
        tokens_of(seq, dye_ref, toep_ref, out_ref, flip * block_len, block_len)
    out_ref[2 * block_len :] = taps_ref[chip ^ far]


def half_of(taps, flip):
    groups = EXTRA // 2
    return taps.astype(jnp.float32)[flip * groups : (flip + 1) * groups]


def stacked(rows):
    return jnp.concatenate(rows, axis=0).astype(jnp.bfloat16)


def near_kernel(masks, flip, dye_ref, toep_ref, taps_ref, out_ref):
    chip, core, _ = place()
    block_len = (out_ref.shape[0] - len(masks) * EXTRA // 2) // len(masks)
    for index, bits in enumerate(masks):
        seq = 2 * (chip ^ bits) + (core ^ flip)
        tokens_of(seq, dye_ref, toep_ref, out_ref, index * block_len, block_len)
    out_ref[len(masks) * block_len :] = stacked(
        [half_of(taps_ref[chip ^ bits], flip) for bits in masks]
    )


def near_pieces_kernel(keep_ref, got_ref, *out_refs):
    _, core, _ = place()
    count = len(out_refs)
    block_len = (out_refs[0].shape[0] - EXTRA) // 2
    groups = EXTRA // 2
    keep_taps = keep_ref[count * block_len :].astype(jnp.float32)
    got_taps = got_ref[count * block_len :].astype(jnp.float32)
    taps = [
        stacked(
            [value[index * groups : (index + 1) * groups] for value in (keep_taps, got_taps)]
        )
        for index in range(count)
    ]
    for index, out_ref in enumerate(out_refs):
        other = (index + 1) % count
        out_ref[:block_len] = keep_ref[rows_at((index + core) % count, block_len)]
        out_ref[block_len : 2 * block_len] = got_ref[rows_at((index + core) % count, block_len)]
        out_ref[2 * block_len :] = jnp.where(core == 0, taps[index], taps[other])


def own_kernel(dye_ref, toep_ref, taps_ref, out_ref):
    chip, core, _ = place()
    block_len = (out_ref.shape[0] - EXTRA) // 2
    for flip in range(2):
        seq = 2 * chip + (core ^ flip)
        tokens_of(seq, dye_ref, toep_ref, out_ref, flip * block_len, block_len)
    out_ref[2 * block_len :] = taps_ref[chip]


def swap_kernel(*refs):
    *in_refs, out_ref = refs
    block_len = (in_refs[0].shape[0] - EXTRA) // 2
    for index, in_ref in enumerate(in_refs):
        out_ref[index * block_len : (index + 1) * block_len] = in_ref[block_len : 2 * block_len]
    out_ref[len(in_refs) * block_len :] = stacked(
        [half_of(in_ref[2 * block_len :], 1) for in_ref in in_refs]
    )


def unpack_kernel(masks, *refs):
    own_ref, far_ref, swapped_ref, *near_refs, dx_ref, dh_ref, rows_ref = refs
    chip, core, _ = place()
    block_len = dx_ref.shape[0]
    taps_here, groups_here = dh_ref.shape
    groups = EXTRA // 2

    def put(from_chip, flip, tokens, taps):
        source = 2 * from_chip + (core ^ flip)
        dx_ref[:, pl.ds(pl.multiple_of(source * LANES, LANES), LANES)] = tokens
        rows_ref[pl.ds(pl.multiple_of(source * groups, groups), groups)] = taps + pltpu.roll(
            taps, taps_here, 1
        )

    swapped_taps = swapped_ref[2 * block_len :]
    for index, ref in enumerate((own_ref, far_ref)):
        put(chip ^ masks[index], 0, ref[:block_len], half_of(ref[2 * block_len :], 0))
        rows = swapped_ref[index * block_len : (index + 1) * block_len]
        put(chip ^ masks[index], 1, rows, half_of(swapped_taps, index))
    near = masks[2:]
    for index, ref in enumerate(near_refs):
        bits = jnp.where(core == 0, near[index], near[(index + 1) % len(near)])
        for flip in range(2):
            rows = ref[flip * block_len : (flip + 1) * block_len]
            put(chip ^ bits, flip, rows, half_of(ref[2 * block_len :], flip))
    dh_ref[...] = rows_ref[...].T[:taps_here]


def local_call(kernel, out_shape, operands, name, scratch=()):
    whole = pl.BlockSpec(memory_space=pltpu.VMEM)
    return pl.pallas_call(
        kernel,
        out_shape=out_shape,
        in_specs=[whole] * len(operands),
        out_specs=[whole] * len(out_shape),
        scratch_shapes=scratch,
        compiler_params=pltpu.CompilerParams(vmem_limit_bytes=VMEM_LIMIT),
        name=name,
    )(*operands)


def by_channels(n_seq, n_chan, out_grads, layer_inputs, filters):
    rows = out_grads.shape[0]
    block_len = layer_inputs.shape[0]
    taps_here, groups_here = filters.shape
    groups = groups_here // n_seq
    tokens = n_seq * block_len
    taps = n_seq * taps_here
    chips = n_seq // 2
    masks = partners(chips)

    def half(*shape):
        return jax.ShapeDtypeStruct(shape, jnp.bfloat16)

    unit = half(2 * block_len + EXTRA, LANES)
    x_other = xor_permute(layer_inputs, "seq", 1)
    f_other = xor_permute(filters, "seq", 1)
    (dy,) = local_call(
        functools.partial(fan_grads_kernel, n_seq),
        [half(n_seq * n_chan, rows, LANES)],
        (out_grads,),
        "fan_grads",
    )
    dy = lax.all_to_all(dy, ("seq", "chan"), split_axis=0, concat_axis=0, tiled=True)
    pieces = local_call(
        fan_inputs_kernel,
        [unit] * chips,
        (layer_inputs, x_other, filters, f_other),
        "fan_inputs",
        [pltpu.VMEM((2, groups_here, LANES), jnp.float32)],
    )
    dye, tap_parts, toeplitz, far = local_call(
        functools.partial(first_kernel, n_seq, taps_here, masks[1]),
        [
            half(tokens + taps + LANES, LANES),
            half(chips, EXTRA, LANES),
            half(groups * SLAB, taps + LANES),
            unit,
        ],
        (dy.reshape(tokens, LANES), *fan_out(pieces, "seq", 2)),
        "first",
        [
            pltpu.VMEM((tokens, LANES), jnp.bfloat16),
            pltpu.VMEM((chips, groups, LANES), jnp.float32),
            pltpu.VMEM((taps + LANES, groups * STEP), jnp.float32),
        ],
    )
    far = xor_permute(far, "seq", 2 * masks[1])
    near = masks[2:]
    near_shape = half(len(near) * (block_len + EXTRA // 2), LANES)
    (send,) = local_call(
        functools.partial(near_kernel, near, 1),
        [near_shape],
        (dye, toeplitz, tap_parts),
        "near_swap",
    )
    got = xor_permute(send, "seq", 1)
    (keep,) = local_call(
        functools.partial(near_kernel, near, 0),
        [near_shape],
        (dye, toeplitz, tap_parts),
        "near_keep",
    )
    pieces = local_call(near_pieces_kernel, [unit] * len(near), (keep, got), "near_pieces")
    pieces = [
        turned_permute(piece, "seq", [2 * bits for bits in near[index:] + near[:index]])
        for index, piece in enumerate(pieces)
    ]
    far, tap_parts = lax.optimization_barrier((far, tap_parts))
    (own,) = local_call(own_kernel, [unit], (dye, toeplitz, tap_parts), "own")
    (send,) = local_call(
        swap_kernel, [half(2 * block_len + EXTRA, LANES)], (own, far), "swap"
    )
    return local_call(
        functools.partial(unpack_kernel, masks),
        [
            half(block_len, n_seq * LANES),
            jax.ShapeDtypeStruct((taps_here, groups_here), jnp.float32),
        ],
        (own, far, xor_permute(send, "seq", 1), *pieces),
        "unpack",
        [pltpu.VMEM((groups_here, LANES), jnp.float32)],
    )


def solution(mesh):
    n_seq, n_chan = mesh.shape["seq"], mesh.shape["chan"]

    def on_device(out_grads, layer_inputs, filters):
        taps_here, groups_here = filters.shape
        fits = (
            n_seq == 8
            and n_chan in (2, 4, 8)
            and layer_inputs.shape[1] == n_seq * LANES
            and groups_here == 8 * n_seq
            and 2 * taps_here == LANES
            and out_grads.shape[0] % 16 == 0
            and layer_inputs.shape[0] % (2 * SLAB) == 0
            and n_seq * layer_inputs.shape[0] % (STEP * DEPTH // LANES) == 0
            and n_seq * taps_here + LANES <= n_seq * layer_inputs.shape[0]
        )
        if fits:
            return tuple(by_channels(n_seq, n_chan, out_grads, layer_inputs, filters))
        return by_tokens(out_grads, layer_inputs, filters)

    in_specs = (P(("seq", "chan"), None), P("seq", "chan"), P("seq", "chan"))
    out_specs = (P("seq", "chan"), P("seq", "chan"))
    return jax.shard_map(
        on_device, mesh=mesh, in_specs=in_specs, out_specs=out_specs, check_vma=False
    )
```

```python
import functools

import jax
import jax.numpy as jnp
from jax import lax
from jax.experimental import pallas as pl
from jax.experimental.pallas import tpu as pltpu
from jax.sharding import PartitionSpec as P

LANES = 128
STEP = 32
SLAB = 64
EXTRA = 16
DEPTH = 1024
VMEM_LIMIT = 40 * 1024 * 1024


def shifted(value, axis, steps):
    count = lax.axis_size(axis)
    pairs = [(source, (source + steps) % count) for source in range(count)]
    return lax.ppermute(value, axis, pairs)


def skewed_sums(products):
    groups_here, length, _ = products.shape
    padded = jnp.pad(products, ((0, 0), (0, 0), (0, length)))
    flat = padded.reshape(groups_here, 2 * length * length)[:, : length * (2 * length - 1)]
    return flat.reshape(groups_here, length, 2 * length - 1).sum(axis=1)


def by_tokens(out_grads, layer_inputs, filters):
    local_grads = lax.all_to_all(out_grads, "chan", split_axis=1, concat_axis=0, tiled=True)
    taps_all = lax.all_gather(filters, "seq", axis=0, tiled=True)
    block_len = local_grads.shape[0]
    chan_width = local_grads.shape[1]
    groups_here = filters.shape[1]
    per_group = chan_width // groups_here
    taps_total = taps_all.shape[0]
    spread_blocks = taps_total // block_len
    filt_rows = taps_all.T
    x_reversed = layer_inputs[::-1].reshape(block_len, groups_here, per_group).transpose(1, 2, 0)
    offsets = lax.broadcasted_iota(jnp.int32, (block_len, block_len), 1) - lax.broadcasted_iota(
        jnp.int32, (block_len, block_len), 0
    )
    dx_total = jnp.zeros((groups_here, per_group, block_len), jnp.float32)
    lag_buffer = jnp.zeros((groups_here, (spread_blocks + 2) * block_len), jnp.float32)
    current = local_grads
    for lag_block in range(spread_blocks + 1):
        if lag_block > 0:
            current = shifted(local_grads, "seq", -lag_block)
        dy_grouped = current.reshape(block_len, groups_here, per_group).transpose(1, 2, 0)
        lag_index = lag_block * block_len + offsets
        inside = (lag_index >= 0) & (lag_index < taps_total)
        picked = jnp.take(filt_rows, jnp.clip(lag_index, 0, taps_total - 1), axis=1)
        toeplitz = jnp.where(inside[None], picked, jnp.zeros((), jnp.bfloat16))
        dx_total = dx_total + jnp.einsum(
            "guv,gkv->gku", toeplitz, dy_grouped, preferred_element_type=jnp.float32
        )
        products = jnp.einsum(
            "gku,gkv->guv", x_reversed, dy_grouped, preferred_element_type=jnp.float32
        )
        start = lag_block * block_len
        lag_buffer = lag_buffer.at[:, start : start + 2 * block_len - 1].add(skewed_sums(products))
    partial_dh = lag_buffer[:, block_len - 1 : block_len - 1 + taps_total].T
    filter_grads = lax.psum_scatter(partial_dh, "seq", scatter_dimension=0, tiled=True)
    input_grads = dx_total.transpose(2, 0, 1).reshape(block_len, chan_width).astype(jnp.bfloat16)
    return (input_grads, filter_grads)


def xor_permute(value, axis, bits):
    pairs = [(source, source ^ bits) for source in range(lax.axis_size(axis))]
    return lax.ppermute(value, axis, pairs)


def turned_permute(value, axis, masks):
    pairs = [(source, source ^ masks[source % 2]) for source in range(lax.axis_size(axis))]
    return lax.ppermute(value, axis, pairs)


def partners(count):
    return [(count - step) % count for step in range(count)]


def fan_out(pieces, axis, unit):
    masks = partners(len(pieces))[1:]
    return [pieces[0]] + [xor_permute(p, axis, m * unit) for p, m in zip(pieces[1:], masks)]


def roll_left(value, steps):
    width = value.shape[-1]
    return pltpu.roll(value, (width - steps) % width, value.ndim - 1)


def place():
    seq = lax.axis_index("seq")
    return seq // 2, seq % 2, lax.axis_index("chan")


def rows_at(index, size):
    return pl.ds(pl.multiple_of(index * size, 16), size)


def fan_grads_kernel(n_seq, in_ref, out_ref):
    n_chan = out_ref.shape[0] // n_seq
    for seq in range(n_seq):
        for chan in range(n_chan):
            start = (chan * n_seq + seq) * LANES
            out_ref[seq * n_chan + chan] = in_ref[:, start : start + LANES]


def fan_inputs_kernel(x_own_ref, x_other_ref, f_own_ref, f_other_ref, *refs):
    *out_refs, taps_ref = refs
    chip, core, _ = place()
    block_len = x_own_ref.shape[0]
    taps_here, groups_here = f_own_ref.shape
    groups = groups_here // (2 * len(out_refs))
    rest = jnp.zeros((groups_here, LANES - taps_here), jnp.float32)
    for flip, f_ref in enumerate((f_own_ref, f_other_ref)):
        taps_ref[flip] = jnp.concatenate([f_ref[...].astype(jnp.float32).T, rest], axis=1)
    for bits, out_ref in zip(partners(len(out_refs)), out_refs):
        target = 2 * (chip ^ bits) + core
        columns = pl.ds(pl.multiple_of(target * LANES, LANES), LANES)
        out_ref[:block_len] = x_own_ref[:, columns]
        out_ref[block_len : 2 * block_len] = x_other_ref[:, columns]
        rows = pl.ds(pl.multiple_of(target * groups, groups), groups)
        taps = jnp.concatenate([taps_ref[0, rows], taps_ref[1, rows]], axis=0)
        out_ref[2 * block_len :] = taps.astype(jnp.bfloat16)


def place_inputs(in_refs, taps_here, x_ref, filt_ref):
    block_len = (in_refs[0].shape[0] - EXTRA) // 2
    groups = EXTRA // 2
    chip, core, _ = place()
    low = lax.broadcasted_iota(jnp.int32, (groups, LANES), 1) < taps_here
    for bits, in_ref in zip(partners(len(in_refs)), in_refs):
        for flip in range(2):
            block = 2 * (chip ^ bits) + (core ^ flip)
            x_ref[rows_at(block, block_len)] = in_ref[flip * block_len : (flip + 1) * block_len]
        taps = in_ref[2 * block_len :].astype(jnp.float32)
        first = jnp.where(core == 0, taps[:groups], taps[groups:])
        second = jnp.where(core == 0, taps[groups:], taps[:groups])
        filt_ref[chip ^ bits] = jnp.where(low, first, pltpu.roll(second, taps_here, 1))


def toeplitz_rows(filt_ref, toep_ref, rest_ref):
    chips, groups, _ = filt_ref.shape
    taps = chips * LANES
    tiles = [filt_ref[tile] for tile in range(chips)]
    filt = jnp.concatenate(tiles + [jnp.zeros((groups, LANES), jnp.float32)], axis=1)
    low = lax.broadcasted_iota(jnp.int32, (SLAB, LANES), 1) < SLAB
    outside = []
    for group in range(groups):
        rows = jnp.broadcast_to(filt[group : group + 1], (SLAB, taps + LANES))
        rows = pltpu.roll(rows, 0, 1, stride=1, stride_axis=0)
        toep_ref[group * SLAB : (group + 1) * SLAB] = rows[:, :taps].astype(jnp.bfloat16)
        outside.append(rows[:, taps:])
    for pair in range(groups // 2):
        both = jnp.where(low, outside[2 * pair], pltpu.roll(outside[2 * pair + 1], SLAB, 1))
        rest_ref[:, pair * LANES : (pair + 1) * LANES] = both.astype(jnp.bfloat16)


def group_of_lane(rows, width, groups):
    lane = lax.broadcasted_iota(jnp.int32, (rows, width), 1)
    return (lane % LANES) // (LANES // groups)


def filtered(dye_ref, start, toep_ref, rest_ref):
    groups = toep_ref.shape[0] // SLAB
    taps = toep_ref.shape[1]

    def window(at, size):
        return jnp.concatenate(
            [
                dye_ref[pl.ds(pl.multiple_of(start + at, SLAB), size)],
                dye_ref[pl.ds(pl.multiple_of(start + at + SLAB, SLAB), size)],
            ],
            axis=1,
        )

    group2 = group_of_lane(SLAB, 2 * LANES, groups)
    after = window(taps, SLAB)
    after = [jnp.where(group2 == group, after, jnp.zeros_like(after)) for group in range(groups)]
    full = jnp.dot(toep_ref[...], window(0, taps), preferred_element_type=jnp.float32)
    rest = jnp.dot(
        rest_ref[...], jnp.concatenate(after, axis=0), preferred_element_type=jnp.float32
    )
    total = full[:SLAB]
    for group in range(1, groups):
        total = jnp.where(group2 == group, full[group * SLAB : (group + 1) * SLAB], total)
    total = total + rest
    return jnp.concatenate([total[:, :LANES], total[:, LANES:]], axis=0).astype(jnp.bfloat16)


def tokens_of(seq, dye_ref, toep_ref, rest_ref, out_ref, at, block_len):
    for row in range(0, block_len, 2 * SLAB):
        out_ref[at + row : at + row + 2 * SLAB] = filtered(
            dye_ref, seq * block_len + row, toep_ref, rest_ref
        )


def first_kernel(n_seq, taps_here, far, dy_ref, *refs):
    chips = n_seq // 2
    in_refs = refs[:chips]
    dye_ref, taps_ref, toep_ref, rest_ref, far_ref, x_ref, filt_ref, lag_ref = refs[chips:]
    tokens = dy_ref.shape[0]
    groups = EXTRA // 2
    taps = n_seq * taps_here
    reach = taps + LANES
    chip, core, _ = place()

    place_inputs(in_refs, taps_here, x_ref, filt_ref)
    dye_ref[:tokens] = dy_ref[...]
    dye_ref[tokens:] = dy_ref[:reach]

    rows = taps + STEP
    deep = DEPTH // LANES
    group_in = group_of_lane(STEP, DEPTH, groups)
    lag_ref[rows:] = jnp.zeros((reach - rows, groups * STEP), jnp.float32)
    for at in range(0, tokens, STEP * deep):
        starts = range(at, at + STEP * deep, STEP)
        windows = jnp.concatenate([dye_ref[row : row + rows] for row in starts], axis=1)
        inputs = jnp.concatenate([x_ref[row : row + STEP] for row in starts], axis=1)
        masked = jnp.concatenate(
            [jnp.where(group_in == group, inputs, jnp.zeros_like(inputs)) for group in range(groups)],
            axis=0,
        )
        part = lax.dot_general(
            windows, masked, (((1,), (1,)), ((), ())), preferred_element_type=jnp.float32
        )
        if at == 0:
            lag_ref[:rows] = part
        else:
            lag_ref[:rows] += part
        if at == 0:
            toeplitz_rows(filt_ref, toep_ref, rest_ref)

    block_len = tokens // n_seq
    blocks = [(2 * (chip ^ far) + (core ^ flip), flip * block_len) for flip in range(2)]
    lags = lag_ref[...].T
    eights = []
    for group in range(groups):
        if group % 2 == 0 and blocks:
            seq, at = blocks.pop(0)
            tokens_of(seq, dye_ref, toep_ref, rest_ref, far_ref, at, block_len)
        at = group * STEP
        rows = lags[at : at + 8]
        for high in range(1, STEP // 8):
            rows = rows + roll_left(lags[at + 8 * high : at + 8 * high + 8], 8 * high)
        eights.append(rows)
    skew = jnp.concatenate(eights, axis=0)
    row_in = lax.broadcasted_iota(jnp.int32, skew.shape, 0) % 8
    for bit in (1, 2, 4):
        skew = jnp.where((row_in & bit) != 0, roll_left(skew, bit), skew)
    dh = skew.reshape(groups, 8, reach).sum(axis=1)[:, :taps]

    high = dh.astype(jnp.bfloat16).astype(jnp.float32)
    rest = dh - high
    low = lax.broadcasted_iota(jnp.int32, (groups, LANES), 1) < taps_here
    for to_chip in range(chips):
        columns = slice(to_chip * LANES, (to_chip + 1) * LANES)
        top, bottom = high[:, columns], rest[:, columns]
        even = jnp.where(low, top, pltpu.roll(bottom, taps_here, 1))
        odd = jnp.where(low, pltpu.roll(top, taps_here, 1), bottom)
        mine = jnp.where(core == 0, even, odd)
        other = jnp.where(core == 0, odd, even)
        taps_ref[to_chip] = jnp.concatenate([mine, other], axis=0).astype(jnp.bfloat16)

    far_ref[2 * block_len :] = taps_ref[chip ^ far]


def half_of(taps, flip):
    groups = EXTRA // 2
    return taps.astype(jnp.float32)[flip * groups : (flip + 1) * groups]


def stacked(rows):
    return jnp.concatenate(rows, axis=0).astype(jnp.bfloat16)


def near_kernel(masks, flip, dye_ref, toep_ref, rest_ref, taps_ref, out_ref):
    chip, core, _ = place()
    block_len = (out_ref.shape[0] - len(masks) * EXTRA // 2) // len(masks)
    for index, bits in enumerate(masks):
        seq = 2 * (chip ^ bits) + (core ^ flip)
        tokens_of(seq, dye_ref, toep_ref, rest_ref, out_ref, index * block_len, block_len)
    out_ref[len(masks) * block_len :] = stacked(
        [half_of(taps_ref[chip ^ bits], flip) for bits in masks]
    )


def near_pieces_kernel(keep_ref, got_ref, *out_refs):
    _, core, _ = place()
    count = len(out_refs)
    block_len = (out_refs[0].shape[0] - EXTRA) // 2
    groups = EXTRA // 2
    keep_taps = keep_ref[count * block_len :].astype(jnp.float32)
    got_taps = got_ref[count * block_len :].astype(jnp.float32)
    taps = [
        stacked(
            [value[index * groups : (index + 1) * groups] for value in (keep_taps, got_taps)]
        )
        for index in range(count)
    ]
    for index, out_ref in enumerate(out_refs):
        other = (index + 1) % count
        out_ref[:block_len] = keep_ref[rows_at((index + core) % count, block_len)]
        out_ref[block_len : 2 * block_len] = got_ref[rows_at((index + core) % count, block_len)]
        out_ref[2 * block_len :] = jnp.where(core == 0, taps[index], taps[other])


def own_kernel(dye_ref, toep_ref, rest_ref, taps_ref, out_ref):
    chip, core, _ = place()
    block_len = (out_ref.shape[0] - EXTRA) // 2
    for flip in range(2):
        seq = 2 * chip + (core ^ flip)
        tokens_of(seq, dye_ref, toep_ref, rest_ref, out_ref, flip * block_len, block_len)
    out_ref[2 * block_len :] = taps_ref[chip]


def swap_kernel(*refs):
    *in_refs, out_ref = refs
    block_len = (in_refs[0].shape[0] - EXTRA) // 2
    for index, in_ref in enumerate(in_refs):
        out_ref[index * block_len : (index + 1) * block_len] = in_ref[block_len : 2 * block_len]
    out_ref[len(in_refs) * block_len :] = stacked(
        [half_of(in_ref[2 * block_len :], 1) for in_ref in in_refs]
    )


def unpack_kernel(masks, *refs):
    own_ref, far_ref, swapped_ref, *near_refs, dx_ref, dh_ref, rows_ref = refs
    chip, core, _ = place()
    block_len = dx_ref.shape[0]
    taps_here, groups_here = dh_ref.shape
    groups = EXTRA // 2

    def put(from_chip, flip, tokens, taps):
        source = 2 * from_chip + (core ^ flip)
        dx_ref[:, pl.ds(pl.multiple_of(source * LANES, LANES), LANES)] = tokens
        rows_ref[pl.ds(pl.multiple_of(source * groups, groups), groups)] = taps + pltpu.roll(
            taps, taps_here, 1
        )

    swapped_taps = swapped_ref[2 * block_len :]
    for index, ref in enumerate((own_ref, far_ref)):
        put(chip ^ masks[index], 0, ref[:block_len], half_of(ref[2 * block_len :], 0))
        rows = swapped_ref[index * block_len : (index + 1) * block_len]
        put(chip ^ masks[index], 1, rows, half_of(swapped_taps, index))
    near = masks[2:]
    for index, ref in enumerate(near_refs):
        bits = jnp.where(core == 0, near[index], near[(index + 1) % len(near)])
        for flip in range(2):
            rows = ref[flip * block_len : (flip + 1) * block_len]
            put(chip ^ bits, flip, rows, half_of(ref[2 * block_len :], flip))
    dh_ref[...] = rows_ref[...].T[:taps_here]


def local_call(kernel, out_shape, operands, name, scratch=()):
    whole = pl.BlockSpec(memory_space=pltpu.VMEM)
    return pl.pallas_call(
        kernel,
        out_shape=out_shape,
        in_specs=[whole] * len(operands),
        out_specs=[whole] * len(out_shape),
        scratch_shapes=scratch,
        compiler_params=pltpu.CompilerParams(vmem_limit_bytes=VMEM_LIMIT),
        name=name,
    )(*operands)


def by_channels(n_seq, n_chan, out_grads, layer_inputs, filters):
    rows = out_grads.shape[0]
    block_len = layer_inputs.shape[0]
    taps_here, groups_here = filters.shape
    groups = groups_here // n_seq
    tokens = n_seq * block_len
    taps = n_seq * taps_here
    chips = n_seq // 2
    masks = partners(chips)

    def half(*shape):
        return jax.ShapeDtypeStruct(shape, jnp.bfloat16)

    unit = half(2 * block_len + EXTRA, LANES)
    x_other = xor_permute(layer_inputs, "seq", 1)
    f_other = xor_permute(filters, "seq", 1)
    (dy,) = local_call(
        functools.partial(fan_grads_kernel, n_seq),
        [half(n_seq * n_chan, rows, LANES)],
        (out_grads,),
        "fan_grads",
    )
    dy = lax.all_to_all(dy, ("seq", "chan"), split_axis=0, concat_axis=0, tiled=True)
    pieces = local_call(
        fan_inputs_kernel,
        [unit] * chips,
        (layer_inputs, x_other, filters, f_other),
        "fan_inputs",
        [pltpu.VMEM((2, groups_here, LANES), jnp.float32)],
    )
    near = masks[2:]
    near_shape = half(len(near) * (block_len + EXTRA // 2), LANES)
    dye, tap_parts, toeplitz, outside, far = local_call(
        functools.partial(first_kernel, n_seq, taps_here, masks[1]),
        [
            half(tokens + taps + LANES, LANES),
            half(chips, EXTRA, LANES),
            half(groups * SLAB, taps),
            half(SLAB, groups * SLAB),
            unit,
        ],
        (dy.reshape(tokens, LANES), *fan_out(pieces, "seq", 2)),
        "first",
        [
            pltpu.VMEM((tokens, LANES), jnp.bfloat16),
            pltpu.VMEM((chips, groups, LANES), jnp.float32),
            pltpu.VMEM((taps + LANES, groups * STEP), jnp.float32),
        ],
    )
    far = xor_permute(far, "seq", 2 * masks[1])
    (send,) = local_call(
        functools.partial(near_kernel, near, 1),
        [near_shape],
        (dye, toeplitz, outside, tap_parts),
        "near_swap",
    )
    got = xor_permute(send, "seq", 1)
    (keep,) = local_call(
        functools.partial(near_kernel, near, 0),
        [near_shape],
        (dye, toeplitz, outside, tap_parts),
        "near_keep",
    )
    pieces = local_call(near_pieces_kernel, [unit] * len(near), (keep, got), "near_pieces")
    pieces = [
        turned_permute(piece, "seq", [2 * bits for bits in near[index:] + near[:index]])
        for index, piece in enumerate(pieces)
    ]
    far, tap_parts = lax.optimization_barrier((far, tap_parts))
    (own,) = local_call(own_kernel, [unit], (dye, toeplitz, outside, tap_parts), "own")
    (send,) = local_call(
        swap_kernel, [half(2 * block_len + EXTRA, LANES)], (own, far), "swap"
    )
    return local_call(
        functools.partial(unpack_kernel, masks),
        [
            half(block_len, n_seq * LANES),
            jax.ShapeDtypeStruct((taps_here, groups_here), jnp.float32),
        ],
        (own, far, xor_permute(send, "seq", 1), *pieces),
        "unpack",
        [pltpu.VMEM((groups_here, LANES), jnp.float32)],
    )


def solution(mesh):
    n_seq, n_chan = mesh.shape["seq"], mesh.shape["chan"]

    def on_device(out_grads, layer_inputs, filters):
        taps_here, groups_here = filters.shape
        fits = (
            n_seq == 8
            and n_chan in (2, 4, 8)
            and layer_inputs.shape[1] == n_seq * LANES
            and groups_here == 8 * n_seq
            and 2 * taps_here == LANES
            and out_grads.shape[0] % 16 == 0
            and layer_inputs.shape[0] % (2 * SLAB) == 0
            and n_seq * layer_inputs.shape[0] % (STEP * DEPTH // LANES) == 0
            and n_seq * taps_here + LANES <= n_seq * layer_inputs.shape[0]
        )
        if fits:
            return tuple(by_channels(n_seq, n_chan, out_grads, layer_inputs, filters))
        return by_tokens(out_grads, layer_inputs, filters)

    in_specs = (P(("seq", "chan"), None), P("seq", "chan"), P("seq", "chan"))
    out_specs = (P("seq", "chan"), P("seq", "chan"))
    return jax.shard_map(
        on_device, mesh=mesh, in_specs=in_specs, out_specs=out_specs, check_vma=False
    )
```

```python
import functools

import jax
import jax.numpy as jnp
from jax import lax
from jax.experimental import pallas as pl
from jax.experimental.pallas import tpu as pltpu
from jax.sharding import PartitionSpec as P

LANES = 128
STEP = 32
SLAB = 64
EXTRA = 16
DEPTH = 1024
VMEM_LIMIT = 40 * 1024 * 1024


def shifted(value, axis, steps):
    count = lax.axis_size(axis)
    pairs = [(source, (source + steps) % count) for source in range(count)]
    return lax.ppermute(value, axis, pairs)


def skewed_sums(products):
    groups_here, length, _ = products.shape
    padded = jnp.pad(products, ((0, 0), (0, 0), (0, length)))
    flat = padded.reshape(groups_here, 2 * length * length)[:, : length * (2 * length - 1)]
    return flat.reshape(groups_here, length, 2 * length - 1).sum(axis=1)


def by_tokens(out_grads, layer_inputs, filters):
    local_grads = lax.all_to_all(out_grads, "chan", split_axis=1, concat_axis=0, tiled=True)
    taps_all = lax.all_gather(filters, "seq", axis=0, tiled=True)
    block_len = local_grads.shape[0]
    chan_width = local_grads.shape[1]
    groups_here = filters.shape[1]
    per_group = chan_width // groups_here
    taps_total = taps_all.shape[0]
    spread_blocks = taps_total // block_len
    filt_rows = taps_all.T
    x_reversed = layer_inputs[::-1].reshape(block_len, groups_here, per_group).transpose(1, 2, 0)
    offsets = lax.broadcasted_iota(jnp.int32, (block_len, block_len), 1) - lax.broadcasted_iota(
        jnp.int32, (block_len, block_len), 0
    )
    dx_total = jnp.zeros((groups_here, per_group, block_len), jnp.float32)
    lag_buffer = jnp.zeros((groups_here, (spread_blocks + 2) * block_len), jnp.float32)
    current = local_grads
    for lag_block in range(spread_blocks + 1):
        if lag_block > 0:
            current = shifted(local_grads, "seq", -lag_block)
        dy_grouped = current.reshape(block_len, groups_here, per_group).transpose(1, 2, 0)
        lag_index = lag_block * block_len + offsets
        inside = (lag_index >= 0) & (lag_index < taps_total)
        picked = jnp.take(filt_rows, jnp.clip(lag_index, 0, taps_total - 1), axis=1)
        toeplitz = jnp.where(inside[None], picked, jnp.zeros((), jnp.bfloat16))
        dx_total = dx_total + jnp.einsum(
            "guv,gkv->gku", toeplitz, dy_grouped, preferred_element_type=jnp.float32
        )
        products = jnp.einsum(
            "gku,gkv->guv", x_reversed, dy_grouped, preferred_element_type=jnp.float32
        )
        start = lag_block * block_len
        lag_buffer = lag_buffer.at[:, start : start + 2 * block_len - 1].add(skewed_sums(products))
    partial_dh = lag_buffer[:, block_len - 1 : block_len - 1 + taps_total].T
    filter_grads = lax.psum_scatter(partial_dh, "seq", scatter_dimension=0, tiled=True)
    input_grads = dx_total.transpose(2, 0, 1).reshape(block_len, chan_width).astype(jnp.bfloat16)
    return (input_grads, filter_grads)


def xor_permute(value, axis, bits):
    pairs = [(source, source ^ bits) for source in range(lax.axis_size(axis))]
    return lax.ppermute(value, axis, pairs)


def turned_permute(value, axis, masks):
    pairs = [(source, source ^ masks[source % 2]) for source in range(lax.axis_size(axis))]
    return lax.ppermute(value, axis, pairs)


def partners(count):
    return [(count - step) % count for step in range(count)]


def fan_out(pieces, axis, unit):
    masks = partners(len(pieces))[1:]
    return [pieces[0]] + [xor_permute(p, axis, m * unit) for p, m in zip(pieces[1:], masks)]


def roll_left(value, steps):
    width = value.shape[-1]
    return pltpu.roll(value, (width - steps) % width, value.ndim - 1)


def place():
    seq = lax.axis_index("seq")
    return seq // 2, seq % 2, lax.axis_index("chan")


def rows_at(index, size):
    return pl.ds(pl.multiple_of(index * size, 16), size)


def fan_grads_kernel(n_seq, in_ref, out_ref):
    n_chan = out_ref.shape[0] // n_seq
    for seq in range(n_seq):
        for chan in range(n_chan):
            start = (chan * n_seq + seq) * LANES
            out_ref[seq * n_chan + chan] = in_ref[:, start : start + LANES]


def fan_inputs_kernel(x_own_ref, x_other_ref, f_own_ref, f_other_ref, *refs):
    *out_refs, taps_ref = refs
    chip, core, _ = place()
    block_len = x_own_ref.shape[0]
    taps_here, groups_here = f_own_ref.shape
    groups = groups_here // (2 * len(out_refs))
    rest = jnp.zeros((groups_here, LANES - taps_here), jnp.float32)
    for flip, f_ref in enumerate((f_own_ref, f_other_ref)):
        taps_ref[flip] = jnp.concatenate([f_ref[...].astype(jnp.float32).T, rest], axis=1)
    for bits, out_ref in zip(partners(len(out_refs)), out_refs):
        target = 2 * (chip ^ bits) + core
        columns = pl.ds(pl.multiple_of(target * LANES, LANES), LANES)
        out_ref[:block_len] = x_own_ref[:, columns]
        out_ref[block_len : 2 * block_len] = x_other_ref[:, columns]
        rows = pl.ds(pl.multiple_of(target * groups, groups), groups)
        taps = jnp.concatenate([taps_ref[0, rows], taps_ref[1, rows]], axis=0)
        out_ref[2 * block_len :] = taps.astype(jnp.bfloat16)


def place_inputs(in_refs, taps_here, x_ref, filt_ref):
    block_len = (in_refs[0].shape[0] - EXTRA) // 2
    groups = EXTRA // 2
    chip, core, _ = place()
    low = lax.broadcasted_iota(jnp.int32, (groups, LANES), 1) < taps_here
    for bits, in_ref in zip(partners(len(in_refs)), in_refs):
        for flip in range(2):
            block = 2 * (chip ^ bits) + (core ^ flip)
            x_ref[rows_at(block, block_len)] = in_ref[flip * block_len : (flip + 1) * block_len]
        taps = in_ref[2 * block_len :].astype(jnp.float32)
        first = jnp.where(core == 0, taps[:groups], taps[groups:])
        second = jnp.where(core == 0, taps[groups:], taps[:groups])
        filt_ref[chip ^ bits] = jnp.where(low, first, pltpu.roll(second, taps_here, 1))


def toeplitz_rows(filt_ref, toep_ref, rest_ref):
    chips, groups, _ = filt_ref.shape
    taps = chips * LANES
    tiles = [filt_ref[tile] for tile in range(chips)]
    filt = jnp.concatenate(tiles + [jnp.zeros((groups, LANES), jnp.float32)], axis=1)
    low = lax.broadcasted_iota(jnp.int32, (SLAB, LANES), 1) < SLAB
    outside = []
    for group in range(groups):
        rows = jnp.broadcast_to(filt[group : group + 1], (SLAB, taps + LANES))
        rows = pltpu.roll(rows, 0, 1, stride=1, stride_axis=0)
        toep_ref[group * SLAB : (group + 1) * SLAB] = rows[:, :taps].astype(jnp.bfloat16)
        outside.append(rows[:, taps:])
    for pair in range(groups // 2):
        both = jnp.where(low, outside[2 * pair], pltpu.roll(outside[2 * pair + 1], SLAB, 1))
        rest_ref[:, pair * LANES : (pair + 1) * LANES] = both.astype(jnp.bfloat16)


def group_of_lane(rows, width, groups):
    lane = lax.broadcasted_iota(jnp.int32, (rows, width), 1)
    return (lane % LANES) // (LANES // groups)


def tokens_of(seqs, dye_ref, toep_ref, rest_ref, out_ref, block_len):
    groups = toep_ref.shape[0] // SLAB
    taps = toep_ref.shape[1]
    starts = [seq * block_len + row for seq in seqs for row in range(0, block_len, SLAB)]

    def windows(at, size):
        return jnp.concatenate(
            [dye_ref[pl.ds(pl.multiple_of(start + at, SLAB), size)] for start in starts], axis=1
        )

    group_in = group_of_lane(SLAB, len(starts) * LANES, groups)
    after = windows(taps, SLAB)
    after = [jnp.where(group_in == group, after, jnp.zeros_like(after)) for group in range(groups)]
    full = jnp.dot(toep_ref[...], windows(0, taps), preferred_element_type=jnp.float32)
    rest = jnp.dot(
        rest_ref[...], jnp.concatenate(after, axis=0), preferred_element_type=jnp.float32
    )
    total = full[:SLAB]
    for group in range(1, groups):
        total = jnp.where(group_in == group, full[group * SLAB : (group + 1) * SLAB], total)
    total = (total + rest).astype(jnp.bfloat16)
    for index in range(len(starts)):
        columns = slice(index * LANES, (index + 1) * LANES)
        out_ref[index * SLAB : (index + 1) * SLAB] = total[:, columns]


def first_kernel(n_seq, taps_here, far, dy_ref, *refs):
    chips = n_seq // 2
    in_refs = refs[:chips]
    dye_ref, taps_ref, toep_ref, rest_ref, far_ref, x_ref, filt_ref, lag_ref = refs[chips:]
    tokens = dy_ref.shape[0]
    groups = EXTRA // 2
    taps = n_seq * taps_here
    reach = taps + LANES
    chip, core, _ = place()

    place_inputs(in_refs, taps_here, x_ref, filt_ref)
    dye_ref[:tokens] = dy_ref[...]
    dye_ref[tokens:] = dy_ref[:reach]

    rows = taps + STEP
    deep = DEPTH // LANES
    group_in = group_of_lane(STEP, DEPTH, groups)
    lag_ref[rows:] = jnp.zeros((reach - rows, groups * STEP), jnp.float32)
    for at in range(0, tokens, STEP * deep):
        starts = range(at, at + STEP * deep, STEP)
        windows = jnp.concatenate([dye_ref[row : row + rows] for row in starts], axis=1)
        inputs = jnp.concatenate([x_ref[row : row + STEP] for row in starts], axis=1)
        masked = jnp.concatenate(
            [jnp.where(group_in == group, inputs, jnp.zeros_like(inputs)) for group in range(groups)],
            axis=0,
        )
        part = lax.dot_general(
            windows, masked, (((1,), (1,)), ((), ())), preferred_element_type=jnp.float32
        )
        if at == 0:
            lag_ref[:rows] = part
        else:
            lag_ref[:rows] += part
        if at == 0:
            toeplitz_rows(filt_ref, toep_ref, rest_ref)

    block_len = tokens // n_seq
    seqs = [2 * (chip ^ far) + (core ^ flip) for flip in range(2)]
    tokens_of(seqs, dye_ref, toep_ref, rest_ref, far_ref, block_len)
    lags = lag_ref[...].T
    eights = []
    for group in range(groups):
        at = group * STEP
        rows = lags[at : at + 8]
        for high in range(1, STEP // 8):
            rows = rows + roll_left(lags[at + 8 * high : at + 8 * high + 8], 8 * high)
        eights.append(rows)
    skew = jnp.concatenate(eights, axis=0)
    row_in = lax.broadcasted_iota(jnp.int32, skew.shape, 0) % 8
    for bit in (1, 2, 4):
        skew = jnp.where((row_in & bit) != 0, roll_left(skew, bit), skew)
    dh = skew.reshape(groups, 8, reach).sum(axis=1)[:, :taps]

    high = dh.astype(jnp.bfloat16).astype(jnp.float32)
    rest = dh - high
    low = lax.broadcasted_iota(jnp.int32, (groups, LANES), 1) < taps_here
    for to_chip in range(chips):
        columns = slice(to_chip * LANES, (to_chip + 1) * LANES)
        top, bottom = high[:, columns], rest[:, columns]
        even = jnp.where(low, top, pltpu.roll(bottom, taps_here, 1))
        odd = jnp.where(low, pltpu.roll(top, taps_here, 1), bottom)
        mine = jnp.where(core == 0, even, odd)
        other = jnp.where(core == 0, odd, even)
        taps_ref[to_chip] = jnp.concatenate([mine, other], axis=0).astype(jnp.bfloat16)

    far_ref[2 * block_len :] = taps_ref[chip ^ far]


def half_of(taps, flip):
    groups = EXTRA // 2
    return taps.astype(jnp.float32)[flip * groups : (flip + 1) * groups]


def stacked(rows):
    return jnp.concatenate(rows, axis=0).astype(jnp.bfloat16)


def near_kernel(masks, flip, dye_ref, toep_ref, rest_ref, taps_ref, out_ref):
    chip, core, _ = place()
    block_len = (out_ref.shape[0] - len(masks) * EXTRA // 2) // len(masks)
    seqs = [2 * (chip ^ bits) + (core ^ flip) for bits in masks]
    tokens_of(seqs, dye_ref, toep_ref, rest_ref, out_ref, block_len)
    out_ref[len(masks) * block_len :] = stacked(
        [half_of(taps_ref[chip ^ bits], flip) for bits in masks]
    )


def near_pieces_kernel(keep_ref, got_ref, *out_refs):
    _, core, _ = place()
    count = len(out_refs)
    block_len = (out_refs[0].shape[0] - EXTRA) // 2
    groups = EXTRA // 2
    keep_taps = keep_ref[count * block_len :].astype(jnp.float32)
    got_taps = got_ref[count * block_len :].astype(jnp.float32)
    taps = [
        stacked(
            [value[index * groups : (index + 1) * groups] for value in (keep_taps, got_taps)]
        )
        for index in range(count)
    ]
    for index, out_ref in enumerate(out_refs):
        other = (index + 1) % count
        out_ref[:block_len] = keep_ref[rows_at((index + core) % count, block_len)]
        out_ref[block_len : 2 * block_len] = got_ref[rows_at((index + core) % count, block_len)]
        out_ref[2 * block_len :] = jnp.where(core == 0, taps[index], taps[other])


def own_kernel(dye_ref, toep_ref, rest_ref, taps_ref, out_ref):
    chip, core, _ = place()
    block_len = (out_ref.shape[0] - EXTRA) // 2
    seqs = [2 * chip + (core ^ flip) for flip in range(2)]
    tokens_of(seqs, dye_ref, toep_ref, rest_ref, out_ref, block_len)
    out_ref[2 * block_len :] = taps_ref[chip]


def swap_kernel(*refs):
    *in_refs, out_ref = refs
    block_len = (in_refs[0].shape[0] - EXTRA) // 2
    for index, in_ref in enumerate(in_refs):
        out_ref[index * block_len : (index + 1) * block_len] = in_ref[block_len : 2 * block_len]
    out_ref[len(in_refs) * block_len :] = stacked(
        [half_of(in_ref[2 * block_len :], 1) for in_ref in in_refs]
    )


def unpack_kernel(masks, *refs):
    own_ref, far_ref, swapped_ref, *near_refs, dx_ref, dh_ref, rows_ref = refs
    chip, core, _ = place()
    block_len = dx_ref.shape[0]
    taps_here, groups_here = dh_ref.shape
    groups = EXTRA // 2

    def put(from_chip, flip, tokens, taps):
        source = 2 * from_chip + (core ^ flip)
        dx_ref[:, pl.ds(pl.multiple_of(source * LANES, LANES), LANES)] = tokens
        rows_ref[pl.ds(pl.multiple_of(source * groups, groups), groups)] = taps + pltpu.roll(
            taps, taps_here, 1
        )

    swapped_taps = swapped_ref[2 * block_len :]
    for index, ref in enumerate((own_ref, far_ref)):
        put(chip ^ masks[index], 0, ref[:block_len], half_of(ref[2 * block_len :], 0))
        rows = swapped_ref[index * block_len : (index + 1) * block_len]
        put(chip ^ masks[index], 1, rows, half_of(swapped_taps, index))
    near = masks[2:]
    for index, ref in enumerate(near_refs):
        bits = jnp.where(core == 0, near[index], near[(index + 1) % len(near)])
        for flip in range(2):
            rows = ref[flip * block_len : (flip + 1) * block_len]
            put(chip ^ bits, flip, rows, half_of(ref[2 * block_len :], flip))
    dh_ref[...] = rows_ref[...].T[:taps_here]


def local_call(kernel, out_shape, operands, name, scratch=()):
    whole = pl.BlockSpec(memory_space=pltpu.VMEM)
    return pl.pallas_call(
        kernel,
        out_shape=out_shape,
        in_specs=[whole] * len(operands),
        out_specs=[whole] * len(out_shape),
        scratch_shapes=scratch,
        compiler_params=pltpu.CompilerParams(vmem_limit_bytes=VMEM_LIMIT),
        name=name,
    )(*operands)


def by_channels(n_seq, n_chan, out_grads, layer_inputs, filters):
    rows = out_grads.shape[0]
    block_len = layer_inputs.shape[0]
    taps_here, groups_here = filters.shape
    groups = groups_here // n_seq
    tokens = n_seq * block_len
    taps = n_seq * taps_here
    chips = n_seq // 2
    masks = partners(chips)

    def half(*shape):
        return jax.ShapeDtypeStruct(shape, jnp.bfloat16)

    unit = half(2 * block_len + EXTRA, LANES)
    x_other = xor_permute(layer_inputs, "seq", 1)
    f_other = xor_permute(filters, "seq", 1)
    (dy,) = local_call(
        functools.partial(fan_grads_kernel, n_seq),
        [half(n_seq * n_chan, rows, LANES)],
        (out_grads,),
        "fan_grads",
    )
    dy = lax.all_to_all(dy, ("seq", "chan"), split_axis=0, concat_axis=0, tiled=True)
    pieces = local_call(
        fan_inputs_kernel,
        [unit] * chips,
        (layer_inputs, x_other, filters, f_other),
        "fan_inputs",
        [pltpu.VMEM((2, groups_here, LANES), jnp.float32)],
    )
    near = masks[2:]
    near_shape = half(len(near) * (block_len + EXTRA // 2), LANES)
    dye, tap_parts, toeplitz, outside, far = local_call(
        functools.partial(first_kernel, n_seq, taps_here, masks[1]),
        [
            half(tokens + taps + LANES, LANES),
            half(chips, EXTRA, LANES),
            half(groups * SLAB, taps),
            half(SLAB, groups * SLAB),
            unit,
        ],
        (dy.reshape(tokens, LANES), *fan_out(pieces, "seq", 2)),
        "first",
        [
            pltpu.VMEM((tokens, LANES), jnp.bfloat16),
            pltpu.VMEM((chips, groups, LANES), jnp.float32),
            pltpu.VMEM((taps + LANES, groups * STEP), jnp.float32),
        ],
    )
    far = xor_permute(far, "seq", 2 * masks[1])
    (send,) = local_call(
        functools.partial(near_kernel, near, 1),
        [near_shape],
        (dye, toeplitz, outside, tap_parts),
        "near_swap",
    )
    got = xor_permute(send, "seq", 1)
    (keep,) = local_call(
        functools.partial(near_kernel, near, 0),
        [near_shape],
        (dye, toeplitz, outside, tap_parts),
        "near_keep",
    )
    pieces = local_call(near_pieces_kernel, [unit] * len(near), (keep, got), "near_pieces")
    pieces = [
        turned_permute(piece, "seq", [2 * bits for bits in near[index:] + near[:index]])
        for index, piece in enumerate(pieces)
    ]
    far, tap_parts = lax.optimization_barrier((far, tap_parts))
    (own,) = local_call(own_kernel, [unit], (dye, toeplitz, outside, tap_parts), "own")
    (send,) = local_call(
        swap_kernel, [half(2 * block_len + EXTRA, LANES)], (own, far), "swap"
    )
    return local_call(
        functools.partial(unpack_kernel, masks),
        [
            half(block_len, n_seq * LANES),
            jax.ShapeDtypeStruct((taps_here, groups_here), jnp.float32),
        ],
        (own, far, xor_permute(send, "seq", 1), *pieces),
        "unpack",
        [pltpu.VMEM((groups_here, LANES), jnp.float32)],
    )


def solution(mesh):
    n_seq, n_chan = mesh.shape["seq"], mesh.shape["chan"]

    def on_device(out_grads, layer_inputs, filters):
        taps_here, groups_here = filters.shape
        fits = (
            n_seq == 8
            and n_chan in (2, 4, 8)
            and layer_inputs.shape[1] == n_seq * LANES
            and groups_here == 8 * n_seq
            and 2 * taps_here == LANES
            and out_grads.shape[0] % 16 == 0
            and layer_inputs.shape[0] % SLAB == 0
            and n_seq * layer_inputs.shape[0] % (STEP * DEPTH // LANES) == 0
            and n_seq * taps_here + LANES <= n_seq * layer_inputs.shape[0]
        )
        if fits:
            return tuple(by_channels(n_seq, n_chan, out_grads, layer_inputs, filters))
        return by_tokens(out_grads, layer_inputs, filters)

    in_specs = (P(("seq", "chan"), None), P("seq", "chan"), P("seq", "chan"))
    out_specs = (P("seq", "chan"), P("seq", "chan"))
    return jax.shard_map(
        on_device, mesh=mesh, in_specs=in_specs, out_specs=out_specs, check_vma=False
    )
```

```python
import functools

import jax
import jax.numpy as jnp
from jax import lax
from jax.experimental import pallas as pl
from jax.experimental.pallas import tpu as pltpu
from jax.sharding import PartitionSpec as P

LANES = 128
STEP = 32
SLAB = 64
EXTRA = 16
DEPTH = 1024
VMEM_LIMIT = 40 * 1024 * 1024


def shifted(value, axis, steps):
    count = lax.axis_size(axis)
    pairs = [(source, (source + steps) % count) for source in range(count)]
    return lax.ppermute(value, axis, pairs)


def skewed_sums(products):
    groups_here, length, _ = products.shape
    padded = jnp.pad(products, ((0, 0), (0, 0), (0, length)))
    flat = padded.reshape(groups_here, 2 * length * length)[:, : length * (2 * length - 1)]
    return flat.reshape(groups_here, length, 2 * length - 1).sum(axis=1)


def by_tokens(out_grads, layer_inputs, filters):
    local_grads = lax.all_to_all(out_grads, "chan", split_axis=1, concat_axis=0, tiled=True)
    taps_all = lax.all_gather(filters, "seq", axis=0, tiled=True)
    block_len = local_grads.shape[0]
    chan_width = local_grads.shape[1]
    groups_here = filters.shape[1]
    per_group = chan_width // groups_here
    taps_total = taps_all.shape[0]
    spread_blocks = taps_total // block_len
    filt_rows = taps_all.T
    x_reversed = layer_inputs[::-1].reshape(block_len, groups_here, per_group).transpose(1, 2, 0)
    offsets = lax.broadcasted_iota(jnp.int32, (block_len, block_len), 1) - lax.broadcasted_iota(
        jnp.int32, (block_len, block_len), 0
    )
    dx_total = jnp.zeros((groups_here, per_group, block_len), jnp.float32)
    lag_buffer = jnp.zeros((groups_here, (spread_blocks + 2) * block_len), jnp.float32)
    current = local_grads
    for lag_block in range(spread_blocks + 1):
        if lag_block > 0:
            current = shifted(local_grads, "seq", -lag_block)
        dy_grouped = current.reshape(block_len, groups_here, per_group).transpose(1, 2, 0)
        lag_index = lag_block * block_len + offsets
        inside = (lag_index >= 0) & (lag_index < taps_total)
        picked = jnp.take(filt_rows, jnp.clip(lag_index, 0, taps_total - 1), axis=1)
        toeplitz = jnp.where(inside[None], picked, jnp.zeros((), jnp.bfloat16))
        dx_total = dx_total + jnp.einsum(
            "guv,gkv->gku", toeplitz, dy_grouped, preferred_element_type=jnp.float32
        )
        products = jnp.einsum(
            "gku,gkv->guv", x_reversed, dy_grouped, preferred_element_type=jnp.float32
        )
        start = lag_block * block_len
        lag_buffer = lag_buffer.at[:, start : start + 2 * block_len - 1].add(skewed_sums(products))
    partial_dh = lag_buffer[:, block_len - 1 : block_len - 1 + taps_total].T
    filter_grads = lax.psum_scatter(partial_dh, "seq", scatter_dimension=0, tiled=True)
    input_grads = dx_total.transpose(2, 0, 1).reshape(block_len, chan_width).astype(jnp.bfloat16)
    return (input_grads, filter_grads)


def xor_permute(value, axis, bits):
    pairs = [(source, source ^ bits) for source in range(lax.axis_size(axis))]
    return lax.ppermute(value, axis, pairs)


def turned_permute(value, axis, masks):
    pairs = [(source, source ^ masks[source % 2]) for source in range(lax.axis_size(axis))]
    return lax.ppermute(value, axis, pairs)


def partners(count):
    return [(count - step) % count for step in range(count)]


def fan_out(pieces, axis, unit):
    masks = partners(len(pieces))[1:]
    return [pieces[0]] + [xor_permute(p, axis, m * unit) for p, m in zip(pieces[1:], masks)]


def roll_left(value, steps):
    width = value.shape[-1]
    return pltpu.roll(value, (width - steps) % width, value.ndim - 1)


def place():
    seq = lax.axis_index("seq")
    return seq // 2, seq % 2, lax.axis_index("chan")


def rows_at(index, size):
    return pl.ds(pl.multiple_of(index * size, 16), size)


def fan_grads_kernel(n_seq, in_ref, out_ref):
    n_chan = out_ref.shape[0] // n_seq
    for seq in range(n_seq):
        for chan in range(n_chan):
            start = (chan * n_seq + seq) * LANES
            out_ref[seq * n_chan + chan] = in_ref[:, start : start + LANES]


def fan_inputs_kernel(x_own_ref, x_other_ref, f_own_ref, f_other_ref, *refs):
    *out_refs, taps_ref = refs
    chip, core, _ = place()
    block_len = x_own_ref.shape[0]
    taps_here, groups_here = f_own_ref.shape
    groups = groups_here // (2 * len(out_refs))
    rest = jnp.zeros((groups_here, LANES - taps_here), jnp.float32)
    for flip, f_ref in enumerate((f_own_ref, f_other_ref)):
        taps_ref[flip] = jnp.concatenate([f_ref[...].astype(jnp.float32).T, rest], axis=1)
    for bits, out_ref in zip(partners(len(out_refs)), out_refs):
        target = 2 * (chip ^ bits) + core
        columns = pl.ds(pl.multiple_of(target * LANES, LANES), LANES)
        out_ref[:block_len] = x_own_ref[:, columns]
        out_ref[block_len : 2 * block_len] = x_other_ref[:, columns]
        rows = pl.ds(pl.multiple_of(target * groups, groups), groups)
        taps = jnp.concatenate([taps_ref[0, rows], taps_ref[1, rows]], axis=0)
        out_ref[2 * block_len :] = taps.astype(jnp.bfloat16)


def place_inputs(in_refs, taps_here, x_ref, filt_ref):
    block_len = (in_refs[0].shape[0] - EXTRA) // 2
    groups = EXTRA // 2
    chip, core, _ = place()
    low = lax.broadcasted_iota(jnp.int32, (groups, LANES), 1) < taps_here
    for bits, in_ref in zip(partners(len(in_refs)), in_refs):
        for flip in range(2):
            block = 2 * (chip ^ bits) + (core ^ flip)
            x_ref[rows_at(block, block_len)] = in_ref[flip * block_len : (flip + 1) * block_len]
        taps = in_ref[2 * block_len :].astype(jnp.float32)
        first = jnp.where(core == 0, taps[:groups], taps[groups:])
        second = jnp.where(core == 0, taps[groups:], taps[:groups])
        filt_ref[chip ^ bits] = jnp.where(low, first, pltpu.roll(second, taps_here, 1))


def toeplitz_rows(filt_ref, toep_ref, rest_ref):
    chips, groups, _ = filt_ref.shape
    taps = chips * LANES
    tiles = [filt_ref[tile] for tile in range(chips)]
    filt = jnp.concatenate(tiles + [jnp.zeros((groups, LANES), jnp.float32)], axis=1)
    low = lax.broadcasted_iota(jnp.int32, (SLAB, LANES), 1) < SLAB
    outside = []
    for group in range(groups):
        rows = jnp.broadcast_to(filt[group : group + 1], (SLAB, taps + LANES))
        rows = pltpu.roll(rows, 0, 1, stride=1, stride_axis=0)
        toep_ref[group * SLAB : (group + 1) * SLAB] = rows[:, :taps].astype(jnp.bfloat16)
        outside.append(rows[:, taps:])
    for pair in range(groups // 2):
        both = jnp.where(low, outside[2 * pair], pltpu.roll(outside[2 * pair + 1], SLAB, 1))
        rest_ref[:, pair * LANES : (pair + 1) * LANES] = both.astype(jnp.bfloat16)


def group_of_lane(rows, width, groups):
    lane = lax.broadcasted_iota(jnp.int32, (rows, width), 1)
    return (lane % LANES) // (LANES // groups)


def tokens_of(seqs, dye_ref, toep_ref, rest_ref, out_ref, block_len):
    groups = toep_ref.shape[0] // SLAB
    taps = toep_ref.shape[1]
    starts = [seq * block_len + row for seq in seqs for row in range(0, block_len, SLAB)]

    def windows(at, size):
        return jnp.concatenate(
            [dye_ref[pl.ds(pl.multiple_of(start + at, SLAB), size)] for start in starts], axis=1
        )

    group_in = group_of_lane(SLAB, len(starts) * LANES, groups)
    after = windows(taps, SLAB)
    after = [jnp.where(group_in == group, after, jnp.zeros_like(after)) for group in range(groups)]
    full = jnp.dot(toep_ref[...], windows(0, taps), preferred_element_type=jnp.float32)
    rest = jnp.dot(
        rest_ref[...], jnp.concatenate(after, axis=0), preferred_element_type=jnp.float32
    )
    total = full[:SLAB]
    for group in range(1, groups):
        total = jnp.where(group_in == group, full[group * SLAB : (group + 1) * SLAB], total)
    total = (total + rest).astype(jnp.bfloat16)
    for index in range(len(starts)):
        columns = slice(index * LANES, (index + 1) * LANES)
        out_ref[index * SLAB : (index + 1) * SLAB] = total[:, columns]


def first_kernel(n_seq, taps_here, far, near, dy_ref, *refs):
    chips = n_seq // 2
    in_refs = refs[:chips]
    dye_ref, taps_ref, toep_ref, rest_ref, far_ref, near_ref, x_ref, filt_ref, lag_ref = refs[chips:]
    tokens = dy_ref.shape[0]
    groups = EXTRA // 2
    taps = n_seq * taps_here
    reach = taps + LANES
    chip, core, _ = place()

    place_inputs(in_refs, taps_here, x_ref, filt_ref)
    dye_ref[:tokens] = dy_ref[...]
    dye_ref[tokens:] = dy_ref[:reach]

    rows = taps + STEP
    deep = DEPTH // LANES
    group_in = group_of_lane(STEP, DEPTH, groups)
    lag_ref[rows:] = jnp.zeros((reach - rows, groups * STEP), jnp.float32)
    for at in range(0, tokens, STEP * deep):
        starts = range(at, at + STEP * deep, STEP)
        windows = jnp.concatenate([dye_ref[row : row + rows] for row in starts], axis=1)
        inputs = jnp.concatenate([x_ref[row : row + STEP] for row in starts], axis=1)
        masked = jnp.concatenate(
            [jnp.where(group_in == group, inputs, jnp.zeros_like(inputs)) for group in range(groups)],
            axis=0,
        )
        part = lax.dot_general(
            windows, masked, (((1,), (1,)), ((), ())), preferred_element_type=jnp.float32
        )
        if at == 0:
            lag_ref[:rows] = part
        else:
            lag_ref[:rows] += part
        if at == 0:
            toeplitz_rows(filt_ref, toep_ref, rest_ref)

    block_len = tokens // n_seq
    seqs = [2 * (chip ^ far) + (core ^ flip) for flip in range(2)]
    tokens_of(seqs, dye_ref, toep_ref, rest_ref, far_ref, block_len)
    seqs = [2 * (chip ^ bits) + (core ^ 1) for bits in near]
    tokens_of(seqs, dye_ref, toep_ref, rest_ref, near_ref, block_len)
    lags = lag_ref[...].T
    eights = []
    for group in range(groups):
        at = group * STEP
        rows = lags[at : at + 8]
        for high in range(1, STEP // 8):
            rows = rows + roll_left(lags[at + 8 * high : at + 8 * high + 8], 8 * high)
        eights.append(rows)
    skew = jnp.concatenate(eights, axis=0)
    row_in = lax.broadcasted_iota(jnp.int32, skew.shape, 0) % 8
    for bit in (1, 2, 4):
        skew = jnp.where((row_in & bit) != 0, roll_left(skew, bit), skew)
    dh = skew.reshape(groups, 8, reach).sum(axis=1)[:, :taps]

    high = dh.astype(jnp.bfloat16).astype(jnp.float32)
    rest = dh - high
    low = lax.broadcasted_iota(jnp.int32, (groups, LANES), 1) < taps_here
    for to_chip in range(chips):
        columns = slice(to_chip * LANES, (to_chip + 1) * LANES)
        top, bottom = high[:, columns], rest[:, columns]
        even = jnp.where(low, top, pltpu.roll(bottom, taps_here, 1))
        odd = jnp.where(low, pltpu.roll(top, taps_here, 1), bottom)
        mine = jnp.where(core == 0, even, odd)
        other = jnp.where(core == 0, odd, even)
        taps_ref[to_chip] = jnp.concatenate([mine, other], axis=0).astype(jnp.bfloat16)

    far_ref[2 * block_len :] = taps_ref[chip ^ far]
    near_ref[len(near) * block_len :] = stacked([half_of(taps_ref[chip ^ bits], 1) for bits in near])


def half_of(taps, flip):
    groups = EXTRA // 2
    return taps.astype(jnp.float32)[flip * groups : (flip + 1) * groups]


def stacked(rows):
    return jnp.concatenate(rows, axis=0).astype(jnp.bfloat16)


def near_kernel(masks, dye_ref, toep_ref, rest_ref, taps_ref, out_ref):
    chip, core, _ = place()
    block_len = (out_ref.shape[0] - len(masks) * EXTRA // 2) // len(masks)
    seqs = [2 * (chip ^ bits) + core for bits in masks]
    tokens_of(seqs, dye_ref, toep_ref, rest_ref, out_ref, block_len)
    out_ref[len(masks) * block_len :] = stacked(
        [half_of(taps_ref[chip ^ bits], 0) for bits in masks]
    )


def near_pieces_kernel(keep_ref, got_ref, *out_refs):
    _, core, _ = place()
    count = len(out_refs)
    block_len = (out_refs[0].shape[0] - EXTRA) // 2
    groups = EXTRA // 2
    keep_taps = keep_ref[count * block_len :].astype(jnp.float32)
    got_taps = got_ref[count * block_len :].astype(jnp.float32)
    taps = [
        stacked(
            [value[index * groups : (index + 1) * groups] for value in (keep_taps, got_taps)]
        )
        for index in range(count)
    ]
    for index, out_ref in enumerate(out_refs):
        other = (index + 1) % count
        out_ref[:block_len] = keep_ref[rows_at((index + core) % count, block_len)]
        out_ref[block_len : 2 * block_len] = got_ref[rows_at((index + core) % count, block_len)]
        out_ref[2 * block_len :] = jnp.where(core == 0, taps[index], taps[other])


def own_kernel(dye_ref, toep_ref, rest_ref, taps_ref, out_ref):
    chip, core, _ = place()
    block_len = (out_ref.shape[0] - EXTRA) // 2
    seqs = [2 * chip + (core ^ flip) for flip in range(2)]
    tokens_of(seqs, dye_ref, toep_ref, rest_ref, out_ref, block_len)
    out_ref[2 * block_len :] = taps_ref[chip]


def swap_kernel(*refs):
    *in_refs, out_ref = refs
    block_len = (in_refs[0].shape[0] - EXTRA) // 2
    for index, in_ref in enumerate(in_refs):
        out_ref[index * block_len : (index + 1) * block_len] = in_ref[block_len : 2 * block_len]
    out_ref[len(in_refs) * block_len :] = stacked(
        [half_of(in_ref[2 * block_len :], 1) for in_ref in in_refs]
    )


def unpack_kernel(masks, *refs):
    *near_refs, own_ref, far_ref, swapped_ref, dx_ref, dh_ref, rows_ref = refs
    chip, core, _ = place()
    block_len = dx_ref.shape[0]
    taps_here, groups_here = dh_ref.shape
    groups = EXTRA // 2

    def put(from_chip, flip, tokens, taps):
        source = 2 * from_chip + (core ^ flip)
        dx_ref[:, pl.ds(pl.multiple_of(source * LANES, LANES), LANES)] = tokens
        rows_ref[pl.ds(pl.multiple_of(source * groups, groups), groups)] = taps + pltpu.roll(
            taps, taps_here, 1
        )

    swapped_taps = swapped_ref[2 * block_len :]
    for index, ref in enumerate((own_ref, far_ref)):
        put(chip ^ masks[index], 0, ref[:block_len], half_of(ref[2 * block_len :], 0))
        rows = swapped_ref[index * block_len : (index + 1) * block_len]
        put(chip ^ masks[index], 1, rows, half_of(swapped_taps, index))
    near = masks[2:]
    for index, ref in enumerate(near_refs):
        bits = jnp.where(core == 0, near[index], near[(index + 1) % len(near)])
        for flip in range(2):
            rows = ref[flip * block_len : (flip + 1) * block_len]
            put(chip ^ bits, flip, rows, half_of(ref[2 * block_len :], flip))
    dh_ref[...] = rows_ref[...].T[:taps_here]


def local_call(kernel, out_shape, operands, name, scratch=()):
    whole = pl.BlockSpec(memory_space=pltpu.VMEM)
    return pl.pallas_call(
        kernel,
        out_shape=out_shape,
        in_specs=[whole] * len(operands),
        out_specs=[whole] * len(out_shape),
        scratch_shapes=scratch,
        compiler_params=pltpu.CompilerParams(vmem_limit_bytes=VMEM_LIMIT),
        name=name,
    )(*operands)


def by_channels(n_seq, n_chan, out_grads, layer_inputs, filters):
    rows = out_grads.shape[0]
    block_len = layer_inputs.shape[0]
    taps_here, groups_here = filters.shape
    groups = groups_here // n_seq
    tokens = n_seq * block_len
    taps = n_seq * taps_here
    chips = n_seq // 2
    masks = partners(chips)

    def half(*shape):
        return jax.ShapeDtypeStruct(shape, jnp.bfloat16)

    unit = half(2 * block_len + EXTRA, LANES)
    x_other = xor_permute(layer_inputs, "seq", 1)
    f_other = xor_permute(filters, "seq", 1)
    (dy,) = local_call(
        functools.partial(fan_grads_kernel, n_seq),
        [half(n_seq * n_chan, rows, LANES)],
        (out_grads,),
        "fan_grads",
    )
    dy = lax.all_to_all(dy, ("seq", "chan"), split_axis=0, concat_axis=0, tiled=True)
    pieces = local_call(
        fan_inputs_kernel,
        [unit] * chips,
        (layer_inputs, x_other, filters, f_other),
        "fan_inputs",
        [pltpu.VMEM((2, groups_here, LANES), jnp.float32)],
    )
    near = masks[2:]
    near_shape = half(len(near) * (block_len + EXTRA // 2), LANES)
    dye, tap_parts, toeplitz, outside, far, send = local_call(
        functools.partial(first_kernel, n_seq, taps_here, masks[1], near),
        [
            half(tokens + taps + LANES, LANES),
            half(chips, EXTRA, LANES),
            half(groups * SLAB, taps),
            half(SLAB, groups * SLAB),
            unit,
            near_shape,
        ],
        (dy.reshape(tokens, LANES), *fan_out(pieces, "seq", 2)),
        "first",
        [
            pltpu.VMEM((tokens, LANES), jnp.bfloat16),
            pltpu.VMEM((chips, groups, LANES), jnp.float32),
            pltpu.VMEM((taps + LANES, groups * STEP), jnp.float32),
        ],
    )
    far = xor_permute(far, "seq", 2 * masks[1])
    got = xor_permute(send, "seq", 1)
    (keep,) = local_call(
        functools.partial(near_kernel, near),
        [near_shape],
        (dye, toeplitz, outside, tap_parts),
        "near_keep",
    )
    pieces = local_call(near_pieces_kernel, [unit] * len(near), (keep, got), "near_pieces")
    pieces = [
        turned_permute(piece, "seq", [2 * bits for bits in near[index:] + near[:index]])
        for index, piece in enumerate(pieces)
    ]
    far, tap_parts = lax.optimization_barrier((far, tap_parts))
    (own,) = local_call(own_kernel, [unit], (dye, toeplitz, outside, tap_parts), "own")
    (send,) = local_call(
        swap_kernel, [half(2 * block_len + EXTRA, LANES)], (own, far), "swap"
    )
    return local_call(
        functools.partial(unpack_kernel, masks),
        [
            half(block_len, n_seq * LANES),
            jax.ShapeDtypeStruct((taps_here, groups_here), jnp.float32),
        ],
        (*pieces, own, far, xor_permute(send, "seq", 1)),
        "unpack",
        [pltpu.VMEM((groups_here, LANES), jnp.float32)],
    )


def solution(mesh):
    n_seq, n_chan = mesh.shape["seq"], mesh.shape["chan"]

    def on_device(out_grads, layer_inputs, filters):
        taps_here, groups_here = filters.shape
        fits = (
            n_seq == 8
            and n_chan in (2, 4, 8)
            and layer_inputs.shape[1] == n_seq * LANES
            and groups_here == 8 * n_seq
            and 2 * taps_here == LANES
            and out_grads.shape[0] % 16 == 0
            and layer_inputs.shape[0] % SLAB == 0
            and n_seq * layer_inputs.shape[0] % (STEP * DEPTH // LANES) == 0
            and n_seq * taps_here + LANES <= n_seq * layer_inputs.shape[0]
        )
        if fits:
            return tuple(by_channels(n_seq, n_chan, out_grads, layer_inputs, filters))
        return by_tokens(out_grads, layer_inputs, filters)

    in_specs = (P(("seq", "chan"), None), P("seq", "chan"), P("seq", "chan"))
    out_specs = (P("seq", "chan"), P("seq", "chan"))
    return jax.shard_map(
        on_device, mesh=mesh, in_specs=in_specs, out_specs=out_specs, check_vma=False
    )
```

```python
import functools

import jax
import jax.numpy as jnp
from jax import lax
from jax.experimental import pallas as pl
from jax.experimental.pallas import tpu as pltpu
from jax.sharding import PartitionSpec as P

LANES = 128
STEP = 32
SLAB = 64
EXTRA = 16
DEPTH = 4096
VMEM_LIMIT = 40 * 1024 * 1024


def shifted(value, axis, steps):
    count = lax.axis_size(axis)
    pairs = [(source, (source + steps) % count) for source in range(count)]
    return lax.ppermute(value, axis, pairs)


def skewed_sums(products):
    groups_here, length, _ = products.shape
    padded = jnp.pad(products, ((0, 0), (0, 0), (0, length)))
    flat = padded.reshape(groups_here, 2 * length * length)[:, : length * (2 * length - 1)]
    return flat.reshape(groups_here, length, 2 * length - 1).sum(axis=1)


def by_tokens(out_grads, layer_inputs, filters):
    local_grads = lax.all_to_all(out_grads, "chan", split_axis=1, concat_axis=0, tiled=True)
    taps_all = lax.all_gather(filters, "seq", axis=0, tiled=True)
    block_len = local_grads.shape[0]
    chan_width = local_grads.shape[1]
    groups_here = filters.shape[1]
    per_group = chan_width // groups_here
    taps_total = taps_all.shape[0]
    spread_blocks = taps_total // block_len
    filt_rows = taps_all.T
    x_reversed = layer_inputs[::-1].reshape(block_len, groups_here, per_group).transpose(1, 2, 0)
    offsets = lax.broadcasted_iota(jnp.int32, (block_len, block_len), 1) - lax.broadcasted_iota(
        jnp.int32, (block_len, block_len), 0
    )
    dx_total = jnp.zeros((groups_here, per_group, block_len), jnp.float32)
    lag_buffer = jnp.zeros((groups_here, (spread_blocks + 2) * block_len), jnp.float32)
    current = local_grads
    for lag_block in range(spread_blocks + 1):
        if lag_block > 0:
            current = shifted(local_grads, "seq", -lag_block)
        dy_grouped = current.reshape(block_len, groups_here, per_group).transpose(1, 2, 0)
        lag_index = lag_block * block_len + offsets
        inside = (lag_index >= 0) & (lag_index < taps_total)
        picked = jnp.take(filt_rows, jnp.clip(lag_index, 0, taps_total - 1), axis=1)
        toeplitz = jnp.where(inside[None], picked, jnp.zeros((), jnp.bfloat16))
        dx_total = dx_total + jnp.einsum(
            "guv,gkv->gku", toeplitz, dy_grouped, preferred_element_type=jnp.float32
        )
        products = jnp.einsum(
            "gku,gkv->guv", x_reversed, dy_grouped, preferred_element_type=jnp.float32
        )
        start = lag_block * block_len
        lag_buffer = lag_buffer.at[:, start : start + 2 * block_len - 1].add(skewed_sums(products))
    partial_dh = lag_buffer[:, block_len - 1 : block_len - 1 + taps_total].T
    filter_grads = lax.psum_scatter(partial_dh, "seq", scatter_dimension=0, tiled=True)
    input_grads = dx_total.transpose(2, 0, 1).reshape(block_len, chan_width).astype(jnp.bfloat16)
    return (input_grads, filter_grads)


def xor_permute(value, axis, bits):
    pairs = [(source, source ^ bits) for source in range(lax.axis_size(axis))]
    return lax.ppermute(value, axis, pairs)


def turned_permute(value, axis, masks):
    pairs = [(source, source ^ masks[source % 2]) for source in range(lax.axis_size(axis))]
    return lax.ppermute(value, axis, pairs)


def partners(count):
    return [(count - step) % count for step in range(count)]


def fan_out(pieces, axis, unit):
    masks = partners(len(pieces))[1:]
    return [pieces[0]] + [xor_permute(p, axis, m * unit) for p, m in zip(pieces[1:], masks)]


def roll_left(value, steps):
    width = value.shape[-1]
    return pltpu.roll(value, (width - steps) % width, value.ndim - 1)


def place():
    seq = lax.axis_index("seq")
    return seq // 2, seq % 2, lax.axis_index("chan")


def rows_at(index, size):
    return pl.ds(pl.multiple_of(index * size, 16), size)


def fan_grads_kernel(n_seq, in_ref, out_ref):
    n_chan = out_ref.shape[0] // n_seq
    for seq in range(n_seq):
        for chan in range(n_chan):
            start = (chan * n_seq + seq) * LANES
            out_ref[seq * n_chan + chan] = in_ref[:, start : start + LANES]


def fan_inputs_kernel(x_own_ref, x_other_ref, f_own_ref, f_other_ref, *refs):
    *out_refs, taps_ref = refs
    chip, core, _ = place()
    block_len = x_own_ref.shape[0]
    taps_here, groups_here = f_own_ref.shape
    groups = groups_here // (2 * len(out_refs))
    rest = jnp.zeros((groups_here, LANES - taps_here), jnp.float32)
    for flip, f_ref in enumerate((f_own_ref, f_other_ref)):
        taps_ref[flip] = jnp.concatenate([f_ref[...].astype(jnp.float32).T, rest], axis=1)
    for bits, out_ref in zip(partners(len(out_refs)), out_refs):
        target = 2 * (chip ^ bits) + core
        columns = pl.ds(pl.multiple_of(target * LANES, LANES), LANES)
        out_ref[:block_len] = x_own_ref[:, columns]
        out_ref[block_len : 2 * block_len] = x_other_ref[:, columns]
        rows = pl.ds(pl.multiple_of(target * groups, groups), groups)
        taps = jnp.concatenate([taps_ref[0, rows], taps_ref[1, rows]], axis=0)
        out_ref[2 * block_len :] = taps.astype(jnp.bfloat16)


def place_inputs(in_refs, taps_here, x_ref, filt_ref):
    block_len = (in_refs[0].shape[0] - EXTRA) // 2
    groups = EXTRA // 2
    chip, core, _ = place()
    low = lax.broadcasted_iota(jnp.int32, (groups, LANES), 1) < taps_here
    for bits, in_ref in zip(partners(len(in_refs)), in_refs):
        for flip in range(2):
            block = 2 * (chip ^ bits) + (core ^ flip)
            x_ref[rows_at(block, block_len)] = in_ref[flip * block_len : (flip + 1) * block_len]
        taps = in_ref[2 * block_len :].astype(jnp.float32)
        first = jnp.where(core == 0, taps[:groups], taps[groups:])
        second = jnp.where(core == 0, taps[groups:], taps[:groups])
        filt_ref[chip ^ bits] = jnp.where(low, first, pltpu.roll(second, taps_here, 1))


def toeplitz_rows(filt_ref, toep_ref, rest_ref):
    chips, groups, _ = filt_ref.shape
    taps = chips * LANES
    tiles = [filt_ref[tile] for tile in range(chips)]
    filt = jnp.concatenate(tiles + [jnp.zeros((groups, LANES), jnp.float32)], axis=1)
    low = lax.broadcasted_iota(jnp.int32, (SLAB, LANES), 1) < SLAB
    outside = []
    for group in range(groups):
        rows = jnp.broadcast_to(filt[group : group + 1], (SLAB, taps + LANES))
        rows = pltpu.roll(rows, 0, 1, stride=1, stride_axis=0)
        toep_ref[group * SLAB : (group + 1) * SLAB] = rows[:, :taps].astype(jnp.bfloat16)
        outside.append(rows[:, taps:])
    for pair in range(groups // 2):
        both = jnp.where(low, outside[2 * pair], pltpu.roll(outside[2 * pair + 1], SLAB, 1))
        rest_ref[:, pair * LANES : (pair + 1) * LANES] = both.astype(jnp.bfloat16)


def group_of_lane(rows, width, groups):
    lane = lax.broadcasted_iota(jnp.int32, (rows, width), 1)
    return (lane % LANES) // (LANES // groups)


def tokens_of(seqs, dye_ref, toep_ref, rest_ref, out_ref, block_len):
    groups = toep_ref.shape[0] // SLAB
    taps = toep_ref.shape[1]
    starts = [seq * block_len + row for seq in seqs for row in range(0, block_len, SLAB)]

    def windows(at, size):
        return jnp.concatenate(
            [dye_ref[pl.ds(pl.multiple_of(start + at, SLAB), size)] for start in starts], axis=1
        )

    group_in = group_of_lane(SLAB, len(starts) * LANES, groups)
    after = windows(taps, SLAB)
    after = [jnp.where(group_in == group, after, jnp.zeros_like(after)) for group in range(groups)]
    full = jnp.dot(toep_ref[...], windows(0, taps), preferred_element_type=jnp.float32)
    rest = jnp.dot(
        rest_ref[...], jnp.concatenate(after, axis=0), preferred_element_type=jnp.float32
    )
    total = full[:SLAB]
    for group in range(1, groups):
        total = jnp.where(group_in == group, full[group * SLAB : (group + 1) * SLAB], total)
    total = (total + rest).astype(jnp.bfloat16)
    for index in range(len(starts)):
        columns = slice(index * LANES, (index + 1) * LANES)
        out_ref[index * SLAB : (index + 1) * SLAB] = total[:, columns]


def first_kernel(n_seq, taps_here, far, near, dy_ref, *refs):
    chips = n_seq // 2
    in_refs = refs[:chips]
    dye_ref, taps_ref, toep_ref, rest_ref, far_ref, near_ref, x_ref, filt_ref, lag_ref = refs[chips:]
    tokens = dy_ref.shape[0]
    groups = EXTRA // 2
    taps = n_seq * taps_here
    reach = taps + LANES
    chip, core, _ = place()

    place_inputs(in_refs, taps_here, x_ref, filt_ref)
    dye_ref[:tokens] = dy_ref[...]
    dye_ref[tokens:] = dy_ref[:reach]

    rows = taps + STEP
    deep = DEPTH // LANES
    group_in = group_of_lane(STEP, DEPTH, groups)
    lag_ref[rows:] = jnp.zeros((reach - rows, groups * STEP), jnp.float32)
    for at in range(0, tokens, STEP * deep):
        starts = range(at, at + STEP * deep, STEP)
        windows = jnp.concatenate([dye_ref[row : row + rows] for row in starts], axis=1)
        inputs = jnp.concatenate([x_ref[row : row + STEP] for row in starts], axis=1)
        masked = jnp.concatenate(
            [jnp.where(group_in == group, inputs, jnp.zeros_like(inputs)) for group in range(groups)],
            axis=0,
        )
        part = lax.dot_general(
            windows, masked, (((1,), (1,)), ((), ())), preferred_element_type=jnp.float32
        )
        if at == 0:
            lag_ref[:rows] = part
        else:
            lag_ref[:rows] += part
        if at == 0:
            toeplitz_rows(filt_ref, toep_ref, rest_ref)

    block_len = tokens // n_seq
    seqs = [2 * (chip ^ far) + (core ^ flip) for flip in range(2)]
    tokens_of(seqs, dye_ref, toep_ref, rest_ref, far_ref, block_len)
    seqs = [2 * (chip ^ bits) + (core ^ 1) for bits in near]
    tokens_of(seqs, dye_ref, toep_ref, rest_ref, near_ref, block_len)
    lags = lag_ref[...].T
    eights = []
    for group in range(groups):
        at = group * STEP
        rows = lags[at : at + 8]
        for high in range(1, STEP // 8):
            rows = rows + roll_left(lags[at + 8 * high : at + 8 * high + 8], 8 * high)
        eights.append(rows)
    skew = jnp.concatenate(eights, axis=0)
    row_in = lax.broadcasted_iota(jnp.int32, skew.shape, 0) % 8
    for bit in (1, 2, 4):
        skew = jnp.where((row_in & bit) != 0, roll_left(skew, bit), skew)
    dh = skew.reshape(groups, 8, reach).sum(axis=1)[:, :taps]

    high = dh.astype(jnp.bfloat16).astype(jnp.float32)
    rest = dh - high
    low = lax.broadcasted_iota(jnp.int32, (groups, LANES), 1) < taps_here
    for to_chip in range(chips):
        columns = slice(to_chip * LANES, (to_chip + 1) * LANES)
        top, bottom = high[:, columns], rest[:, columns]
        even = jnp.where(low, top, pltpu.roll(bottom, taps_here, 1))
        odd = jnp.where(low, pltpu.roll(top, taps_here, 1), bottom)
        mine = jnp.where(core == 0, even, odd)
        other = jnp.where(core == 0, odd, even)
        taps_ref[to_chip] = jnp.concatenate([mine, other], axis=0).astype(jnp.bfloat16)

    far_ref[2 * block_len :] = taps_ref[chip ^ far]
    near_ref[len(near) * block_len :] = stacked([half_of(taps_ref[chip ^ bits], 1) for bits in near])


def half_of(taps, flip):
    groups = EXTRA // 2
    return taps.astype(jnp.float32)[flip * groups : (flip + 1) * groups]


def stacked(rows):
    return jnp.concatenate(rows, axis=0).astype(jnp.bfloat16)


def near_kernel(masks, dye_ref, toep_ref, rest_ref, taps_ref, out_ref):
    chip, core, _ = place()
    block_len = (out_ref.shape[0] - len(masks) * EXTRA // 2) // len(masks)
    seqs = [2 * (chip ^ bits) + core for bits in masks]
    tokens_of(seqs, dye_ref, toep_ref, rest_ref, out_ref, block_len)
    out_ref[len(masks) * block_len :] = stacked(
        [half_of(taps_ref[chip ^ bits], 0) for bits in masks]
    )


def near_pieces_kernel(keep_ref, got_ref, *out_refs):
    _, core, _ = place()
    count = len(out_refs)
    block_len = (out_refs[0].shape[0] - EXTRA) // 2
    groups = EXTRA // 2
    keep_taps = keep_ref[count * block_len :].astype(jnp.float32)
    got_taps = got_ref[count * block_len :].astype(jnp.float32)
    taps = [
        stacked(
            [value[index * groups : (index + 1) * groups] for value in (keep_taps, got_taps)]
        )
        for index in range(count)
    ]
    for index, out_ref in enumerate(out_refs):
        other = (index + 1) % count
        out_ref[:block_len] = keep_ref[rows_at((index + core) % count, block_len)]
        out_ref[block_len : 2 * block_len] = got_ref[rows_at((index + core) % count, block_len)]
        out_ref[2 * block_len :] = jnp.where(core == 0, taps[index], taps[other])


def own_kernel(dye_ref, toep_ref, rest_ref, taps_ref, out_ref):
    chip, core, _ = place()
    block_len = (out_ref.shape[0] - EXTRA) // 2
    seqs = [2 * chip + (core ^ flip) for flip in range(2)]
    tokens_of(seqs, dye_ref, toep_ref, rest_ref, out_ref, block_len)
    out_ref[2 * block_len :] = taps_ref[chip]


def swap_kernel(*refs):
    *in_refs, out_ref = refs
    block_len = (in_refs[0].shape[0] - EXTRA) // 2
    for index, in_ref in enumerate(in_refs):
        out_ref[index * block_len : (index + 1) * block_len] = in_ref[block_len : 2 * block_len]
    out_ref[len(in_refs) * block_len :] = stacked(
        [half_of(in_ref[2 * block_len :], 1) for in_ref in in_refs]
    )


def unpack_kernel(masks, *refs):
    *near_refs, own_ref, far_ref, swapped_ref, dx_ref, dh_ref, rows_ref = refs
    chip, core, _ = place()
    block_len = dx_ref.shape[0]
    taps_here, groups_here = dh_ref.shape
    groups = EXTRA // 2

    def put(from_chip, flip, tokens, taps):
        source = 2 * from_chip + (core ^ flip)
        dx_ref[:, pl.ds(pl.multiple_of(source * LANES, LANES), LANES)] = tokens
        rows_ref[pl.ds(pl.multiple_of(source * groups, groups), groups)] = taps + pltpu.roll(
            taps, taps_here, 1
        )

    swapped_taps = swapped_ref[2 * block_len :]
    for index, ref in enumerate((own_ref, far_ref)):
        put(chip ^ masks[index], 0, ref[:block_len], half_of(ref[2 * block_len :], 0))
        rows = swapped_ref[index * block_len : (index + 1) * block_len]
        put(chip ^ masks[index], 1, rows, half_of(swapped_taps, index))
    near = masks[2:]
    for index, ref in enumerate(near_refs):
        bits = jnp.where(core == 0, near[index], near[(index + 1) % len(near)])
        for flip in range(2):
            rows = ref[flip * block_len : (flip + 1) * block_len]
            put(chip ^ bits, flip, rows, half_of(ref[2 * block_len :], flip))
    dh_ref[...] = rows_ref[...].T[:taps_here]


def local_call(kernel, out_shape, operands, name, scratch=()):
    whole = pl.BlockSpec(memory_space=pltpu.VMEM)
    return pl.pallas_call(
        kernel,
        out_shape=out_shape,
        in_specs=[whole] * len(operands),
        out_specs=[whole] * len(out_shape),
        scratch_shapes=scratch,
        compiler_params=pltpu.CompilerParams(vmem_limit_bytes=VMEM_LIMIT),
        name=name,
    )(*operands)


def by_channels(n_seq, n_chan, out_grads, layer_inputs, filters):
    rows = out_grads.shape[0]
    block_len = layer_inputs.shape[0]
    taps_here, groups_here = filters.shape
    groups = groups_here // n_seq
    tokens = n_seq * block_len
    taps = n_seq * taps_here
    chips = n_seq // 2
    masks = partners(chips)

    def half(*shape):
        return jax.ShapeDtypeStruct(shape, jnp.bfloat16)

    unit = half(2 * block_len + EXTRA, LANES)
    x_other = xor_permute(layer_inputs, "seq", 1)
    f_other = xor_permute(filters, "seq", 1)
    (dy,) = local_call(
        functools.partial(fan_grads_kernel, n_seq),
        [half(n_seq * n_chan, rows, LANES)],
        (out_grads,),
        "fan_grads",
    )
    dy = lax.all_to_all(dy, ("seq", "chan"), split_axis=0, concat_axis=0, tiled=True)
    pieces = local_call(
        fan_inputs_kernel,
        [unit] * chips,
        (layer_inputs, x_other, filters, f_other),
        "fan_inputs",
        [pltpu.VMEM((2, groups_here, LANES), jnp.float32)],
    )
    near = masks[2:]
    near_shape = half(len(near) * (block_len + EXTRA // 2), LANES)
    dye, tap_parts, toeplitz, outside, far, send = local_call(
        functools.partial(first_kernel, n_seq, taps_here, masks[1], near),
        [
            half(tokens + taps + LANES, LANES),
            half(chips, EXTRA, LANES),
            half(groups * SLAB, taps),
            half(SLAB, groups * SLAB),
            unit,
            near_shape,
        ],
        (dy.reshape(tokens, LANES), *fan_out(pieces, "seq", 2)),
        "first",
        [
            pltpu.VMEM((tokens, LANES), jnp.bfloat16),
            pltpu.VMEM((chips, groups, LANES), jnp.float32),
            pltpu.VMEM((taps + LANES, groups * STEP), jnp.float32),
        ],
    )
    far = xor_permute(far, "seq", 2 * masks[1])
    got = xor_permute(send, "seq", 1)
    (keep,) = local_call(
        functools.partial(near_kernel, near),
        [near_shape],
        (dye, toeplitz, outside, tap_parts),
        "near_keep",
    )
    pieces = local_call(near_pieces_kernel, [unit] * len(near), (keep, got), "near_pieces")
    pieces = [
        turned_permute(piece, "seq", [2 * bits for bits in near[index:] + near[:index]])
        for index, piece in enumerate(pieces)
    ]
    far, tap_parts = lax.optimization_barrier((far, tap_parts))
    (own,) = local_call(own_kernel, [unit], (dye, toeplitz, outside, tap_parts), "own")
    (send,) = local_call(
        swap_kernel, [half(2 * block_len + EXTRA, LANES)], (own, far), "swap"
    )
    return local_call(
        functools.partial(unpack_kernel, masks),
        [
            half(block_len, n_seq * LANES),
            jax.ShapeDtypeStruct((taps_here, groups_here), jnp.float32),
        ],
        (*pieces, own, far, xor_permute(send, "seq", 1)),
        "unpack",
        [pltpu.VMEM((groups_here, LANES), jnp.float32)],
    )


def solution(mesh):
    n_seq, n_chan = mesh.shape["seq"], mesh.shape["chan"]

    def on_device(out_grads, layer_inputs, filters):
        taps_here, groups_here = filters.shape
        fits = (
            n_seq == 8
            and n_chan in (2, 4, 8)
            and layer_inputs.shape[1] == n_seq * LANES
            and groups_here == 8 * n_seq
            and 2 * taps_here == LANES
            and out_grads.shape[0] % 16 == 0
            and layer_inputs.shape[0] % SLAB == 0
            and n_seq * layer_inputs.shape[0] % (STEP * DEPTH // LANES) == 0
            and n_seq * taps_here + LANES <= n_seq * layer_inputs.shape[0]
        )
        if fits:
            return tuple(by_channels(n_seq, n_chan, out_grads, layer_inputs, filters))
        return by_tokens(out_grads, layer_inputs, filters)

    in_specs = (P(("seq", "chan"), None), P("seq", "chan"), P("seq", "chan"))
    out_specs = (P("seq", "chan"), P("seq", "chan"))
    return jax.shard_map(
        on_device, mesh=mesh, in_specs=in_specs, out_specs=out_specs, check_vma=False
    )
```

```python
import functools

import jax
import jax.numpy as jnp
from jax import lax
from jax.experimental import pallas as pl
from jax.experimental.pallas import tpu as pltpu
from jax.sharding import PartitionSpec as P

LANES = 128
STEP = 32
SLAB = 64
EXTRA = 16
DEPTH = 4096
VMEM_LIMIT = 40 * 1024 * 1024


def shifted(value, axis, steps):
    count = lax.axis_size(axis)
    pairs = [(source, (source + steps) % count) for source in range(count)]
    return lax.ppermute(value, axis, pairs)


def skewed_sums(products):
    groups_here, length, _ = products.shape
    padded = jnp.pad(products, ((0, 0), (0, 0), (0, length)))
    flat = padded.reshape(groups_here, 2 * length * length)[:, : length * (2 * length - 1)]
    return flat.reshape(groups_here, length, 2 * length - 1).sum(axis=1)


def by_tokens(out_grads, layer_inputs, filters):
    local_grads = lax.all_to_all(out_grads, "chan", split_axis=1, concat_axis=0, tiled=True)
    taps_all = lax.all_gather(filters, "seq", axis=0, tiled=True)
    block_len = local_grads.shape[0]
    chan_width = local_grads.shape[1]
    groups_here = filters.shape[1]
    per_group = chan_width // groups_here
    taps_total = taps_all.shape[0]
    spread_blocks = taps_total // block_len
    filt_rows = taps_all.T
    x_reversed = layer_inputs[::-1].reshape(block_len, groups_here, per_group).transpose(1, 2, 0)
    offsets = lax.broadcasted_iota(jnp.int32, (block_len, block_len), 1) - lax.broadcasted_iota(
        jnp.int32, (block_len, block_len), 0
    )
    dx_total = jnp.zeros((groups_here, per_group, block_len), jnp.float32)
    lag_buffer = jnp.zeros((groups_here, (spread_blocks + 2) * block_len), jnp.float32)
    current = local_grads
    for lag_block in range(spread_blocks + 1):
        if lag_block > 0:
            current = shifted(local_grads, "seq", -lag_block)
        dy_grouped = current.reshape(block_len, groups_here, per_group).transpose(1, 2, 0)
        lag_index = lag_block * block_len + offsets
        inside = (lag_index >= 0) & (lag_index < taps_total)
        picked = jnp.take(filt_rows, jnp.clip(lag_index, 0, taps_total - 1), axis=1)
        toeplitz = jnp.where(inside[None], picked, jnp.zeros((), jnp.bfloat16))
        dx_total = dx_total + jnp.einsum(
            "guv,gkv->gku", toeplitz, dy_grouped, preferred_element_type=jnp.float32
        )
        products = jnp.einsum(
            "gku,gkv->guv", x_reversed, dy_grouped, preferred_element_type=jnp.float32
        )
        start = lag_block * block_len
        lag_buffer = lag_buffer.at[:, start : start + 2 * block_len - 1].add(skewed_sums(products))
    partial_dh = lag_buffer[:, block_len - 1 : block_len - 1 + taps_total].T
    filter_grads = lax.psum_scatter(partial_dh, "seq", scatter_dimension=0, tiled=True)
    input_grads = dx_total.transpose(2, 0, 1).reshape(block_len, chan_width).astype(jnp.bfloat16)
    return (input_grads, filter_grads)


def xor_permute(value, axis, bits):
    pairs = [(source, source ^ bits) for source in range(lax.axis_size(axis))]
    return lax.ppermute(value, axis, pairs)


def turned_permute(value, axis, masks):
    pairs = [(source, source ^ masks[source % 2]) for source in range(lax.axis_size(axis))]
    return lax.ppermute(value, axis, pairs)


def partners(count):
    return [(count - step) % count for step in range(count)]


def fan_out(pieces, axis, unit):
    masks = partners(len(pieces))[1:]
    return [pieces[0]] + [xor_permute(p, axis, m * unit) for p, m in zip(pieces[1:], masks)]


def roll_left(value, steps):
    width = value.shape[-1]
    return pltpu.roll(value, (width - steps) % width, value.ndim - 1)


def place():
    seq = lax.axis_index("seq")
    return seq // 2, seq % 2, lax.axis_index("chan")


def rows_at(index, size):
    return pl.ds(pl.multiple_of(index * size, 16), size)


def fan_grads_kernel(n_seq, order, in_ref, out_ref):
    n_chan = out_ref.shape[0] // n_seq
    for index, device in enumerate(order):
        start = (device % n_chan * n_seq + device // n_chan) * LANES
        out_ref[index] = in_ref[:, start : start + LANES]


def fan_inputs_kernel(x_own_ref, x_other_ref, f_own_ref, f_other_ref, *refs):
    *out_refs, taps_ref = refs
    chip, core, _ = place()
    block_len = x_own_ref.shape[0]
    taps_here, groups_here = f_own_ref.shape
    groups = groups_here // (2 * len(out_refs))
    rest = jnp.zeros((groups_here, LANES - taps_here), jnp.float32)
    for flip, f_ref in enumerate((f_own_ref, f_other_ref)):
        taps_ref[flip] = jnp.concatenate([f_ref[...].astype(jnp.float32).T, rest], axis=1)
    for bits, out_ref in zip(partners(len(out_refs)), out_refs):
        target = 2 * (chip ^ bits) + core
        columns = pl.ds(pl.multiple_of(target * LANES, LANES), LANES)
        out_ref[:block_len] = x_own_ref[:, columns]
        out_ref[block_len : 2 * block_len] = x_other_ref[:, columns]
        rows = pl.ds(pl.multiple_of(target * groups, groups), groups)
        taps = jnp.concatenate([taps_ref[0, rows], taps_ref[1, rows]], axis=0)
        out_ref[2 * block_len :] = taps.astype(jnp.bfloat16)


def place_inputs(in_refs, taps_here, x_ref, filt_ref):
    block_len = (in_refs[0].shape[0] - EXTRA) // 2
    groups = EXTRA // 2
    chip, core, _ = place()
    low = lax.broadcasted_iota(jnp.int32, (groups, LANES), 1) < taps_here
    for bits, in_ref in zip(partners(len(in_refs)), in_refs):
        for flip in range(2):
            block = 2 * (chip ^ bits) + (core ^ flip)
            x_ref[rows_at(block, block_len)] = in_ref[flip * block_len : (flip + 1) * block_len]
        taps = in_ref[2 * block_len :].astype(jnp.float32)
        first = jnp.where(core == 0, taps[:groups], taps[groups:])
        second = jnp.where(core == 0, taps[groups:], taps[:groups])
        filt_ref[chip ^ bits] = jnp.where(low, first, pltpu.roll(second, taps_here, 1))


def toeplitz_rows(filt_ref, toep_ref, rest_ref):
    chips, groups, _ = filt_ref.shape
    taps = chips * LANES
    tiles = [filt_ref[tile] for tile in range(chips)]
    filt = jnp.concatenate(tiles + [jnp.zeros((groups, LANES), jnp.float32)], axis=1)
    low = lax.broadcasted_iota(jnp.int32, (SLAB, LANES), 1) < SLAB
    outside = []
    for group in range(groups):
        rows = jnp.broadcast_to(filt[group : group + 1], (SLAB, taps + LANES))
        rows = pltpu.roll(rows, 0, 1, stride=1, stride_axis=0)
        toep_ref[group * SLAB : (group + 1) * SLAB] = rows[:, :taps].astype(jnp.bfloat16)
        outside.append(rows[:, taps:])
    for pair in range(groups // 2):
        both = jnp.where(low, outside[2 * pair], pltpu.roll(outside[2 * pair + 1], SLAB, 1))
        rest_ref[:, pair * LANES : (pair + 1) * LANES] = both.astype(jnp.bfloat16)


def group_of_lane(rows, width, groups):
    lane = lax.broadcasted_iota(jnp.int32, (rows, width), 1)
    return (lane % LANES) // (LANES // groups)


def tokens_of(seqs, dye_ref, toep_ref, rest_ref, out_ref, block_len):
    groups = toep_ref.shape[0] // SLAB
    taps = toep_ref.shape[1]
    starts = [seq * block_len + row for seq in seqs for row in range(0, block_len, SLAB)]

    def windows(at, size):
        return jnp.concatenate(
            [dye_ref[pl.ds(pl.multiple_of(start + at, SLAB), size)] for start in starts], axis=1
        )

    group_in = group_of_lane(SLAB, len(starts) * LANES, groups)
    after = windows(taps, SLAB)
    after = [jnp.where(group_in == group, after, jnp.zeros_like(after)) for group in range(groups)]
    full = jnp.dot(toep_ref[...], windows(0, taps), preferred_element_type=jnp.float32)
    rest = jnp.dot(
        rest_ref[...], jnp.concatenate(after, axis=0), preferred_element_type=jnp.float32
    )
    total = full[:SLAB]
    for group in range(1, groups):
        total = jnp.where(group_in == group, full[group * SLAB : (group + 1) * SLAB], total)
    total = (total + rest).astype(jnp.bfloat16)
    for index in range(len(starts)):
        columns = slice(index * LANES, (index + 1) * LANES)
        out_ref[index * SLAB : (index + 1) * SLAB] = total[:, columns]


def first_kernel(n_seq, taps_here, far, near, ahead, dy_ref, *refs):
    chips = n_seq // 2
    in_refs = refs[:chips]
    dye_ref, taps_ref, toep_ref, rest_ref, far_ref, near_ref, x_ref, filt_ref, lag_ref = refs[chips:]
    tokens = dy_ref.shape[0]
    groups = EXTRA // 2
    taps = n_seq * taps_here
    reach = taps + LANES
    chip, core, _ = place()

    place_inputs(in_refs, taps_here, x_ref, filt_ref)
    dye_ref[ahead:tokens] = dy_ref[: tokens - ahead]
    dye_ref[:ahead] = dy_ref[tokens - ahead :]
    dye_ref[tokens:] = dye_ref[:reach]

    rows = taps + STEP
    deep = DEPTH // LANES
    group_in = group_of_lane(STEP, DEPTH, groups)
    lag_ref[rows:] = jnp.zeros((reach - rows, groups * STEP), jnp.float32)
    for at in range(0, tokens, STEP * deep):
        starts = range(at, at + STEP * deep, STEP)
        windows = jnp.concatenate([dye_ref[row : row + rows] for row in starts], axis=1)
        inputs = jnp.concatenate([x_ref[row : row + STEP] for row in starts], axis=1)
        masked = jnp.concatenate(
            [jnp.where(group_in == group, inputs, jnp.zeros_like(inputs)) for group in range(groups)],
            axis=0,
        )
        part = lax.dot_general(
            windows, masked, (((1,), (1,)), ((), ())), preferred_element_type=jnp.float32
        )
        if at == 0:
            lag_ref[:rows] = part
        else:
            lag_ref[:rows] += part
        if at == 0:
            toeplitz_rows(filt_ref, toep_ref, rest_ref)

    block_len = tokens // n_seq
    seqs = [2 * (chip ^ far) + (core ^ flip) for flip in range(2)]
    tokens_of(seqs, dye_ref, toep_ref, rest_ref, far_ref, block_len)
    seqs = [2 * (chip ^ bits) + (core ^ 1) for bits in near]
    tokens_of(seqs, dye_ref, toep_ref, rest_ref, near_ref, block_len)
    lags = lag_ref[...].T
    eights = []
    for group in range(groups):
        at = group * STEP
        rows = lags[at : at + 8]
        for high in range(1, STEP // 8):
            rows = rows + roll_left(lags[at + 8 * high : at + 8 * high + 8], 8 * high)
        eights.append(rows)
    skew = jnp.concatenate(eights, axis=0)
    row_in = lax.broadcasted_iota(jnp.int32, skew.shape, 0) % 8
    for bit in (1, 2, 4):
        skew = jnp.where((row_in & bit) != 0, roll_left(skew, bit), skew)
    dh = skew.reshape(groups, 8, reach).sum(axis=1)[:, :taps]

    high = dh.astype(jnp.bfloat16).astype(jnp.float32)
    rest = dh - high
    low = lax.broadcasted_iota(jnp.int32, (groups, LANES), 1) < taps_here
    for to_chip in range(chips):
        columns = slice(to_chip * LANES, (to_chip + 1) * LANES)
        top, bottom = high[:, columns], rest[:, columns]
        even = jnp.where(low, top, pltpu.roll(bottom, taps_here, 1))
        odd = jnp.where(low, pltpu.roll(top, taps_here, 1), bottom)
        mine = jnp.where(core == 0, even, odd)
        other = jnp.where(core == 0, odd, even)
        taps_ref[to_chip] = jnp.concatenate([mine, other], axis=0).astype(jnp.bfloat16)

    far_ref[2 * block_len :] = taps_ref[chip ^ far]
    near_ref[len(near) * block_len :] = stacked([half_of(taps_ref[chip ^ bits], 1) for bits in near])


def half_of(taps, flip):
    groups = EXTRA // 2
    return taps.astype(jnp.float32)[flip * groups : (flip + 1) * groups]


def stacked(rows):
    return jnp.concatenate(rows, axis=0).astype(jnp.bfloat16)


def near_kernel(masks, dye_ref, toep_ref, rest_ref, taps_ref, out_ref):
    chip, core, _ = place()
    block_len = (out_ref.shape[0] - len(masks) * EXTRA // 2) // len(masks)
    seqs = [2 * (chip ^ bits) + core for bits in masks]
    tokens_of(seqs, dye_ref, toep_ref, rest_ref, out_ref, block_len)
    out_ref[len(masks) * block_len :] = stacked(
        [half_of(taps_ref[chip ^ bits], 0) for bits in masks]
    )


def near_pieces_kernel(keep_ref, got_ref, *out_refs):
    _, core, _ = place()
    count = len(out_refs)
    block_len = (out_refs[0].shape[0] - EXTRA) // 2
    groups = EXTRA // 2
    keep_taps = keep_ref[count * block_len :].astype(jnp.float32)
    got_taps = got_ref[count * block_len :].astype(jnp.float32)
    taps = [
        stacked(
            [value[index * groups : (index + 1) * groups] for value in (keep_taps, got_taps)]
        )
        for index in range(count)
    ]
    for index, out_ref in enumerate(out_refs):
        other = (index + 1) % count
        out_ref[:block_len] = keep_ref[rows_at((index + core) % count, block_len)]
        out_ref[block_len : 2 * block_len] = got_ref[rows_at((index + core) % count, block_len)]
        out_ref[2 * block_len :] = jnp.where(core == 0, taps[index], taps[other])


def own_kernel(dye_ref, toep_ref, rest_ref, taps_ref, out_ref):
    chip, core, _ = place()
    block_len = (out_ref.shape[0] - EXTRA) // 2
    seqs = [2 * chip + (core ^ flip) for flip in range(2)]
    tokens_of(seqs, dye_ref, toep_ref, rest_ref, out_ref, block_len)
    out_ref[2 * block_len :] = taps_ref[chip]


def swap_kernel(*refs):
    *in_refs, out_ref = refs
    block_len = (in_refs[0].shape[0] - EXTRA) // 2
    for index, in_ref in enumerate(in_refs):
        out_ref[index * block_len : (index + 1) * block_len] = in_ref[block_len : 2 * block_len]
    out_ref[len(in_refs) * block_len :] = stacked(
        [half_of(in_ref[2 * block_len :], 1) for in_ref in in_refs]
    )


def unpack_kernel(masks, *refs):
    *near_refs, own_ref, far_ref, swapped_ref, dx_ref, dh_ref, rows_ref = refs
    chip, core, _ = place()
    block_len = dx_ref.shape[0]
    taps_here, groups_here = dh_ref.shape
    groups = EXTRA // 2

    def put(from_chip, flip, tokens, taps):
        source = 2 * from_chip + (core ^ flip)
        dx_ref[:, pl.ds(pl.multiple_of(source * LANES, LANES), LANES)] = tokens
        rows_ref[pl.ds(pl.multiple_of(source * groups, groups), groups)] = taps + pltpu.roll(
            taps, taps_here, 1
        )

    swapped_taps = swapped_ref[2 * block_len :]
    for index, ref in enumerate((own_ref, far_ref)):
        put(chip ^ masks[index], 0, ref[:block_len], half_of(ref[2 * block_len :], 0))
        rows = swapped_ref[index * block_len : (index + 1) * block_len]
        put(chip ^ masks[index], 1, rows, half_of(swapped_taps, index))
    near = masks[2:]
    for index, ref in enumerate(near_refs):
        bits = jnp.where(core == 0, near[index], near[(index + 1) % len(near)])
        for flip in range(2):
            rows = ref[flip * block_len : (flip + 1) * block_len]
            put(chip ^ bits, flip, rows, half_of(ref[2 * block_len :], flip))
    dh_ref[...] = rows_ref[...].T[:taps_here]


def local_call(kernel, out_shape, operands, name, scratch=()):
    whole = pl.BlockSpec(memory_space=pltpu.VMEM)
    return pl.pallas_call(
        kernel,
        out_shape=out_shape,
        in_specs=[whole] * len(operands),
        out_specs=[whole] * len(out_shape),
        scratch_shapes=scratch,
        compiler_params=pltpu.CompilerParams(vmem_limit_bytes=VMEM_LIMIT),
        name=name,
    )(*operands)


def by_channels(n_seq, n_chan, out_grads, layer_inputs, filters):
    rows = out_grads.shape[0]
    block_len = layer_inputs.shape[0]
    taps_here, groups_here = filters.shape
    groups = groups_here // n_seq
    tokens = n_seq * block_len
    taps = n_seq * taps_here
    chips = n_seq // 2
    masks = partners(chips)

    def half(*shape):
        return jax.ShapeDtypeStruct(shape, jnp.bfloat16)

    unit = half(2 * block_len + EXTRA, LANES)
    order = [(n_chan // 2 + index) % (n_seq * n_chan) for index in range(n_seq * n_chan)]
    x_other = xor_permute(layer_inputs, "seq", 1)
    f_other = xor_permute(filters, "seq", 1)
    (dy,) = local_call(
        functools.partial(fan_grads_kernel, n_seq, order),
        [half(n_seq * n_chan, rows, LANES)],
        (out_grads,),
        "fan_grads",
    )
    dy = lax.all_to_all(
        dy, ("seq", "chan"), split_axis=0, concat_axis=0, axis_index_groups=[order], tiled=True
    )
    pieces = local_call(
        fan_inputs_kernel,
        [unit] * chips,
        (layer_inputs, x_other, filters, f_other),
        "fan_inputs",
        [pltpu.VMEM((2, groups_here, LANES), jnp.float32)],
    )
    near = masks[2:]
    near_shape = half(len(near) * (block_len + EXTRA // 2), LANES)
    dye, tap_parts, toeplitz, outside, far, send = local_call(
        functools.partial(first_kernel, n_seq, taps_here, masks[1], near, order[0] * rows),
        [
            half(tokens + taps + LANES, LANES),
            half(chips, EXTRA, LANES),
            half(groups * SLAB, taps),
            half(SLAB, groups * SLAB),
            unit,
            near_shape,
        ],
        (dy.reshape(tokens, LANES), *fan_out(pieces, "seq", 2)),
        "first",
        [
            pltpu.VMEM((tokens, LANES), jnp.bfloat16),
            pltpu.VMEM((chips, groups, LANES), jnp.float32),
            pltpu.VMEM((taps + LANES, groups * STEP), jnp.float32),
        ],
    )
    far = xor_permute(far, "seq", 2 * masks[1])
    got = xor_permute(send, "seq", 1)
    (keep,) = local_call(
        functools.partial(near_kernel, near),
        [near_shape],
        (dye, toeplitz, outside, tap_parts),
        "near_keep",
    )
    pieces = local_call(near_pieces_kernel, [unit] * len(near), (keep, got), "near_pieces")
    pieces = [
        turned_permute(piece, "seq", [2 * bits for bits in near[index:] + near[:index]])
        for index, piece in enumerate(pieces)
    ]
    far, tap_parts = lax.optimization_barrier((far, tap_parts))
    (own,) = local_call(own_kernel, [unit], (dye, toeplitz, outside, tap_parts), "own")
    (send,) = local_call(
        swap_kernel, [half(2 * block_len + EXTRA, LANES)], (own, far), "swap"
    )
    return local_call(
        functools.partial(unpack_kernel, masks),
        [
            half(block_len, n_seq * LANES),
            jax.ShapeDtypeStruct((taps_here, groups_here), jnp.float32),
        ],
        (*pieces, own, far, xor_permute(send, "seq", 1)),
        "unpack",
        [pltpu.VMEM((groups_here, LANES), jnp.float32)],
    )


def solution(mesh):
    n_seq, n_chan = mesh.shape["seq"], mesh.shape["chan"]

    def on_device(out_grads, layer_inputs, filters):
        taps_here, groups_here = filters.shape
        fits = (
            n_seq == 8
            and n_chan in (2, 4, 8)
            and layer_inputs.shape[1] == n_seq * LANES
            and groups_here == 8 * n_seq
            and 2 * taps_here == LANES
            and out_grads.shape[0] % 16 == 0
            and layer_inputs.shape[0] % SLAB == 0
            and n_seq * layer_inputs.shape[0] % (STEP * DEPTH // LANES) == 0
            and n_seq * taps_here + LANES <= n_seq * layer_inputs.shape[0]
        )
        if fits:
            return tuple(by_channels(n_seq, n_chan, out_grads, layer_inputs, filters))
        return by_tokens(out_grads, layer_inputs, filters)

    in_specs = (P(("seq", "chan"), None), P("seq", "chan"), P("seq", "chan"))
    out_specs = (P("seq", "chan"), P("seq", "chan"))
    return jax.shard_map(
        on_device, mesh=mesh, in_specs=in_specs, out_specs=out_specs, check_vma=False
    )
```

```python
import functools

import jax
import jax.numpy as jnp
from jax import lax
from jax.experimental import pallas as pl
from jax.experimental.pallas import tpu as pltpu
from jax.sharding import PartitionSpec as P

LANES = 128
STEP = 32
SLAB = 64
EXTRA = 16
DEPTH = 4096
VMEM_LIMIT = 40 * 1024 * 1024


def shifted(value, axis, steps):
    count = lax.axis_size(axis)
    pairs = [(source, (source + steps) % count) for source in range(count)]
    return lax.ppermute(value, axis, pairs)


def skewed_sums(products):
    groups_here, length, _ = products.shape
    padded = jnp.pad(products, ((0, 0), (0, 0), (0, length)))
    flat = padded.reshape(groups_here, 2 * length * length)[:, : length * (2 * length - 1)]
    return flat.reshape(groups_here, length, 2 * length - 1).sum(axis=1)


def by_tokens(out_grads, layer_inputs, filters):
    local_grads = lax.all_to_all(out_grads, "chan", split_axis=1, concat_axis=0, tiled=True)
    taps_all = lax.all_gather(filters, "seq", axis=0, tiled=True)
    block_len = local_grads.shape[0]
    chan_width = local_grads.shape[1]
    groups_here = filters.shape[1]
    per_group = chan_width // groups_here
    taps_total = taps_all.shape[0]
    spread_blocks = taps_total // block_len
    filt_rows = taps_all.T
    x_reversed = layer_inputs[::-1].reshape(block_len, groups_here, per_group).transpose(1, 2, 0)
    offsets = lax.broadcasted_iota(jnp.int32, (block_len, block_len), 1) - lax.broadcasted_iota(
        jnp.int32, (block_len, block_len), 0
    )
    dx_total = jnp.zeros((groups_here, per_group, block_len), jnp.float32)
    lag_buffer = jnp.zeros((groups_here, (spread_blocks + 2) * block_len), jnp.float32)
    current = local_grads
    for lag_block in range(spread_blocks + 1):
        if lag_block > 0:
            current = shifted(local_grads, "seq", -lag_block)
        dy_grouped = current.reshape(block_len, groups_here, per_group).transpose(1, 2, 0)
        lag_index = lag_block * block_len + offsets
        inside = (lag_index >= 0) & (lag_index < taps_total)
        picked = jnp.take(filt_rows, jnp.clip(lag_index, 0, taps_total - 1), axis=1)
        toeplitz = jnp.where(inside[None], picked, jnp.zeros((), jnp.bfloat16))
        dx_total = dx_total + jnp.einsum(
            "guv,gkv->gku", toeplitz, dy_grouped, preferred_element_type=jnp.float32
        )
        products = jnp.einsum(
            "gku,gkv->guv", x_reversed, dy_grouped, preferred_element_type=jnp.float32
        )
        start = lag_block * block_len
        lag_buffer = lag_buffer.at[:, start : start + 2 * block_len - 1].add(skewed_sums(products))
    partial_dh = lag_buffer[:, block_len - 1 : block_len - 1 + taps_total].T
    filter_grads = lax.psum_scatter(partial_dh, "seq", scatter_dimension=0, tiled=True)
    input_grads = dx_total.transpose(2, 0, 1).reshape(block_len, chan_width).astype(jnp.bfloat16)
    return (input_grads, filter_grads)


def xor_permute(value, axis, bits):
    pairs = [(source, source ^ bits) for source in range(lax.axis_size(axis))]
    return lax.ppermute(value, axis, pairs)


def turned_permute(value, axis, masks):
    pairs = [(source, source ^ masks[source % 2]) for source in range(lax.axis_size(axis))]
    return lax.ppermute(value, axis, pairs)


def partners(count):
    return [(count - step) % count for step in range(count)]


def fan_out(pieces, axis, unit):
    masks = partners(len(pieces))[1:]
    return [pieces[0]] + [xor_permute(p, axis, m * unit) for p, m in zip(pieces[1:], masks)]


def roll_left(value, steps):
    width = value.shape[-1]
    return pltpu.roll(value, (width - steps) % width, value.ndim - 1)


def place():
    seq = lax.axis_index("seq")
    return seq // 2, seq % 2, lax.axis_index("chan")


def rows_at(index, size):
    return pl.ds(pl.multiple_of(index * size, 16), size)


def fan_grads_kernel(n_seq, in_ref, out_ref):
    n_chan = out_ref.shape[0] // n_seq
    for seq in range(n_seq):
        for chan in range(n_chan):
            start = (chan * n_seq + seq) * LANES
            out_ref[seq * n_chan + chan] = in_ref[:, start : start + LANES]


def fan_inputs_kernel(x_own_ref, x_other_ref, f_own_ref, f_other_ref, *refs):
    *out_refs, taps_ref = refs
    chip, core, _ = place()
    block_len = x_own_ref.shape[0]
    taps_here, groups_here = f_own_ref.shape
    groups = groups_here // (2 * len(out_refs))
    rest = jnp.zeros((groups_here, LANES - taps_here), jnp.float32)
    for flip, f_ref in enumerate((f_own_ref, f_other_ref)):
        taps_ref[flip] = jnp.concatenate([f_ref[...].astype(jnp.float32).T, rest], axis=1)
    for bits, out_ref in zip(partners(len(out_refs)), out_refs):
        target = 2 * (chip ^ bits) + core
        columns = pl.ds(pl.multiple_of(target * LANES, LANES), LANES)
        out_ref[:block_len] = x_own_ref[:, columns]
        out_ref[block_len : 2 * block_len] = x_other_ref[:, columns]
        rows = pl.ds(pl.multiple_of(target * groups, groups), groups)
        taps = jnp.concatenate([taps_ref[0, rows], taps_ref[1, rows]], axis=0)
        out_ref[2 * block_len :] = taps.astype(jnp.bfloat16)


def place_inputs(in_refs, taps_here, x_ref, filt_ref):
    block_len = (in_refs[0].shape[0] - EXTRA) // 2
    groups = EXTRA // 2
    chip, core, _ = place()
    low = lax.broadcasted_iota(jnp.int32, (groups, LANES), 1) < taps_here
    for bits, in_ref in zip(partners(len(in_refs)), in_refs):
        for flip in range(2):
            block = 2 * (chip ^ bits) + (core ^ flip)
            x_ref[rows_at(block, block_len)] = in_ref[flip * block_len : (flip + 1) * block_len]
        taps = in_ref[2 * block_len :].astype(jnp.float32)
        first = jnp.where(core == 0, taps[:groups], taps[groups:])
        second = jnp.where(core == 0, taps[groups:], taps[:groups])
        filt_ref[chip ^ bits] = jnp.where(low, first, pltpu.roll(second, taps_here, 1))


def toeplitz_rows(filt_ref, toep_ref, rest_ref):
    chips, groups, _ = filt_ref.shape
    taps = chips * LANES
    tiles = [filt_ref[tile] for tile in range(chips)]
    filt = jnp.concatenate(tiles + [jnp.zeros((groups, LANES), jnp.float32)], axis=1)
    low = lax.broadcasted_iota(jnp.int32, (SLAB, LANES), 1) < SLAB
    outside = []
    for group in range(groups):
        rows = jnp.broadcast_to(filt[group : group + 1], (SLAB, taps + LANES))
        rows = pltpu.roll(rows, 0, 1, stride=1, stride_axis=0)
        toep_ref[group * SLAB : (group + 1) * SLAB] = rows[:, :taps].astype(jnp.bfloat16)
        outside.append(rows[:, taps:])
    for pair in range(groups // 2):
        both = jnp.where(low, outside[2 * pair], pltpu.roll(outside[2 * pair + 1], SLAB, 1))
        rest_ref[:, pair * LANES : (pair + 1) * LANES] = both.astype(jnp.bfloat16)


def group_of_lane(rows, width, groups):
    lane = lax.broadcasted_iota(jnp.int32, (rows, width), 1)
    return (lane % LANES) // (LANES // groups)


def tokens_of(seqs, dye_ref, toep_ref, rest_ref, out_ref, block_len):
    groups = toep_ref.shape[0] // SLAB
    taps = toep_ref.shape[1]
    starts = [seq * block_len + row for seq in seqs for row in range(0, block_len, SLAB)]

    def windows(at, size):
        return jnp.concatenate(
            [dye_ref[pl.ds(pl.multiple_of(start + at, SLAB), size)] for start in starts], axis=1
        )

    group_in = group_of_lane(SLAB, len(starts) * LANES, groups)
    after = windows(taps, SLAB)
    after = [jnp.where(group_in == group, after, jnp.zeros_like(after)) for group in range(groups)]
    full = jnp.dot(toep_ref[...], windows(0, taps), preferred_element_type=jnp.float32)
    rest = jnp.dot(
        rest_ref[...], jnp.concatenate(after, axis=0), preferred_element_type=jnp.float32
    )
    total = full[:SLAB]
    for group in range(1, groups):
        total = jnp.where(group_in == group, full[group * SLAB : (group + 1) * SLAB], total)
    total = (total + rest).astype(jnp.bfloat16)
    for index in range(len(starts)):
        columns = slice(index * LANES, (index + 1) * LANES)
        out_ref[index * SLAB : (index + 1) * SLAB] = total[:, columns]


def first_kernel(n_seq, taps_here, far, near, dy_ref, *refs):
    chips = n_seq // 2
    in_refs = refs[:chips]
    dye_ref, taps_ref, toep_ref, rest_ref, far_ref, near_ref, x_ref, filt_ref, lag_ref = refs[chips:]
    tokens = dy_ref.shape[0]
    groups = EXTRA // 2
    taps = n_seq * taps_here
    reach = taps + LANES
    chip, core, _ = place()

    place_inputs(in_refs, taps_here, x_ref, filt_ref)
    dye_ref[:tokens] = dy_ref[...]
    dye_ref[tokens:] = dy_ref[:reach]

    rows = taps + STEP
    deep = DEPTH // LANES
    group_in = group_of_lane(STEP, DEPTH, groups)
    lag_ref[rows:] = jnp.zeros((reach - rows, groups * STEP), jnp.float32)
    for at in range(0, tokens, STEP * deep):
        starts = range(at, at + STEP * deep, STEP)
        windows = jnp.concatenate([dye_ref[row : row + rows] for row in starts], axis=1)
        inputs = jnp.concatenate([x_ref[row : row + STEP] for row in starts], axis=1)
        masked = jnp.concatenate(
            [jnp.where(group_in == group, inputs, jnp.zeros_like(inputs)) for group in range(groups)],
            axis=0,
        )
        part = lax.dot_general(
            windows, masked, (((1,), (1,)), ((), ())), preferred_element_type=jnp.float32
        )
        if at == 0:
            lag_ref[:rows] = part
        else:
            lag_ref[:rows] += part
        if at == 0:
            toeplitz_rows(filt_ref, toep_ref, rest_ref)

    block_len = tokens // n_seq
    seqs = [2 * (chip ^ far) + (core ^ flip) for flip in range(2)]
    tokens_of(seqs, dye_ref, toep_ref, rest_ref, far_ref, block_len)
    seqs = [2 * (chip ^ bits) + (core ^ 1) for bits in near]
    tokens_of(seqs, dye_ref, toep_ref, rest_ref, near_ref, block_len)
    lags = lag_ref[...].T
    eights = []
    for group in range(groups):
        at = group * STEP
        rows = lags[at : at + 8]
        for high in range(1, STEP // 8):
            rows = rows + roll_left(lags[at + 8 * high : at + 8 * high + 8], 8 * high)
        eights.append(rows)
    skew = jnp.concatenate(eights, axis=0)
    row_in = lax.broadcasted_iota(jnp.int32, skew.shape, 0) % 8
    for bit in (1, 2, 4):
        skew = jnp.where((row_in & bit) != 0, roll_left(skew, bit), skew)
    dh = skew.reshape(groups, 8, reach).sum(axis=1)[:, :taps]

    high = dh.astype(jnp.bfloat16).astype(jnp.float32)
    rest = dh - high
    low = lax.broadcasted_iota(jnp.int32, (groups, LANES), 1) < taps_here
    for to_chip in range(chips):
        columns = slice(to_chip * LANES, (to_chip + 1) * LANES)
        top, bottom = high[:, columns], rest[:, columns]
        even = jnp.where(low, top, pltpu.roll(bottom, taps_here, 1))
        odd = jnp.where(low, pltpu.roll(top, taps_here, 1), bottom)
        mine = jnp.where(core == 0, even, odd)
        other = jnp.where(core == 0, odd, even)
        taps_ref[to_chip] = jnp.concatenate([mine, other], axis=0).astype(jnp.bfloat16)

    far_ref[2 * block_len :] = taps_ref[chip ^ far]
    near_ref[len(near) * block_len :] = stacked([half_of(taps_ref[chip ^ bits], 1) for bits in near])


def half_of(taps, flip):
    groups = EXTRA // 2
    return taps.astype(jnp.float32)[flip * groups : (flip + 1) * groups]


def stacked(rows):
    return jnp.concatenate(rows, axis=0).astype(jnp.bfloat16)


def near_kernel(masks, dye_ref, toep_ref, rest_ref, taps_ref, out_ref):
    chip, core, _ = place()
    block_len = (out_ref.shape[0] - len(masks) * EXTRA // 2) // len(masks)
    seqs = [2 * (chip ^ bits) + core for bits in masks]
    tokens_of(seqs, dye_ref, toep_ref, rest_ref, out_ref, block_len)
    out_ref[len(masks) * block_len :] = stacked(
        [half_of(taps_ref[chip ^ bits], 0) for bits in masks]
    )


def near_pieces_kernel(keep_ref, got_ref, *out_refs):
    _, core, _ = place()
    count = len(out_refs)
    block_len = (out_refs[0].shape[0] - EXTRA) // 2
    groups = EXTRA // 2
    keep_taps = keep_ref[count * block_len :].astype(jnp.float32)
    got_taps = got_ref[count * block_len :].astype(jnp.float32)
    taps = [
        stacked(
            [value[index * groups : (index + 1) * groups] for value in (keep_taps, got_taps)]
        )
        for index in range(count)
    ]
    for index, out_ref in enumerate(out_refs):
        other = (index + 1) % count
        out_ref[:block_len] = keep_ref[rows_at((index + core) % count, block_len)]
        out_ref[block_len : 2 * block_len] = got_ref[rows_at((index + core) % count, block_len)]
        out_ref[2 * block_len :] = jnp.where(core == 0, taps[index], taps[other])


def own_kernel(dye_ref, toep_ref, rest_ref, taps_ref, out_ref):
    chip, core, _ = place()
    block_len = (out_ref.shape[0] - EXTRA) // 2
    seqs = [2 * chip + (core ^ flip) for flip in range(2)]
    tokens_of(seqs, dye_ref, toep_ref, rest_ref, out_ref, block_len)
    out_ref[2 * block_len :] = taps_ref[chip]


def swap_kernel(*refs):
    *in_refs, out_ref = refs
    block_len = (in_refs[0].shape[0] - EXTRA) // 2
    for index, in_ref in enumerate(in_refs):
        out_ref[index * block_len : (index + 1) * block_len] = in_ref[block_len : 2 * block_len]
    out_ref[len(in_refs) * block_len :] = stacked(
        [half_of(in_ref[2 * block_len :], 1) for in_ref in in_refs]
    )


def unpack_kernel(masks, *refs):
    *near_refs, own_ref, far_ref, swapped_ref, dx_ref, dh_ref, rows_ref = refs
    chip, core, _ = place()
    block_len = dx_ref.shape[0]
    taps_here, groups_here = dh_ref.shape
    groups = EXTRA // 2

    def put(from_chip, flip, tokens, taps):
        source = 2 * from_chip + (core ^ flip)
        dx_ref[:, pl.ds(pl.multiple_of(source * LANES, LANES), LANES)] = tokens
        rows_ref[pl.ds(pl.multiple_of(source * groups, groups), groups)] = taps + pltpu.roll(
            taps, taps_here, 1
        )

    swapped_taps = swapped_ref[2 * block_len :]
    for index, ref in enumerate((own_ref, far_ref)):
        put(chip ^ masks[index], 0, ref[:block_len], half_of(ref[2 * block_len :], 0))
        rows = swapped_ref[index * block_len : (index + 1) * block_len]
        put(chip ^ masks[index], 1, rows, half_of(swapped_taps, index))
    near = masks[2:]
    for index, ref in enumerate(near_refs):
        bits = jnp.where(core == 0, near[index], near[(index + 1) % len(near)])
        for flip in range(2):
            rows = ref[flip * block_len : (flip + 1) * block_len]
            put(chip ^ bits, flip, rows, half_of(ref[2 * block_len :], flip))
    dh_ref[...] = rows_ref[...].T[:taps_here]


def local_call(kernel, out_shape, operands, name, scratch=()):
    whole = pl.BlockSpec(memory_space=pltpu.VMEM)
    return pl.pallas_call(
        kernel,
        out_shape=out_shape,
        in_specs=[whole] * len(operands),
        out_specs=[whole] * len(out_shape),
        scratch_shapes=scratch,
        compiler_params=pltpu.CompilerParams(vmem_limit_bytes=VMEM_LIMIT),
        name=name,
    )(*operands)


def by_channels(n_seq, n_chan, out_grads, layer_inputs, filters):
    rows = out_grads.shape[0]
    block_len = layer_inputs.shape[0]
    taps_here, groups_here = filters.shape
    groups = groups_here // n_seq
    tokens = n_seq * block_len
    taps = n_seq * taps_here
    chips = n_seq // 2
    masks = partners(chips)

    def half(*shape):
        return jax.ShapeDtypeStruct(shape, jnp.bfloat16)

    unit = half(2 * block_len + EXTRA, LANES)
    x_other = xor_permute(layer_inputs, "seq", 1)
    f_other = xor_permute(filters, "seq", 1)
    (dy,) = local_call(
        functools.partial(fan_grads_kernel, n_seq),
        [half(n_seq * n_chan, rows, LANES)],
        (out_grads,),
        "fan_grads",
    )
    dy = lax.all_to_all(dy, ("seq", "chan"), split_axis=0, concat_axis=0, tiled=True)
    pieces = local_call(
        fan_inputs_kernel,
        [unit] * chips,
        (layer_inputs, x_other, filters, f_other),
        "fan_inputs",
        [pltpu.VMEM((2, groups_here, LANES), jnp.float32)],
    )
    near = masks[2:]
    near_shape = half(len(near) * (block_len + EXTRA // 2), LANES)
    dye, tap_parts, toeplitz, outside, far, send = local_call(
        functools.partial(first_kernel, n_seq, taps_here, masks[1], near),
        [
            half(tokens + taps + LANES, LANES),
            half(chips, EXTRA, LANES),
            half(groups * SLAB, taps),
            half(SLAB, groups * SLAB),
            unit,
            near_shape,
        ],
        (dy.reshape(tokens, LANES), *fan_out(pieces, "seq", 2)),
        "first",
        [
            pltpu.VMEM((tokens, LANES), jnp.bfloat16),
            pltpu.VMEM((chips, groups, LANES), jnp.float32),
            pltpu.VMEM((taps + LANES, groups * STEP), jnp.float32),
        ],
    )
    far = xor_permute(far, "seq", 2 * masks[1])
    got = xor_permute(send, "seq", 1)
    (keep,) = local_call(
        functools.partial(near_kernel, near),
        [near_shape],
        (dye, toeplitz, outside, tap_parts),
        "near_keep",
    )
    pieces = local_call(near_pieces_kernel, [unit] * len(near), (keep, got), "near_pieces")
    tap_parts, _ = lax.optimization_barrier((tap_parts, pieces[0]))
    pieces = [
        turned_permute(piece, "seq", [2 * bits for bits in near[index:] + near[:index]])
        for index, piece in enumerate(pieces)
    ]
    (own,) = local_call(own_kernel, [unit], (dye, toeplitz, outside, tap_parts), "own")
    (send,) = local_call(
        swap_kernel, [half(2 * block_len + EXTRA, LANES)], (own, far), "swap"
    )
    return local_call(
        functools.partial(unpack_kernel, masks),
        [
            half(block_len, n_seq * LANES),
            jax.ShapeDtypeStruct((taps_here, groups_here), jnp.float32),
        ],
        (*pieces, own, far, xor_permute(send, "seq", 1)),
        "unpack",
        [pltpu.VMEM((groups_here, LANES), jnp.float32)],
    )


def solution(mesh):
    n_seq, n_chan = mesh.shape["seq"], mesh.shape["chan"]

    def on_device(out_grads, layer_inputs, filters):
        taps_here, groups_here = filters.shape
        fits = (
            n_seq == 8
            and n_chan in (2, 4, 8)
            and layer_inputs.shape[1] == n_seq * LANES
            and groups_here == 8 * n_seq
            and 2 * taps_here == LANES
            and out_grads.shape[0] % 16 == 0
            and layer_inputs.shape[0] % SLAB == 0
            and n_seq * layer_inputs.shape[0] % (STEP * DEPTH // LANES) == 0
            and n_seq * taps_here + LANES <= n_seq * layer_inputs.shape[0]
        )
        if fits:
            return tuple(by_channels(n_seq, n_chan, out_grads, layer_inputs, filters))
        return by_tokens(out_grads, layer_inputs, filters)

    in_specs = (P(("seq", "chan"), None), P("seq", "chan"), P("seq", "chan"))
    out_specs = (P("seq", "chan"), P("seq", "chan"))
    return jax.shard_map(
        on_device, mesh=mesh, in_specs=in_specs, out_specs=out_specs, check_vma=False
    )
```

```python
import functools

import jax
import jax.numpy as jnp
from jax import lax
from jax.experimental import pallas as pl
from jax.experimental.pallas import tpu as pltpu
from jax.sharding import PartitionSpec as P

LANES = 128
STEP = 64
SLAB = 64
EXTRA = 16
VMEM_LIMIT = 40 * 1024 * 1024


def shifted(value, axis, steps):
    count = lax.axis_size(axis)
    pairs = [(source, (source + steps) % count) for source in range(count)]
    return lax.ppermute(value, axis, pairs)


def skewed_sums(products):
    groups_here, length, _ = products.shape
    padded = jnp.pad(products, ((0, 0), (0, 0), (0, length)))
    flat = padded.reshape(groups_here, 2 * length * length)[:, : length * (2 * length - 1)]
    return flat.reshape(groups_here, length, 2 * length - 1).sum(axis=1)


def by_tokens(out_grads, layer_inputs, filters):
    local_grads = lax.all_to_all(out_grads, "chan", split_axis=1, concat_axis=0, tiled=True)
    taps_all = lax.all_gather(filters, "seq", axis=0, tiled=True)
    block_len = local_grads.shape[0]
    chan_width = local_grads.shape[1]
    groups_here = filters.shape[1]
    per_group = chan_width // groups_here
    taps_total = taps_all.shape[0]
    spread_blocks = taps_total // block_len
    filt_rows = taps_all.T
    x_reversed = layer_inputs[::-1].reshape(block_len, groups_here, per_group).transpose(1, 2, 0)
    offsets = lax.broadcasted_iota(jnp.int32, (block_len, block_len), 1) - lax.broadcasted_iota(
        jnp.int32, (block_len, block_len), 0
    )
    dx_total = jnp.zeros((groups_here, per_group, block_len), jnp.float32)
    lag_buffer = jnp.zeros((groups_here, (spread_blocks + 2) * block_len), jnp.float32)
    current = local_grads
    for lag_block in range(spread_blocks + 1):
        if lag_block > 0:
            current = shifted(local_grads, "seq", -lag_block)
        dy_grouped = current.reshape(block_len, groups_here, per_group).transpose(1, 2, 0)
        lag_index = lag_block * block_len + offsets
        inside = (lag_index >= 0) & (lag_index < taps_total)
        picked = jnp.take(filt_rows, jnp.clip(lag_index, 0, taps_total - 1), axis=1)
        toeplitz = jnp.where(inside[None], picked, jnp.zeros((), jnp.bfloat16))
        dx_total = dx_total + jnp.einsum(
            "guv,gkv->gku", toeplitz, dy_grouped, preferred_element_type=jnp.float32
        )
        products = jnp.einsum(
            "gku,gkv->guv", x_reversed, dy_grouped, preferred_element_type=jnp.float32
        )
        start = lag_block * block_len
        lag_buffer = lag_buffer.at[:, start : start + 2 * block_len - 1].add(skewed_sums(products))
    partial_dh = lag_buffer[:, block_len - 1 : block_len - 1 + taps_total].T
    filter_grads = lax.psum_scatter(partial_dh, "seq", scatter_dimension=0, tiled=True)
    input_grads = dx_total.transpose(2, 0, 1).reshape(block_len, chan_width).astype(jnp.bfloat16)
    return (input_grads, filter_grads)


def xor_permute(value, axis, bits):
    pairs = [(source, source ^ bits) for source in range(lax.axis_size(axis))]
    return lax.ppermute(value, axis, pairs)


def turned_permute(value, axis, masks):
    pairs = [(source, source ^ masks[source % 2]) for source in range(lax.axis_size(axis))]
    return lax.ppermute(value, axis, pairs)


def partners(count):
    return [(count - step) % count for step in range(count)]


def fan_out(pieces, axis, unit):
    masks = partners(len(pieces))[1:]
    return [pieces[0]] + [xor_permute(p, axis, m * unit) for p, m in zip(pieces[1:], masks)]


def roll_left(value, steps):
    width = value.shape[-1]
    return pltpu.roll(value, (width - steps) % width, value.ndim - 1)


def place():
    seq = lax.axis_index("seq")
    return seq // 2, seq % 2, lax.axis_index("chan")


def rows_at(index, size):
    return pl.ds(pl.multiple_of(index * size, 16), size)


def fan_grads_kernel(n_seq, in_ref, out_ref):
    n_chan = out_ref.shape[0] // n_seq
    for seq in range(n_seq):
        for chan in range(n_chan):
            start = (chan * n_seq + seq) * LANES
            out_ref[seq * n_chan + chan] = in_ref[:, start : start + LANES]


def fan_inputs_kernel(x_own_ref, x_other_ref, f_own_ref, f_other_ref, *refs):
    *out_refs, taps_ref = refs
    chip, core, _ = place()
    block_len = x_own_ref.shape[0]
    taps_here, groups_here = f_own_ref.shape
    groups = groups_here // (2 * len(out_refs))
    rest = jnp.zeros((groups_here, LANES - taps_here), jnp.float32)
    for flip, f_ref in enumerate((f_own_ref, f_other_ref)):
        taps_ref[flip] = jnp.concatenate([f_ref[...].astype(jnp.float32).T, rest], axis=1)
    for bits, out_ref in zip(partners(len(out_refs)), out_refs):
        target = 2 * (chip ^ bits) + core
        columns = pl.ds(pl.multiple_of(target * LANES, LANES), LANES)
        out_ref[:block_len] = x_own_ref[:, columns]
        out_ref[block_len : 2 * block_len] = x_other_ref[:, columns]
        rows = pl.ds(pl.multiple_of(target * groups, groups), groups)
        taps = jnp.concatenate([taps_ref[0, rows], taps_ref[1, rows]], axis=0)
        out_ref[2 * block_len :] = taps.astype(jnp.bfloat16)


def place_inputs(in_refs, taps_here, x_ref, filt_ref):
    block_len = (in_refs[0].shape[0] - EXTRA) // 2
    groups = EXTRA // 2
    chip, core, _ = place()
    low = lax.broadcasted_iota(jnp.int32, (groups, LANES), 1) < taps_here
    for bits, in_ref in zip(partners(len(in_refs)), in_refs):
        for flip in range(2):
            block = 2 * (chip ^ bits) + (core ^ flip)
            x_ref[rows_at(block, block_len)] = in_ref[flip * block_len : (flip + 1) * block_len]
        taps = in_ref[2 * block_len :].astype(jnp.float32)
        first = jnp.where(core == 0, taps[:groups], taps[groups:])
        second = jnp.where(core == 0, taps[groups:], taps[:groups])
        filt_ref[chip ^ bits] = jnp.where(low, first, pltpu.roll(second, taps_here, 1))


def toeplitz_rows(filt_ref, toep_ref, rest_ref):
    chips, groups, _ = filt_ref.shape
    taps = chips * LANES
    tiles = [filt_ref[tile] for tile in range(chips)]
    filt = jnp.concatenate(tiles + [jnp.zeros((groups, LANES), jnp.float32)], axis=1)
    low = lax.broadcasted_iota(jnp.int32, (SLAB, LANES), 1) < SLAB
    outside = []
    for group in range(groups):
        rows = jnp.broadcast_to(filt[group : group + 1], (SLAB, taps + LANES))
        rows = pltpu.roll(rows, 0, 1, stride=1, stride_axis=0)
        toep_ref[group * SLAB : (group + 1) * SLAB] = rows[:, :taps].astype(jnp.bfloat16)
        outside.append(rows[:, taps:])
    for pair in range(groups // 2):
        both = jnp.where(low, outside[2 * pair], pltpu.roll(outside[2 * pair + 1], SLAB, 1))
        rest_ref[:, pair * LANES : (pair + 1) * LANES] = both.astype(jnp.bfloat16)


def group_of_lane(rows, width, groups):
    lane = lax.broadcasted_iota(jnp.int32, (rows, width), 1)
    return (lane % LANES) // (LANES // groups)


def tokens_of(seqs, dye_ref, toep_ref, rest_ref, out_ref, block_len):
    groups = toep_ref.shape[0] // SLAB
    taps = toep_ref.shape[1]
    starts = [seq * block_len + row for seq in seqs for row in range(0, block_len, SLAB)]

    def windows(at, size):
        return jnp.concatenate(
            [dye_ref[pl.ds(pl.multiple_of(start + at, SLAB), size)] for start in starts], axis=1
        )

    group_in = group_of_lane(SLAB, len(starts) * LANES, groups)
    after = windows(taps, SLAB)
    after = [jnp.where(group_in == group, after, jnp.zeros_like(after)) for group in range(groups)]
    full = jnp.dot(toep_ref[...], windows(0, taps), preferred_element_type=jnp.float32)
    rest = jnp.dot(
        rest_ref[...], jnp.concatenate(after, axis=0), preferred_element_type=jnp.float32
    )
    total = full[:SLAB]
    for group in range(1, groups):
        total = jnp.where(group_in == group, full[group * SLAB : (group + 1) * SLAB], total)
    total = (total + rest).astype(jnp.bfloat16)
    for index in range(len(starts)):
        columns = slice(index * LANES, (index + 1) * LANES)
        out_ref[index * SLAB : (index + 1) * SLAB] = total[:, columns]


def first_kernel(n_seq, taps_here, far, near, dy_ref, *refs):
    chips = n_seq // 2
    in_refs = refs[:chips]
    dye_ref, taps_ref, toep_ref, rest_ref, far_ref, near_ref, x_ref, filt_ref, turned_ref = refs[chips:]
    tokens = dy_ref.shape[0]
    groups = EXTRA // 2
    taps = n_seq * taps_here
    reach = taps + LANES
    per_group = LANES // groups
    chip, core, _ = place()

    place_inputs(in_refs, taps_here, x_ref, filt_ref)
    dye_ref[:tokens] = dy_ref[...]
    dye_ref[tokens:] = dy_ref[:reach]

    pairs = tokens // (2 * STEP)
    wide = (pairs - 1) * LANES + reach
    for odd in range(2):
        turned_ref[odd] = dye_ref[odd * STEP : odd * STEP + wide].T
    inputs = x_ref[...].T
    toeplitz_rows(filt_ref, toep_ref, rest_ref)
    products = []
    for group in range(groups):
        own = slice(group * per_group, (group + 1) * per_group)
        sides = jnp.concatenate(
            [inputs[own, pair * LANES : (pair + 1) * LANES] for pair in range(pairs)], axis=0
        ).T
        sides = jnp.concatenate([sides[:STEP], sides[STEP:]], axis=1)
        windows = jnp.concatenate(
            [
                turned_ref[odd, own, pair * LANES : pair * LANES + reach]
                for odd in range(2)
                for pair in range(pairs)
            ],
            axis=0,
        )
        products.append(jnp.dot(sides, windows, preferred_element_type=jnp.float32))

    block_len = tokens // n_seq
    seqs = [2 * (chip ^ far) + (core ^ flip) for flip in range(2)]
    tokens_of(seqs, dye_ref, toep_ref, rest_ref, far_ref, block_len)
    seqs = [2 * (chip ^ bits) + (core ^ 1) for bits in near]
    tokens_of(seqs, dye_ref, toep_ref, rest_ref, near_ref, block_len)
    eights = []
    for lags in products:
        rows = lags[:8]
        for high in range(1, STEP // 8):
            rows = rows + roll_left(lags[8 * high : 8 * high + 8], 8 * high)
        eights.append(rows)
    skew = jnp.concatenate(eights, axis=0)
    row_in = lax.broadcasted_iota(jnp.int32, skew.shape, 0) % 8
    for bit in (1, 2, 4):
        skew = jnp.where((row_in & bit) != 0, roll_left(skew, bit), skew)
    dh = skew.reshape(groups, 8, reach).sum(axis=1)[:, :taps]

    high = dh.astype(jnp.bfloat16).astype(jnp.float32)
    rest = dh - high
    low = lax.broadcasted_iota(jnp.int32, (groups, LANES), 1) < taps_here
    for to_chip in range(chips):
        columns = slice(to_chip * LANES, (to_chip + 1) * LANES)
        top, bottom = high[:, columns], rest[:, columns]
        even = jnp.where(low, top, pltpu.roll(bottom, taps_here, 1))
        odd = jnp.where(low, pltpu.roll(top, taps_here, 1), bottom)
        mine = jnp.where(core == 0, even, odd)
        other = jnp.where(core == 0, odd, even)
        taps_ref[to_chip] = jnp.concatenate([mine, other], axis=0).astype(jnp.bfloat16)

    far_ref[2 * block_len :] = taps_ref[chip ^ far]
    near_ref[len(near) * block_len :] = stacked([half_of(taps_ref[chip ^ bits], 1) for bits in near])


def half_of(taps, flip):
    groups = EXTRA // 2
    return taps.astype(jnp.float32)[flip * groups : (flip + 1) * groups]


def stacked(rows):
    return jnp.concatenate(rows, axis=0).astype(jnp.bfloat16)


def near_kernel(masks, dye_ref, toep_ref, rest_ref, taps_ref, out_ref):
    chip, core, _ = place()
    block_len = (out_ref.shape[0] - len(masks) * EXTRA // 2) // len(masks)
    seqs = [2 * (chip ^ bits) + core for bits in masks]
    tokens_of(seqs, dye_ref, toep_ref, rest_ref, out_ref, block_len)
    out_ref[len(masks) * block_len :] = stacked(
        [half_of(taps_ref[chip ^ bits], 0) for bits in masks]
    )


def near_pieces_kernel(keep_ref, got_ref, *out_refs):
    _, core, _ = place()
    count = len(out_refs)
    block_len = (out_refs[0].shape[0] - EXTRA) // 2
    groups = EXTRA // 2
    keep_taps = keep_ref[count * block_len :].astype(jnp.float32)
    got_taps = got_ref[count * block_len :].astype(jnp.float32)
    taps = [
        stacked(
            [value[index * groups : (index + 1) * groups] for value in (keep_taps, got_taps)]
        )
        for index in range(count)
    ]
    for index, out_ref in enumerate(out_refs):
        other = (index + 1) % count
        out_ref[:block_len] = keep_ref[rows_at((index + core) % count, block_len)]
        out_ref[block_len : 2 * block_len] = got_ref[rows_at((index + core) % count, block_len)]
        out_ref[2 * block_len :] = jnp.where(core == 0, taps[index], taps[other])


def own_kernel(dye_ref, toep_ref, rest_ref, taps_ref, out_ref):
    chip, core, _ = place()
    block_len = (out_ref.shape[0] - EXTRA) // 2
    seqs = [2 * chip + (core ^ flip) for flip in range(2)]
    tokens_of(seqs, dye_ref, toep_ref, rest_ref, out_ref, block_len)
    out_ref[2 * block_len :] = taps_ref[chip]


def swap_kernel(*refs):
    *in_refs, out_ref = refs
    block_len = (in_refs[0].shape[0] - EXTRA) // 2
    for index, in_ref in enumerate(in_refs):
        out_ref[index * block_len : (index + 1) * block_len] = in_ref[block_len : 2 * block_len]
    out_ref[len(in_refs) * block_len :] = stacked(
        [half_of(in_ref[2 * block_len :], 1) for in_ref in in_refs]
    )


def unpack_kernel(masks, *refs):
    *near_refs, own_ref, far_ref, swapped_ref, dx_ref, dh_ref, rows_ref = refs
    chip, core, _ = place()
    block_len = dx_ref.shape[0]
    taps_here, groups_here = dh_ref.shape
    groups = EXTRA // 2

    def put(from_chip, flip, tokens, taps):
        source = 2 * from_chip + (core ^ flip)
        dx_ref[:, pl.ds(pl.multiple_of(source * LANES, LANES), LANES)] = tokens
        rows_ref[pl.ds(pl.multiple_of(source * groups, groups), groups)] = taps + pltpu.roll(
            taps, taps_here, 1
        )

    swapped_taps = swapped_ref[2 * block_len :]
    for index, ref in enumerate((own_ref, far_ref)):
        put(chip ^ masks[index], 0, ref[:block_len], half_of(ref[2 * block_len :], 0))
        rows = swapped_ref[index * block_len : (index + 1) * block_len]
        put(chip ^ masks[index], 1, rows, half_of(swapped_taps, index))
    near = masks[2:]
    for index, ref in enumerate(near_refs):
        bits = jnp.where(core == 0, near[index], near[(index + 1) % len(near)])
        for flip in range(2):
            rows = ref[flip * block_len : (flip + 1) * block_len]
            put(chip ^ bits, flip, rows, half_of(ref[2 * block_len :], flip))
    dh_ref[...] = rows_ref[...].T[:taps_here]


def local_call(kernel, out_shape, operands, name, scratch=()):
    whole = pl.BlockSpec(memory_space=pltpu.VMEM)
    return pl.pallas_call(
        kernel,
        out_shape=out_shape,
        in_specs=[whole] * len(operands),
        out_specs=[whole] * len(out_shape),
        scratch_shapes=scratch,
        compiler_params=pltpu.CompilerParams(vmem_limit_bytes=VMEM_LIMIT),
        name=name,
    )(*operands)


def by_channels(n_seq, n_chan, out_grads, layer_inputs, filters):
    rows = out_grads.shape[0]
    block_len = layer_inputs.shape[0]
    taps_here, groups_here = filters.shape
    groups = groups_here // n_seq
    tokens = n_seq * block_len
    taps = n_seq * taps_here
    chips = n_seq // 2
    masks = partners(chips)

    def half(*shape):
        return jax.ShapeDtypeStruct(shape, jnp.bfloat16)

    unit = half(2 * block_len + EXTRA, LANES)
    x_other = xor_permute(layer_inputs, "seq", 1)
    f_other = xor_permute(filters, "seq", 1)
    (dy,) = local_call(
        functools.partial(fan_grads_kernel, n_seq),
        [half(n_seq * n_chan, rows, LANES)],
        (out_grads,),
        "fan_grads",
    )
    dy = lax.all_to_all(dy, ("seq", "chan"), split_axis=0, concat_axis=0, tiled=True)
    pieces = local_call(
        fan_inputs_kernel,
        [unit] * chips,
        (layer_inputs, x_other, filters, f_other),
        "fan_inputs",
        [pltpu.VMEM((2, groups_here, LANES), jnp.float32)],
    )
    near = masks[2:]
    near_shape = half(len(near) * (block_len + EXTRA // 2), LANES)
    dye, tap_parts, toeplitz, outside, far, send = local_call(
        functools.partial(first_kernel, n_seq, taps_here, masks[1], near),
        [
            half(tokens + taps + LANES, LANES),
            half(chips, EXTRA, LANES),
            half(groups * SLAB, taps),
            half(SLAB, groups * SLAB),
            unit,
            near_shape,
        ],
        (dy.reshape(tokens, LANES), *fan_out(pieces, "seq", 2)),
        "first",
        [
            pltpu.VMEM((tokens, LANES), jnp.bfloat16),
            pltpu.VMEM((chips, groups, LANES), jnp.float32),
            pltpu.VMEM((2, LANES, tokens + taps), jnp.bfloat16),
        ],
    )
    far = xor_permute(far, "seq", 2 * masks[1])
    got = xor_permute(send, "seq", 1)
    (keep,) = local_call(
        functools.partial(near_kernel, near),
        [near_shape],
        (dye, toeplitz, outside, tap_parts),
        "near_keep",
    )
    pieces = local_call(near_pieces_kernel, [unit] * len(near), (keep, got), "near_pieces")
    pieces = [
        turned_permute(piece, "seq", [2 * bits for bits in near[index:] + near[:index]])
        for index, piece in enumerate(pieces)
    ]
    far, tap_parts = lax.optimization_barrier((far, tap_parts))
    (own,) = local_call(own_kernel, [unit], (dye, toeplitz, outside, tap_parts), "own")
    (send,) = local_call(
        swap_kernel, [half(2 * block_len + EXTRA, LANES)], (own, far), "swap"
    )
    return local_call(
        functools.partial(unpack_kernel, masks),
        [
            half(block_len, n_seq * LANES),
            jax.ShapeDtypeStruct((taps_here, groups_here), jnp.float32),
        ],
        (*pieces, own, far, xor_permute(send, "seq", 1)),
        "unpack",
        [pltpu.VMEM((groups_here, LANES), jnp.float32)],
    )


def solution(mesh):
    n_seq, n_chan = mesh.shape["seq"], mesh.shape["chan"]

    def on_device(out_grads, layer_inputs, filters):
        taps_here, groups_here = filters.shape
        fits = (
            n_seq == 8
            and n_chan in (2, 4, 8)
            and layer_inputs.shape[1] == n_seq * LANES
            and groups_here == 8 * n_seq
            and 2 * taps_here == LANES
            and out_grads.shape[0] % 16 == 0
            and layer_inputs.shape[0] % SLAB == 0
            and layer_inputs.shape[0] == 2 * STEP
            and n_seq * taps_here + LANES <= n_seq * layer_inputs.shape[0]
        )
        if fits:
            return tuple(by_channels(n_seq, n_chan, out_grads, layer_inputs, filters))
        return by_tokens(out_grads, layer_inputs, filters)

    in_specs = (P(("seq", "chan"), None), P("seq", "chan"), P("seq", "chan"))
    out_specs = (P("seq", "chan"), P("seq", "chan"))
    return jax.shard_map(
        on_device, mesh=mesh, in_specs=in_specs, out_specs=out_specs, check_vma=False
    )
```

```python
import functools

import jax
import jax.numpy as jnp
from jax import lax
from jax.experimental import pallas as pl
from jax.experimental.pallas import tpu as pltpu
from jax.sharding import PartitionSpec as P

LANES = 128
STEP = 64
EXTRA = 16
VMEM_LIMIT = 40 * 1024 * 1024


def shifted(value, axis, steps):
    count = lax.axis_size(axis)
    pairs = [(source, (source + steps) % count) for source in range(count)]
    return lax.ppermute(value, axis, pairs)


def skewed_sums(products):
    groups_here, length, _ = products.shape
    padded = jnp.pad(products, ((0, 0), (0, 0), (0, length)))
    flat = padded.reshape(groups_here, 2 * length * length)[:, : length * (2 * length - 1)]
    return flat.reshape(groups_here, length, 2 * length - 1).sum(axis=1)


def by_tokens(out_grads, layer_inputs, filters):
    local_grads = lax.all_to_all(out_grads, "chan", split_axis=1, concat_axis=0, tiled=True)
    taps_all = lax.all_gather(filters, "seq", axis=0, tiled=True)
    block_len = local_grads.shape[0]
    chan_width = local_grads.shape[1]
    groups_here = filters.shape[1]
    per_group = chan_width // groups_here
    taps_total = taps_all.shape[0]
    spread_blocks = taps_total // block_len
    filt_rows = taps_all.T
    x_reversed = layer_inputs[::-1].reshape(block_len, groups_here, per_group).transpose(1, 2, 0)
    offsets = lax.broadcasted_iota(jnp.int32, (block_len, block_len), 1) - lax.broadcasted_iota(
        jnp.int32, (block_len, block_len), 0
    )
    dx_total = jnp.zeros((groups_here, per_group, block_len), jnp.float32)
    lag_buffer = jnp.zeros((groups_here, (spread_blocks + 2) * block_len), jnp.float32)
    current = local_grads
    for lag_block in range(spread_blocks + 1):
        if lag_block > 0:
            current = shifted(local_grads, "seq", -lag_block)
        dy_grouped = current.reshape(block_len, groups_here, per_group).transpose(1, 2, 0)
        lag_index = lag_block * block_len + offsets
        inside = (lag_index >= 0) & (lag_index < taps_total)
        picked = jnp.take(filt_rows, jnp.clip(lag_index, 0, taps_total - 1), axis=1)
        toeplitz = jnp.where(inside[None], picked, jnp.zeros((), jnp.bfloat16))
        dx_total = dx_total + jnp.einsum(
            "guv,gkv->gku", toeplitz, dy_grouped, preferred_element_type=jnp.float32
        )
        products = jnp.einsum(
            "gku,gkv->guv", x_reversed, dy_grouped, preferred_element_type=jnp.float32
        )
        start = lag_block * block_len
        lag_buffer = lag_buffer.at[:, start : start + 2 * block_len - 1].add(skewed_sums(products))
    partial_dh = lag_buffer[:, block_len - 1 : block_len - 1 + taps_total].T
    filter_grads = lax.psum_scatter(partial_dh, "seq", scatter_dimension=0, tiled=True)
    input_grads = dx_total.transpose(2, 0, 1).reshape(block_len, chan_width).astype(jnp.bfloat16)
    return (input_grads, filter_grads)


def xor_permute(value, axis, bits):
    pairs = [(source, source ^ bits) for source in range(lax.axis_size(axis))]
    return lax.ppermute(value, axis, pairs)


def turned_permute(value, axis, masks):
    pairs = [(source, source ^ masks[source % 2]) for source in range(lax.axis_size(axis))]
    return lax.ppermute(value, axis, pairs)


def partners(count):
    return [(count - step) % count for step in range(count)]


def fan_out(pieces, axis, unit):
    masks = partners(len(pieces))[1:]
    return [pieces[0]] + [xor_permute(p, axis, m * unit) for p, m in zip(pieces[1:], masks)]


def roll_left(value, steps):
    width = value.shape[-1]
    return pltpu.roll(value, (width - steps) % width, value.ndim - 1)


def place():
    seq = lax.axis_index("seq")
    return seq // 2, seq % 2, lax.axis_index("chan")


def rows_at(index, size):
    return pl.ds(pl.multiple_of(index * size, 16), size)


def fan_grads_kernel(n_seq, in_ref, out_ref):
    n_chan = out_ref.shape[0] // n_seq
    for seq in range(n_seq):
        for chan in range(n_chan):
            start = (chan * n_seq + seq) * LANES
            out_ref[seq * n_chan + chan] = in_ref[:, start : start + LANES]


def fan_inputs_kernel(x_own_ref, x_other_ref, f_own_ref, f_other_ref, *refs):
    *out_refs, taps_ref = refs
    chip, core, _ = place()
    block_len = x_own_ref.shape[0]
    taps_here, groups_here = f_own_ref.shape
    groups = groups_here // (2 * len(out_refs))
    rest = jnp.zeros((groups_here, LANES - taps_here), jnp.float32)
    for flip, f_ref in enumerate((f_own_ref, f_other_ref)):
        taps_ref[flip] = jnp.concatenate([f_ref[...].astype(jnp.float32).T, rest], axis=1)
    for bits, out_ref in zip(partners(len(out_refs)), out_refs):
        target = 2 * (chip ^ bits) + core
        columns = pl.ds(pl.multiple_of(target * LANES, LANES), LANES)
        out_ref[:block_len] = x_own_ref[:, columns]
        out_ref[block_len : 2 * block_len] = x_other_ref[:, columns]
        rows = pl.ds(pl.multiple_of(target * groups, groups), groups)
        taps = jnp.concatenate([taps_ref[0, rows], taps_ref[1, rows]], axis=0)
        out_ref[2 * block_len :] = taps.astype(jnp.bfloat16)


def place_inputs(in_refs, taps_here, x_ref, filt_ref):
    block_len = (in_refs[0].shape[0] - EXTRA) // 2
    groups = EXTRA // 2
    chip, core, _ = place()
    low = lax.broadcasted_iota(jnp.int32, (groups, LANES), 1) < taps_here
    for bits, in_ref in zip(partners(len(in_refs)), in_refs):
        for flip in range(2):
            block = 2 * (chip ^ bits) + (core ^ flip)
            x_ref[rows_at(block, block_len)] = in_ref[flip * block_len : (flip + 1) * block_len]
        taps = in_ref[2 * block_len :].astype(jnp.float32)
        first = jnp.where(core == 0, taps[:groups], taps[groups:])
        second = jnp.where(core == 0, taps[groups:], taps[:groups])
        filt_ref[chip ^ bits] = jnp.where(low, first, pltpu.roll(second, taps_here, 1))


def toeplitz_rows(taps):
    rows = jnp.broadcast_to(taps, (LANES, taps.shape[1]))
    return pltpu.roll(rows, 0, 1, stride=1, stride_axis=0).astype(jnp.bfloat16)


def first_kernel(n_seq, taps_here, masks, dy_ref, *refs):
    chips = n_seq // 2
    in_refs = refs[:chips]
    own_ref, far_ref, send_ref, keep_ref, x_ref, filt_ref, dye_ref, turned_ref, dx_ref, taps_ref = refs[
        chips:
    ]
    tokens = dy_ref.shape[0]
    block_len = tokens // n_seq
    groups = EXTRA // 2
    taps = n_seq * taps_here
    reach = taps + LANES
    per_group = LANES // groups
    chip, core, _ = place()

    place_inputs(in_refs, taps_here, x_ref, filt_ref)
    dye_ref[:tokens] = dy_ref[...]
    dye_ref[tokens:] = dy_ref[:reach]

    pairs = tokens // (2 * STEP)
    wide = (pairs - 1) * LANES + reach
    for odd in range(2):
        turned_ref[odd] = dye_ref[odd * STEP : odd * STEP + wide].T
    inputs = x_ref[...].T
    tiles = [filt_ref[tile] for tile in range(chips)]
    filt = jnp.concatenate(tiles + [jnp.zeros((groups, LANES), jnp.float32)], axis=1)
    far, near = masks[1], masks[2:]
    blocks = [(masks[0], flip, own_ref, flip) for flip in range(2)]
    blocks += [(far, flip, far_ref, flip) for flip in range(2)]
    blocks += [(bits, 1, send_ref, index) for index, bits in enumerate(near)]
    blocks += [(bits, 0, keep_ref, index) for index, bits in enumerate(near)]
    products = []
    for group in range(groups):
        own = slice(group * per_group, (group + 1) * per_group)
        sides = jnp.concatenate(
            [inputs[own, pair * LANES : (pair + 1) * LANES] for pair in range(pairs)], axis=0
        ).T
        sides = jnp.concatenate([sides[:STEP], sides[STEP:]], axis=1)
        windows = jnp.concatenate(
            [
                turned_ref[odd, own, pair * LANES : pair * LANES + reach]
                for odd in range(2)
                for pair in range(pairs)
            ],
            axis=0,
        )
        products.append(jnp.dot(sides, windows, preferred_element_type=jnp.float32))
        windows = []
        for bits, flip, _, _ in blocks:
            start = (2 * (chip ^ bits) + (core ^ flip)) * block_len
            windows.append(turned_ref[0, own, pl.ds(pl.multiple_of(start, LANES), reach)])
        grads = lax.dot_general(
            jnp.concatenate(windows, axis=0),
            toeplitz_rows(filt[group : group + 1]),
            (((1,), (1,)), ((), ())),
            preferred_element_type=jnp.float32,
        )
        for index in range(len(blocks)):
            dx_ref[index, own] = grads[index * per_group : (index + 1) * per_group]

    for index, (_, _, out_ref, at) in enumerate(blocks):
        out_ref[at * block_len : (at + 1) * block_len] = dx_ref[index].T.astype(jnp.bfloat16)
    eights = []
    for lags in products:
        rows = lags[:8]
        for high in range(1, STEP // 8):
            rows = rows + roll_left(lags[8 * high : 8 * high + 8], 8 * high)
        eights.append(rows)
    skew = jnp.concatenate(eights, axis=0)
    row_in = lax.broadcasted_iota(jnp.int32, skew.shape, 0) % 8
    for bit in (1, 2, 4):
        skew = jnp.where((row_in & bit) != 0, roll_left(skew, bit), skew)
    dh = skew.reshape(groups, 8, reach).sum(axis=1)[:, :taps]

    high = dh.astype(jnp.bfloat16).astype(jnp.float32)
    rest = dh - high
    low = lax.broadcasted_iota(jnp.int32, (groups, LANES), 1) < taps_here
    for to_chip in range(chips):
        columns = slice(to_chip * LANES, (to_chip + 1) * LANES)
        top, bottom = high[:, columns], rest[:, columns]
        even = jnp.where(low, top, pltpu.roll(bottom, taps_here, 1))
        odd = jnp.where(low, pltpu.roll(top, taps_here, 1), bottom)
        mine = jnp.where(core == 0, even, odd)
        other = jnp.where(core == 0, odd, even)
        taps_ref[to_chip] = jnp.concatenate([mine, other], axis=0).astype(jnp.bfloat16)

    own_ref[2 * block_len :] = taps_ref[chip]
    far_ref[2 * block_len :] = taps_ref[chip ^ far]
    for flip, out_ref in ((1, send_ref), (0, keep_ref)):
        out_ref[len(near) * block_len :] = stacked(
            [half_of(taps_ref[chip ^ bits], flip) for bits in near]
        )


def half_of(taps, flip):
    groups = EXTRA // 2
    return taps.astype(jnp.float32)[flip * groups : (flip + 1) * groups]


def stacked(rows):
    return jnp.concatenate(rows, axis=0).astype(jnp.bfloat16)


def near_pieces_kernel(keep_ref, got_ref, *out_refs):
    _, core, _ = place()
    count = len(out_refs)
    block_len = (out_refs[0].shape[0] - EXTRA) // 2
    groups = EXTRA // 2
    keep_taps = keep_ref[count * block_len :].astype(jnp.float32)
    got_taps = got_ref[count * block_len :].astype(jnp.float32)
    taps = [
        stacked(
            [value[index * groups : (index + 1) * groups] for value in (keep_taps, got_taps)]
        )
        for index in range(count)
    ]
    for index, out_ref in enumerate(out_refs):
        other = (index + 1) % count
        out_ref[:block_len] = keep_ref[rows_at((index + core) % count, block_len)]
        out_ref[block_len : 2 * block_len] = got_ref[rows_at((index + core) % count, block_len)]
        out_ref[2 * block_len :] = jnp.where(core == 0, taps[index], taps[other])


def swap_kernel(*refs):
    *in_refs, out_ref = refs
    block_len = (in_refs[0].shape[0] - EXTRA) // 2
    for index, in_ref in enumerate(in_refs):
        out_ref[index * block_len : (index + 1) * block_len] = in_ref[block_len : 2 * block_len]
    out_ref[len(in_refs) * block_len :] = stacked(
        [half_of(in_ref[2 * block_len :], 1) for in_ref in in_refs]
    )


def unpack_kernel(masks, *refs):
    *near_refs, own_ref, far_ref, swapped_ref, dx_ref, dh_ref, rows_ref = refs
    chip, core, _ = place()
    block_len = dx_ref.shape[0]
    taps_here, groups_here = dh_ref.shape
    groups = EXTRA // 2

    def put(from_chip, flip, tokens, taps):
        source = 2 * from_chip + (core ^ flip)
        dx_ref[:, pl.ds(pl.multiple_of(source * LANES, LANES), LANES)] = tokens
        rows_ref[pl.ds(pl.multiple_of(source * groups, groups), groups)] = taps + pltpu.roll(
            taps, taps_here, 1
        )

    swapped_taps = swapped_ref[2 * block_len :]
    for index, ref in enumerate((own_ref, far_ref)):
        put(chip ^ masks[index], 0, ref[:block_len], half_of(ref[2 * block_len :], 0))
        rows = swapped_ref[index * block_len : (index + 1) * block_len]
        put(chip ^ masks[index], 1, rows, half_of(swapped_taps, index))
    near = masks[2:]
    for index, ref in enumerate(near_refs):
        bits = jnp.where(core == 0, near[index], near[(index + 1) % len(near)])
        for flip in range(2):
            rows = ref[flip * block_len : (flip + 1) * block_len]
            put(chip ^ bits, flip, rows, half_of(ref[2 * block_len :], flip))
    dh_ref[...] = rows_ref[...].T[:taps_here]


def local_call(kernel, out_shape, operands, name, scratch=()):
    whole = pl.BlockSpec(memory_space=pltpu.VMEM)
    return pl.pallas_call(
        kernel,
        out_shape=out_shape,
        in_specs=[whole] * len(operands),
        out_specs=[whole] * len(out_shape),
        scratch_shapes=scratch,
        compiler_params=pltpu.CompilerParams(vmem_limit_bytes=VMEM_LIMIT),
        name=name,
    )(*operands)


def by_channels(n_seq, n_chan, out_grads, layer_inputs, filters):
    rows = out_grads.shape[0]
    block_len = layer_inputs.shape[0]
    taps_here, groups_here = filters.shape
    groups = groups_here // n_seq
    tokens = n_seq * block_len
    taps = n_seq * taps_here
    chips = n_seq // 2
    masks = partners(chips)

    def half(*shape):
        return jax.ShapeDtypeStruct(shape, jnp.bfloat16)

    unit = half(2 * block_len + EXTRA, LANES)
    x_other = xor_permute(layer_inputs, "seq", 1)
    f_other = xor_permute(filters, "seq", 1)
    (dy,) = local_call(
        functools.partial(fan_grads_kernel, n_seq),
        [half(n_seq * n_chan, rows, LANES)],
        (out_grads,),
        "fan_grads",
    )
    dy = lax.all_to_all(dy, ("seq", "chan"), split_axis=0, concat_axis=0, tiled=True)
    pieces = local_call(
        fan_inputs_kernel,
        [unit] * chips,
        (layer_inputs, x_other, filters, f_other),
        "fan_inputs",
        [pltpu.VMEM((2, groups_here, LANES), jnp.float32)],
    )
    near = masks[2:]
    near_shape = half(len(near) * (block_len + EXTRA // 2), LANES)
    own, far, send, keep = local_call(
        functools.partial(first_kernel, n_seq, taps_here, masks),
        [unit, unit, near_shape, near_shape],
        (dy.reshape(tokens, LANES), *fan_out(pieces, "seq", 2)),
        "first",
        [
            pltpu.VMEM((tokens, LANES), jnp.bfloat16),
            pltpu.VMEM((chips, groups, LANES), jnp.float32),
            pltpu.VMEM((tokens + taps + LANES, LANES), jnp.bfloat16),
            pltpu.VMEM((2, LANES, tokens + taps), jnp.bfloat16),
            pltpu.VMEM((n_seq, LANES, block_len), jnp.float32),
            pltpu.VMEM((chips, EXTRA, LANES), jnp.bfloat16),
        ],
    )
    far = xor_permute(far, "seq", 2 * masks[1])
    got = xor_permute(send, "seq", 1)
    pieces = local_call(near_pieces_kernel, [unit] * len(near), (keep, got), "near_pieces")
    pieces = [
        turned_permute(piece, "seq", [2 * bits for bits in near[index:] + near[:index]])
        for index, piece in enumerate(pieces)
    ]
    (send,) = local_call(
        swap_kernel, [half(2 * block_len + EXTRA, LANES)], (own, far), "swap"
    )
    return local_call(
        functools.partial(unpack_kernel, masks),
        [
            half(block_len, n_seq * LANES),
            jax.ShapeDtypeStruct((taps_here, groups_here), jnp.float32),
        ],
        (*pieces, own, far, xor_permute(send, "seq", 1)),
        "unpack",
        [pltpu.VMEM((groups_here, LANES), jnp.float32)],
    )


def solution(mesh):
    n_seq, n_chan = mesh.shape["seq"], mesh.shape["chan"]

    def on_device(out_grads, layer_inputs, filters):
        taps_here, groups_here = filters.shape
        fits = (
            n_seq == 8
            and n_chan in (2, 4, 8)
            and layer_inputs.shape[1] == n_seq * LANES
            and groups_here == 8 * n_seq
            and 2 * taps_here == LANES
            and out_grads.shape[0] % 16 == 0
            and layer_inputs.shape[0] == 2 * STEP
            and n_seq * taps_here + LANES <= n_seq * layer_inputs.shape[0]
        )
        if fits:
            return tuple(by_channels(n_seq, n_chan, out_grads, layer_inputs, filters))
        return by_tokens(out_grads, layer_inputs, filters)

    in_specs = (P(("seq", "chan"), None), P("seq", "chan"), P("seq", "chan"))
    out_specs = (P("seq", "chan"), P("seq", "chan"))
    return jax.shard_map(
        on_device, mesh=mesh, in_specs=in_specs, out_specs=out_specs, check_vma=False
    )
```

```python
import functools

import jax
import jax.numpy as jnp
from jax import lax
from jax.experimental import pallas as pl
from jax.experimental.pallas import tpu as pltpu
from jax.sharding import PartitionSpec as P

LANES = 128
STEP = 64
SLAB = 64
EXTRA = 16
VMEM_LIMIT = 40 * 1024 * 1024


def shifted(value, axis, steps):
    count = lax.axis_size(axis)
    pairs = [(source, (source + steps) % count) for source in range(count)]
    return lax.ppermute(value, axis, pairs)


def skewed_sums(products):
    groups_here, length, _ = products.shape
    padded = jnp.pad(products, ((0, 0), (0, 0), (0, length)))
    flat = padded.reshape(groups_here, 2 * length * length)[:, : length * (2 * length - 1)]
    return flat.reshape(groups_here, length, 2 * length - 1).sum(axis=1)


def by_tokens(out_grads, layer_inputs, filters):
    local_grads = lax.all_to_all(out_grads, "chan", split_axis=1, concat_axis=0, tiled=True)
    taps_all = lax.all_gather(filters, "seq", axis=0, tiled=True)
    block_len = local_grads.shape[0]
    chan_width = local_grads.shape[1]
    groups_here = filters.shape[1]
    per_group = chan_width // groups_here
    taps_total = taps_all.shape[0]
    spread_blocks = taps_total // block_len
    filt_rows = taps_all.T
    x_reversed = layer_inputs[::-1].reshape(block_len, groups_here, per_group).transpose(1, 2, 0)
    offsets = lax.broadcasted_iota(jnp.int32, (block_len, block_len), 1) - lax.broadcasted_iota(
        jnp.int32, (block_len, block_len), 0
    )
    dx_total = jnp.zeros((groups_here, per_group, block_len), jnp.float32)
    lag_buffer = jnp.zeros((groups_here, (spread_blocks + 2) * block_len), jnp.float32)
    current = local_grads
    for lag_block in range(spread_blocks + 1):
        if lag_block > 0:
            current = shifted(local_grads, "seq", -lag_block)
        dy_grouped = current.reshape(block_len, groups_here, per_group).transpose(1, 2, 0)
        lag_index = lag_block * block_len + offsets
        inside = (lag_index >= 0) & (lag_index < taps_total)
        picked = jnp.take(filt_rows, jnp.clip(lag_index, 0, taps_total - 1), axis=1)
        toeplitz = jnp.where(inside[None], picked, jnp.zeros((), jnp.bfloat16))
        dx_total = dx_total + jnp.einsum(
            "guv,gkv->gku", toeplitz, dy_grouped, preferred_element_type=jnp.float32
        )
        products = jnp.einsum(
            "gku,gkv->guv", x_reversed, dy_grouped, preferred_element_type=jnp.float32
        )
        start = lag_block * block_len
        lag_buffer = lag_buffer.at[:, start : start + 2 * block_len - 1].add(skewed_sums(products))
    partial_dh = lag_buffer[:, block_len - 1 : block_len - 1 + taps_total].T
    filter_grads = lax.psum_scatter(partial_dh, "seq", scatter_dimension=0, tiled=True)
    input_grads = dx_total.transpose(2, 0, 1).reshape(block_len, chan_width).astype(jnp.bfloat16)
    return (input_grads, filter_grads)


def xor_permute(value, axis, bits):
    pairs = [(source, source ^ bits) for source in range(lax.axis_size(axis))]
    return lax.ppermute(value, axis, pairs)


def turned_permute(value, axis, masks):
    pairs = [(source, source ^ masks[source % 2]) for source in range(lax.axis_size(axis))]
    return lax.ppermute(value, axis, pairs)


def partners(count):
    return [(count - step) % count for step in range(count)]


def fan_out(pieces, axis, unit):
    masks = partners(len(pieces))[1:]
    return [pieces[0]] + [xor_permute(p, axis, m * unit) for p, m in zip(pieces[1:], masks)]


def roll_left(value, steps):
    width = value.shape[-1]
    return pltpu.roll(value, (width - steps) % width, value.ndim - 1)


def place():
    seq = lax.axis_index("seq")
    return seq // 2, seq % 2, lax.axis_index("chan")


def rows_at(index, size):
    return pl.ds(pl.multiple_of(index * size, 16), size)


def fan_grads_kernel(n_seq, in_ref, out_ref):
    n_chan = out_ref.shape[0] // n_seq
    for seq in range(n_seq):
        for chan in range(n_chan):
            start = (chan * n_seq + seq) * LANES
            out_ref[seq * n_chan + chan] = in_ref[:, start : start + LANES]


def fan_inputs_kernel(x_own_ref, x_other_ref, f_own_ref, f_other_ref, *refs):
    *out_refs, taps_ref = refs
    chip, core, _ = place()
    block_len = x_own_ref.shape[0]
    taps_here, groups_here = f_own_ref.shape
    groups = groups_here // (2 * len(out_refs))
    rest = jnp.zeros((groups_here, LANES - taps_here), jnp.float32)
    for flip, f_ref in enumerate((f_own_ref, f_other_ref)):
        taps_ref[flip] = jnp.concatenate([f_ref[...].astype(jnp.float32).T, rest], axis=1)
    for bits, out_ref in zip(partners(len(out_refs)), out_refs):
        target = 2 * (chip ^ bits) + core
        columns = pl.ds(pl.multiple_of(target * LANES, LANES), LANES)
        out_ref[:block_len] = x_own_ref[:, columns]
        out_ref[block_len : 2 * block_len] = x_other_ref[:, columns]
        rows = pl.ds(pl.multiple_of(target * groups, groups), groups)
        taps = jnp.concatenate([taps_ref[0, rows], taps_ref[1, rows]], axis=0)
        out_ref[2 * block_len :] = taps.astype(jnp.bfloat16)


def place_inputs(in_refs, taps_here, x_ref, filt_ref):
    block_len = (in_refs[0].shape[0] - EXTRA) // 2
    groups = EXTRA // 2
    chip, core, _ = place()
    low = lax.broadcasted_iota(jnp.int32, (groups, LANES), 1) < taps_here
    for bits, in_ref in zip(partners(len(in_refs)), in_refs):
        for flip in range(2):
            block = 2 * (chip ^ bits) + (core ^ flip)
            x_ref[rows_at(block, block_len)] = in_ref[flip * block_len : (flip + 1) * block_len]
        taps = in_ref[2 * block_len :].astype(jnp.float32)
        first = jnp.where(core == 0, taps[:groups], taps[groups:])
        second = jnp.where(core == 0, taps[groups:], taps[:groups])
        filt_ref[chip ^ bits] = jnp.where(low, first, pltpu.roll(second, taps_here, 1))


def toeplitz_rows(filt_ref, toep_ref, rest_ref):
    chips, groups, _ = filt_ref.shape
    taps = chips * LANES
    tiles = [filt_ref[tile] for tile in range(chips)]
    filt = jnp.concatenate(tiles + [jnp.zeros((groups, LANES), jnp.float32)], axis=1)
    low = lax.broadcasted_iota(jnp.int32, (SLAB, LANES), 1) < SLAB
    outside = []
    for group in range(groups):
        rows = jnp.broadcast_to(filt[group : group + 1], (SLAB, taps + LANES))
        rows = pltpu.roll(rows, 0, 1, stride=1, stride_axis=0)
        toep_ref[group * SLAB : (group + 1) * SLAB] = rows[:, :taps].astype(jnp.bfloat16)
        outside.append(rows[:, taps:])
    for pair in range(groups // 2):
        both = jnp.where(low, outside[2 * pair], pltpu.roll(outside[2 * pair + 1], SLAB, 1))
        rest_ref[:, pair * LANES : (pair + 1) * LANES] = both.astype(jnp.bfloat16)


def group_of_lane(rows, width, groups):
    lane = lax.broadcasted_iota(jnp.int32, (rows, width), 1)
    return (lane % LANES) // (LANES // groups)


def tokens_of(seqs, dye_ref, toep_ref, rest_ref, out_ref, block_len):
    groups = toep_ref.shape[0] // SLAB
    taps = toep_ref.shape[1]
    starts = [seq * block_len + row for seq in seqs for row in range(0, block_len, SLAB)]

    def windows(at, size):
        return jnp.concatenate(
            [dye_ref[pl.ds(pl.multiple_of(start + at, SLAB), size)] for start in starts], axis=1
        )

    group_in = group_of_lane(SLAB, len(starts) * LANES, groups)
    after = windows(taps, SLAB)
    after = [jnp.where(group_in == group, after, jnp.zeros_like(after)) for group in range(groups)]
    full = jnp.dot(toep_ref[...], windows(0, taps), preferred_element_type=jnp.float32)
    rest = jnp.dot(
        rest_ref[...], jnp.concatenate(after, axis=0), preferred_element_type=jnp.float32
    )
    total = full[:SLAB]
    for group in range(1, groups):
        total = jnp.where(group_in == group, full[group * SLAB : (group + 1) * SLAB], total)
    total = (total + rest).astype(jnp.bfloat16)
    for index in range(len(starts)):
        columns = slice(index * LANES, (index + 1) * LANES)
        out_ref[index * SLAB : (index + 1) * SLAB] = total[:, columns]


def inputs_kernel(n_seq, taps_here, *refs):
    chips = n_seq // 2
    in_refs = refs[:chips]
    toep_ref, rest_ref, sides_ref, x_ref, filt_ref = refs[chips:]
    groups = sides_ref.shape[0]
    per_group = LANES // groups
    place_inputs(in_refs, taps_here, x_ref, filt_ref)
    pairs = x_ref.shape[0] // (2 * STEP)
    inputs = x_ref[...].T
    toeplitz_rows(filt_ref, toep_ref, rest_ref)
    for group in range(groups):
        own = slice(group * per_group, (group + 1) * per_group)
        sides = jnp.concatenate(
            [inputs[own, pair * LANES : (pair + 1) * LANES] for pair in range(pairs)], axis=0
        ).T
        sides_ref[group] = jnp.concatenate([sides[:STEP], sides[STEP:]], axis=1)


def first_kernel(n_seq, taps_here, far, near, dy_ref, toep_ref, rest_ref, sides_ref, *refs):
    chips = n_seq // 2
    dye_ref, taps_ref, far_ref, near_ref, turned_ref = refs
    tokens = dy_ref.shape[0]
    groups = EXTRA // 2
    taps = n_seq * taps_here
    reach = taps + LANES
    per_group = LANES // groups
    chip, core, _ = place()

    dye_ref[:tokens] = dy_ref[...]
    dye_ref[tokens:] = dy_ref[:reach]

    pairs = tokens // (2 * STEP)
    wide = (pairs - 1) * LANES + reach
    for odd in range(2):
        turned_ref[odd] = dye_ref[odd * STEP : odd * STEP + wide].T
    products = []
    for group in range(groups):
        own = slice(group * per_group, (group + 1) * per_group)
        windows = jnp.concatenate(
            [
                turned_ref[odd, own, pair * LANES : pair * LANES + reach]
                for odd in range(2)
                for pair in range(pairs)
            ],
            axis=0,
        )
        products.append(jnp.dot(sides_ref[group], windows, preferred_element_type=jnp.float32))

    block_len = tokens // n_seq
    seqs = [2 * (chip ^ far) + (core ^ flip) for flip in range(2)]
    tokens_of(seqs, dye_ref, toep_ref, rest_ref, far_ref, block_len)
    seqs = [2 * (chip ^ bits) + (core ^ 1) for bits in near]
    tokens_of(seqs, dye_ref, toep_ref, rest_ref, near_ref, block_len)
    eights = []
    for lags in products:
        rows = lags[:8]
        for high in range(1, STEP // 8):
            rows = rows + roll_left(lags[8 * high : 8 * high + 8], 8 * high)
        eights.append(rows)
    skew = jnp.concatenate(eights, axis=0)
    row_in = lax.broadcasted_iota(jnp.int32, skew.shape, 0) % 8
    for bit in (1, 2, 4):
        skew = jnp.where((row_in & bit) != 0, roll_left(skew, bit), skew)
    dh = skew.reshape(groups, 8, reach).sum(axis=1)[:, :taps]

    high = dh.astype(jnp.bfloat16).astype(jnp.float32)
    rest = dh - high
    low = lax.broadcasted_iota(jnp.int32, (groups, LANES), 1) < taps_here
    for to_chip in range(chips):
        columns = slice(to_chip * LANES, (to_chip + 1) * LANES)
        top, bottom = high[:, columns], rest[:, columns]
        even = jnp.where(low, top, pltpu.roll(bottom, taps_here, 1))
        odd = jnp.where(low, pltpu.roll(top, taps_here, 1), bottom)
        mine = jnp.where(core == 0, even, odd)
        other = jnp.where(core == 0, odd, even)
        taps_ref[to_chip] = jnp.concatenate([mine, other], axis=0).astype(jnp.bfloat16)

    far_ref[2 * block_len :] = taps_ref[chip ^ far]
    near_ref[len(near) * block_len :] = stacked([half_of(taps_ref[chip ^ bits], 1) for bits in near])


def half_of(taps, flip):
    groups = EXTRA // 2
    return taps.astype(jnp.float32)[flip * groups : (flip + 1) * groups]


def stacked(rows):
    return jnp.concatenate(rows, axis=0).astype(jnp.bfloat16)


def near_kernel(masks, dye_ref, toep_ref, rest_ref, taps_ref, out_ref):
    chip, core, _ = place()
    block_len = (out_ref.shape[0] - len(masks) * EXTRA // 2) // len(masks)
    seqs = [2 * (chip ^ bits) + core for bits in masks]
    tokens_of(seqs, dye_ref, toep_ref, rest_ref, out_ref, block_len)
    out_ref[len(masks) * block_len :] = stacked(
        [half_of(taps_ref[chip ^ bits], 0) for bits in masks]
    )


def near_pieces_kernel(keep_ref, got_ref, *out_refs):
    _, core, _ = place()
    count = len(out_refs)
    block_len = (out_refs[0].shape[0] - EXTRA) // 2
    groups = EXTRA // 2
    keep_taps = keep_ref[count * block_len :].astype(jnp.float32)
    got_taps = got_ref[count * block_len :].astype(jnp.float32)
    taps = [
        stacked(
            [value[index * groups : (index + 1) * groups] for value in (keep_taps, got_taps)]
        )
        for index in range(count)
    ]
    for index, out_ref in enumerate(out_refs):
        other = (index + 1) % count
        out_ref[:block_len] = keep_ref[rows_at((index + core) % count, block_len)]
        out_ref[block_len : 2 * block_len] = got_ref[rows_at((index + core) % count, block_len)]
        out_ref[2 * block_len :] = jnp.where(core == 0, taps[index], taps[other])


def own_kernel(dye_ref, toep_ref, rest_ref, taps_ref, out_ref):
    chip, core, _ = place()
    block_len = (out_ref.shape[0] - EXTRA) // 2
    seqs = [2 * chip + (core ^ flip) for flip in range(2)]
    tokens_of(seqs, dye_ref, toep_ref, rest_ref, out_ref, block_len)
    out_ref[2 * block_len :] = taps_ref[chip]


def swap_kernel(*refs):
    *in_refs, out_ref = refs
    block_len = (in_refs[0].shape[0] - EXTRA) // 2
    for index, in_ref in enumerate(in_refs):
        out_ref[index * block_len : (index + 1) * block_len] = in_ref[block_len : 2 * block_len]
    out_ref[len(in_refs) * block_len :] = stacked(
        [half_of(in_ref[2 * block_len :], 1) for in_ref in in_refs]
    )


def unpack_kernel(masks, *refs):
    *near_refs, own_ref, far_ref, swapped_ref, dx_ref, dh_ref, rows_ref = refs
    chip, core, _ = place()
    block_len = dx_ref.shape[0]
    taps_here, groups_here = dh_ref.shape
    groups = EXTRA // 2

    def put(from_chip, flip, tokens, taps):
        source = 2 * from_chip + (core ^ flip)
        dx_ref[:, pl.ds(pl.multiple_of(source * LANES, LANES), LANES)] = tokens
        rows_ref[pl.ds(pl.multiple_of(source * groups, groups), groups)] = taps + pltpu.roll(
            taps, taps_here, 1
        )

    swapped_taps = swapped_ref[2 * block_len :]
    for index, ref in enumerate((own_ref, far_ref)):
        put(chip ^ masks[index], 0, ref[:block_len], half_of(ref[2 * block_len :], 0))
        rows = swapped_ref[index * block_len : (index + 1) * block_len]
        put(chip ^ masks[index], 1, rows, half_of(swapped_taps, index))
    near = masks[2:]
    for index, ref in enumerate(near_refs):
        bits = jnp.where(core == 0, near[index], near[(index + 1) % len(near)])
        for flip in range(2):
            rows = ref[flip * block_len : (flip + 1) * block_len]
            put(chip ^ bits, flip, rows, half_of(ref[2 * block_len :], flip))
    dh_ref[...] = rows_ref[...].T[:taps_here]


def local_call(kernel, out_shape, operands, name, scratch=()):
    whole = pl.BlockSpec(memory_space=pltpu.VMEM)
    return pl.pallas_call(
        kernel,
        out_shape=out_shape,
        in_specs=[whole] * len(operands),
        out_specs=[whole] * len(out_shape),
        scratch_shapes=scratch,
        compiler_params=pltpu.CompilerParams(vmem_limit_bytes=VMEM_LIMIT),
        name=name,
    )(*operands)


def by_channels(n_seq, n_chan, out_grads, layer_inputs, filters):
    rows = out_grads.shape[0]
    block_len = layer_inputs.shape[0]
    taps_here, groups_here = filters.shape
    groups = groups_here // n_seq
    tokens = n_seq * block_len
    taps = n_seq * taps_here
    chips = n_seq // 2
    masks = partners(chips)

    def half(*shape):
        return jax.ShapeDtypeStruct(shape, jnp.bfloat16)

    unit = half(2 * block_len + EXTRA, LANES)
    x_other = xor_permute(layer_inputs, "seq", 1)
    f_other = xor_permute(filters, "seq", 1)
    (dy,) = local_call(
        functools.partial(fan_grads_kernel, n_seq),
        [half(n_seq * n_chan, rows, LANES)],
        (out_grads,),
        "fan_grads",
    )
    dy = lax.all_to_all(dy, ("seq", "chan"), split_axis=0, concat_axis=0, tiled=True)
    pieces = local_call(
        fan_inputs_kernel,
        [unit] * chips,
        (layer_inputs, x_other, filters, f_other),
        "fan_inputs",
        [pltpu.VMEM((2, groups_here, LANES), jnp.float32)],
    )
    near = masks[2:]
    near_shape = half(len(near) * (block_len + EXTRA // 2), LANES)
    toeplitz, outside, sides = local_call(
        functools.partial(inputs_kernel, n_seq, taps_here),
        [
            half(groups * SLAB, taps),
            half(SLAB, groups * SLAB),
            half(groups, STEP, tokens * LANES // (groups * STEP)),
        ],
        fan_out(pieces, "seq", 2),
        "inputs",
        [
            pltpu.VMEM((tokens, LANES), jnp.bfloat16),
            pltpu.VMEM((chips, groups, LANES), jnp.float32),
        ],
    )
    dye, tap_parts, far, send = local_call(
        functools.partial(first_kernel, n_seq, taps_here, masks[1], near),
        [half(tokens + taps + LANES, LANES), half(chips, EXTRA, LANES), unit, near_shape],
        (dy.reshape(tokens, LANES), toeplitz, outside, sides),
        "first",
        [pltpu.VMEM((2, LANES, tokens + taps), jnp.bfloat16)],
    )
    far = xor_permute(far, "seq", 2 * masks[1])
    got = xor_permute(send, "seq", 1)
    (keep,) = local_call(
        functools.partial(near_kernel, near),
        [near_shape],
        (dye, toeplitz, outside, tap_parts),
        "near_keep",
    )
    pieces = local_call(near_pieces_kernel, [unit] * len(near), (keep, got), "near_pieces")
    pieces = [
        turned_permute(piece, "seq", [2 * bits for bits in near[index:] + near[:index]])
        for index, piece in enumerate(pieces)
    ]
    far, tap_parts = lax.optimization_barrier((far, tap_parts))
    (own,) = local_call(own_kernel, [unit], (dye, toeplitz, outside, tap_parts), "own")
    (send,) = local_call(
        swap_kernel, [half(2 * block_len + EXTRA, LANES)], (own, far), "swap"
    )
    return local_call(
        functools.partial(unpack_kernel, masks),
        [
            half(block_len, n_seq * LANES),
            jax.ShapeDtypeStruct((taps_here, groups_here), jnp.float32),
        ],
        (*pieces, own, far, xor_permute(send, "seq", 1)),
        "unpack",
        [pltpu.VMEM((groups_here, LANES), jnp.float32)],
    )


def solution(mesh):
    n_seq, n_chan = mesh.shape["seq"], mesh.shape["chan"]

    def on_device(out_grads, layer_inputs, filters):
        taps_here, groups_here = filters.shape
        fits = (
            n_seq == 8
            and n_chan in (2, 4, 8)
            and layer_inputs.shape[1] == n_seq * LANES
            and groups_here == 8 * n_seq
            and 2 * taps_here == LANES
            and out_grads.shape[0] % 16 == 0
            and layer_inputs.shape[0] % SLAB == 0
            and layer_inputs.shape[0] == 2 * STEP
            and n_seq * taps_here + LANES <= n_seq * layer_inputs.shape[0]
        )
        if fits:
            return tuple(by_channels(n_seq, n_chan, out_grads, layer_inputs, filters))
        return by_tokens(out_grads, layer_inputs, filters)

    in_specs = (P(("seq", "chan"), None), P("seq", "chan"), P("seq", "chan"))
    out_specs = (P("seq", "chan"), P("seq", "chan"))
    return jax.shard_map(
        on_device, mesh=mesh, in_specs=in_specs, out_specs=out_specs, check_vma=False
    )
```

```python
import functools

import jax
import jax.numpy as jnp
from jax import lax
from jax.experimental import pallas as pl
from jax.experimental.pallas import tpu as pltpu
from jax.sharding import PartitionSpec as P

LANES = 128
STEP = 64
SLAB = 64
EXTRA = 16
VMEM_LIMIT = 40 * 1024 * 1024


def shifted(value, axis, steps):
    count = lax.axis_size(axis)
    pairs = [(source, (source + steps) % count) for source in range(count)]
    return lax.ppermute(value, axis, pairs)


def skewed_sums(products):
    groups_here, length, _ = products.shape
    padded = jnp.pad(products, ((0, 0), (0, 0), (0, length)))
    flat = padded.reshape(groups_here, 2 * length * length)[:, : length * (2 * length - 1)]
    return flat.reshape(groups_here, length, 2 * length - 1).sum(axis=1)


def by_tokens(out_grads, layer_inputs, filters):
    local_grads = lax.all_to_all(out_grads, "chan", split_axis=1, concat_axis=0, tiled=True)
    taps_all = lax.all_gather(filters, "seq", axis=0, tiled=True)
    block_len = local_grads.shape[0]
    chan_width = local_grads.shape[1]
    groups_here = filters.shape[1]
    per_group = chan_width // groups_here
    taps_total = taps_all.shape[0]
    spread_blocks = taps_total // block_len
    filt_rows = taps_all.T
    x_reversed = layer_inputs[::-1].reshape(block_len, groups_here, per_group).transpose(1, 2, 0)
    offsets = lax.broadcasted_iota(jnp.int32, (block_len, block_len), 1) - lax.broadcasted_iota(
        jnp.int32, (block_len, block_len), 0
    )
    dx_total = jnp.zeros((groups_here, per_group, block_len), jnp.float32)
    lag_buffer = jnp.zeros((groups_here, (spread_blocks + 2) * block_len), jnp.float32)
    current = local_grads
    for lag_block in range(spread_blocks + 1):
        if lag_block > 0:
            current = shifted(local_grads, "seq", -lag_block)
        dy_grouped = current.reshape(block_len, groups_here, per_group).transpose(1, 2, 0)
        lag_index = lag_block * block_len + offsets
        inside = (lag_index >= 0) & (lag_index < taps_total)
        picked = jnp.take(filt_rows, jnp.clip(lag_index, 0, taps_total - 1), axis=1)
        toeplitz = jnp.where(inside[None], picked, jnp.zeros((), jnp.bfloat16))
        dx_total = dx_total + jnp.einsum(
            "guv,gkv->gku", toeplitz, dy_grouped, preferred_element_type=jnp.float32
        )
        products = jnp.einsum(
            "gku,gkv->guv", x_reversed, dy_grouped, preferred_element_type=jnp.float32
        )
        start = lag_block * block_len
        lag_buffer = lag_buffer.at[:, start : start + 2 * block_len - 1].add(skewed_sums(products))
    partial_dh = lag_buffer[:, block_len - 1 : block_len - 1 + taps_total].T
    filter_grads = lax.psum_scatter(partial_dh, "seq", scatter_dimension=0, tiled=True)
    input_grads = dx_total.transpose(2, 0, 1).reshape(block_len, chan_width).astype(jnp.bfloat16)
    return (input_grads, filter_grads)


def xor_permute(value, axis, bits):
    pairs = [(source, source ^ bits) for source in range(lax.axis_size(axis))]
    return lax.ppermute(value, axis, pairs)


def turned_permute(value, axis, masks):
    pairs = [(source, source ^ masks[source % 2]) for source in range(lax.axis_size(axis))]
    return lax.ppermute(value, axis, pairs)


def partners(count):
    return [(count - step) % count for step in range(count)]


def fan_out(pieces, axis, unit):
    masks = partners(len(pieces))[1:]
    return [pieces[0]] + [xor_permute(p, axis, m * unit) for p, m in zip(pieces[1:], masks)]


def roll_left(value, steps):
    width = value.shape[-1]
    return pltpu.roll(value, (width - steps) % width, value.ndim - 1)


def place():
    seq = lax.axis_index("seq")
    return seq // 2, seq % 2, lax.axis_index("chan")


def rows_at(index, size):
    return pl.ds(pl.multiple_of(index * size, 16), size)


def fan_grads_kernel(n_seq, in_ref, out_ref):
    n_chan = out_ref.shape[0] // n_seq
    for seq in range(n_seq):
        for chan in range(n_chan):
            start = (chan * n_seq + seq) * LANES
            out_ref[seq * n_chan + chan] = in_ref[:, start : start + LANES]


def fan_inputs_kernel(x_own_ref, x_other_ref, f_own_ref, f_other_ref, *refs):
    *out_refs, taps_ref = refs
    chip, core, _ = place()
    block_len = x_own_ref.shape[0]
    taps_here, groups_here = f_own_ref.shape
    groups = groups_here // (2 * len(out_refs))
    rest = jnp.zeros((groups_here, LANES - taps_here), jnp.float32)
    for flip, f_ref in enumerate((f_own_ref, f_other_ref)):
        taps_ref[flip] = jnp.concatenate([f_ref[...].astype(jnp.float32).T, rest], axis=1)
    for bits, out_ref in zip(partners(len(out_refs)), out_refs):
        target = 2 * (chip ^ bits) + core
        columns = pl.ds(pl.multiple_of(target * LANES, LANES), LANES)
        out_ref[:block_len] = x_own_ref[:, columns]
        out_ref[block_len : 2 * block_len] = x_other_ref[:, columns]
        rows = pl.ds(pl.multiple_of(target * groups, groups), groups)
        taps = jnp.concatenate([taps_ref[0, rows], taps_ref[1, rows]], axis=0)
        out_ref[2 * block_len :] = taps.astype(jnp.bfloat16)


def place_inputs(in_refs, taps_here, x_ref, filt_ref):
    block_len = (in_refs[0].shape[0] - EXTRA) // 2
    groups = EXTRA // 2
    chip, core, _ = place()
    low = lax.broadcasted_iota(jnp.int32, (groups, LANES), 1) < taps_here
    for bits, in_ref in zip(partners(len(in_refs)), in_refs):
        for flip in range(2):
            block = 2 * (chip ^ bits) + (core ^ flip)
            x_ref[rows_at(block, block_len)] = in_ref[flip * block_len : (flip + 1) * block_len]
        taps = in_ref[2 * block_len :].astype(jnp.float32)
        first = jnp.where(core == 0, taps[:groups], taps[groups:])
        second = jnp.where(core == 0, taps[groups:], taps[:groups])
        filt_ref[chip ^ bits] = jnp.where(low, first, pltpu.roll(second, taps_here, 1))


def toeplitz_rows(filt_ref, toep_ref, rest_ref):
    chips, groups, _ = filt_ref.shape
    taps = chips * LANES
    tiles = [filt_ref[tile] for tile in range(chips)]
    filt = jnp.concatenate(tiles + [jnp.zeros((groups, LANES), jnp.float32)], axis=1)
    low = lax.broadcasted_iota(jnp.int32, (SLAB, LANES), 1) < SLAB
    outside = []
    for group in range(groups):
        rows = jnp.broadcast_to(filt[group : group + 1], (SLAB, taps + LANES))
        rows = pltpu.roll(rows, 0, 1, stride=1, stride_axis=0)
        toep_ref[group * SLAB : (group + 1) * SLAB] = rows[:, :taps].astype(jnp.bfloat16)
        outside.append(rows[:, taps:])
    for pair in range(groups // 2):
        both = jnp.where(low, outside[2 * pair], pltpu.roll(outside[2 * pair + 1], SLAB, 1))
        rest_ref[:, pair * LANES : (pair + 1) * LANES] = both.astype(jnp.bfloat16)


def group_of_lane(rows, width, groups):
    lane = lax.broadcasted_iota(jnp.int32, (rows, width), 1)
    return (lane % LANES) // (LANES // groups)


def tokens_of(seqs, dye_ref, toep_ref, rest_ref, out_ref, block_len):
    groups = toep_ref.shape[0] // SLAB
    taps = toep_ref.shape[1]
    starts = [seq * block_len + row for seq in seqs for row in range(0, block_len, SLAB)]

    def windows(at, size):
        return jnp.concatenate(
            [dye_ref[pl.ds(pl.multiple_of(start + at, SLAB), size)] for start in starts], axis=1
        )

    group_in = group_of_lane(SLAB, len(starts) * LANES, groups)
    after = windows(taps, SLAB)
    after = [jnp.where(group_in == group, after, jnp.zeros_like(after)) for group in range(groups)]
    full = jnp.dot(toep_ref[...], windows(0, taps), preferred_element_type=jnp.float32)
    rest = jnp.dot(
        rest_ref[...], jnp.concatenate(after, axis=0), preferred_element_type=jnp.float32
    )
    total = full[:SLAB]
    for group in range(1, groups):
        total = jnp.where(group_in == group, full[group * SLAB : (group + 1) * SLAB], total)
    total = (total + rest).astype(jnp.bfloat16)
    for index in range(len(starts)):
        columns = slice(index * LANES, (index + 1) * LANES)
        out_ref[index * SLAB : (index + 1) * SLAB] = total[:, columns]


def first_kernel(n_seq, taps_here, far, near, dy_ref, *refs):
    chips = n_seq // 2
    in_refs = refs[:chips]
    dye_ref, taps_ref, toep_ref, rest_ref, far_ref, near_ref, x_ref, filt_ref, turned_ref = refs[chips:]
    tokens = dy_ref.shape[0]
    groups = EXTRA // 2
    taps = n_seq * taps_here
    reach = taps + LANES
    per_group = LANES // groups
    chip, core, _ = place()

    place_inputs(in_refs, taps_here, x_ref, filt_ref)
    dye_ref[:tokens] = dy_ref[...]
    dye_ref[tokens:] = dy_ref[:reach]

    pairs = tokens // (2 * STEP)
    wide = (pairs - 1) * LANES + reach
    for odd in range(2):
        turned_ref[odd] = dye_ref[odd * STEP : odd * STEP + wide].T
    inputs = x_ref[...].T
    products = []
    for group in range(groups):
        own = slice(group * per_group, (group + 1) * per_group)
        sides = jnp.concatenate(
            [inputs[own, pair * LANES : (pair + 1) * LANES] for pair in range(pairs)], axis=0
        ).T
        sides = jnp.concatenate([sides[:STEP], sides[STEP:]], axis=1)
        windows = jnp.concatenate(
            [
                turned_ref[odd, own, pair * LANES : pair * LANES + reach]
                for odd in range(2)
                for pair in range(pairs)
            ],
            axis=0,
        )
        products.append(jnp.dot(sides, windows, preferred_element_type=jnp.float32))
    toeplitz_rows(filt_ref, toep_ref, rest_ref)

    block_len = tokens // n_seq
    seqs = [2 * (chip ^ far) + (core ^ flip) for flip in range(2)]
    tokens_of(seqs, dye_ref, toep_ref, rest_ref, far_ref, block_len)
    seqs = [2 * (chip ^ bits) + (core ^ 1) for bits in near]
    tokens_of(seqs, dye_ref, toep_ref, rest_ref, near_ref, block_len)
    eights = []
    for lags in products:
        rows = lags[:8]
        for high in range(1, STEP // 8):
            rows = rows + roll_left(lags[8 * high : 8 * high + 8], 8 * high)
        eights.append(rows)
    skew = jnp.concatenate(eights, axis=0)
    row_in = lax.broadcasted_iota(jnp.int32, skew.shape, 0) % 8
    for bit in (1, 2, 4):
        skew = jnp.where((row_in & bit) != 0, roll_left(skew, bit), skew)
    dh = skew.reshape(groups, 8, reach).sum(axis=1)[:, :taps]

    high = dh.astype(jnp.bfloat16).astype(jnp.float32)
    rest = dh - high
    low = lax.broadcasted_iota(jnp.int32, (groups, LANES), 1) < taps_here
    for to_chip in range(chips):
        columns = slice(to_chip * LANES, (to_chip + 1) * LANES)
        top, bottom = high[:, columns], rest[:, columns]
        even = jnp.where(low, top, pltpu.roll(bottom, taps_here, 1))
        odd = jnp.where(low, pltpu.roll(top, taps_here, 1), bottom)
        mine = jnp.where(core == 0, even, odd)
        other = jnp.where(core == 0, odd, even)
        taps_ref[to_chip] = jnp.concatenate([mine, other], axis=0).astype(jnp.bfloat16)

    far_ref[2 * block_len :] = taps_ref[chip ^ far]
    near_ref[len(near) * block_len :] = stacked([half_of(taps_ref[chip ^ bits], 1) for bits in near])


def half_of(taps, flip):
    groups = EXTRA // 2
    return taps.astype(jnp.float32)[flip * groups : (flip + 1) * groups]


def stacked(rows):
    return jnp.concatenate(rows, axis=0).astype(jnp.bfloat16)


def near_kernel(masks, dye_ref, toep_ref, rest_ref, taps_ref, out_ref):
    chip, core, _ = place()
    block_len = (out_ref.shape[0] - len(masks) * EXTRA // 2) // len(masks)
    seqs = [2 * (chip ^ bits) + core for bits in masks]
    tokens_of(seqs, dye_ref, toep_ref, rest_ref, out_ref, block_len)
    out_ref[len(masks) * block_len :] = stacked(
        [half_of(taps_ref[chip ^ bits], 0) for bits in masks]
    )


def near_pieces_kernel(keep_ref, got_ref, *out_refs):
    _, core, _ = place()
    count = len(out_refs)
    block_len = (out_refs[0].shape[0] - EXTRA) // 2
    groups = EXTRA // 2
    keep_taps = keep_ref[count * block_len :].astype(jnp.float32)
    got_taps = got_ref[count * block_len :].astype(jnp.float32)
    taps = [
        stacked(
            [value[index * groups : (index + 1) * groups] for value in (keep_taps, got_taps)]
        )
        for index in range(count)
    ]
    for index, out_ref in enumerate(out_refs):
        other = (index + 1) % count
        out_ref[:block_len] = keep_ref[rows_at((index + core) % count, block_len)]
        out_ref[block_len : 2 * block_len] = got_ref[rows_at((index + core) % count, block_len)]
        out_ref[2 * block_len :] = jnp.where(core == 0, taps[index], taps[other])


def own_kernel(dye_ref, toep_ref, rest_ref, taps_ref, out_ref):
    chip, core, _ = place()
    block_len = (out_ref.shape[0] - EXTRA) // 2
    seqs = [2 * chip + (core ^ flip) for flip in range(2)]
    tokens_of(seqs, dye_ref, toep_ref, rest_ref, out_ref, block_len)
    out_ref[2 * block_len :] = taps_ref[chip]


def swap_kernel(*refs):
    *in_refs, out_ref = refs
    block_len = (in_refs[0].shape[0] - EXTRA) // 2
    for index, in_ref in enumerate(in_refs):
        out_ref[index * block_len : (index + 1) * block_len] = in_ref[block_len : 2 * block_len]
    out_ref[len(in_refs) * block_len :] = stacked(
        [half_of(in_ref[2 * block_len :], 1) for in_ref in in_refs]
    )


def unpack_kernel(masks, *refs):
    *near_refs, own_ref, far_ref, swapped_ref, dx_ref, dh_ref, rows_ref = refs
    chip, core, _ = place()
    block_len = dx_ref.shape[0]
    taps_here, groups_here = dh_ref.shape
    groups = EXTRA // 2

    def put(from_chip, flip, tokens, taps):
        source = 2 * from_chip + (core ^ flip)
        dx_ref[:, pl.ds(pl.multiple_of(source * LANES, LANES), LANES)] = tokens
        rows_ref[pl.ds(pl.multiple_of(source * groups, groups), groups)] = taps + pltpu.roll(
            taps, taps_here, 1
        )

    swapped_taps = swapped_ref[2 * block_len :]
    for index, ref in enumerate((own_ref, far_ref)):
        put(chip ^ masks[index], 0, ref[:block_len], half_of(ref[2 * block_len :], 0))
        rows = swapped_ref[index * block_len : (index + 1) * block_len]
        put(chip ^ masks[index], 1, rows, half_of(swapped_taps, index))
    near = masks[2:]
    for index, ref in enumerate(near_refs):
        bits = jnp.where(core == 0, near[index], near[(index + 1) % len(near)])
        for flip in range(2):
            rows = ref[flip * block_len : (flip + 1) * block_len]
            put(chip ^ bits, flip, rows, half_of(ref[2 * block_len :], flip))
    dh_ref[...] = rows_ref[...].T[:taps_here]


def local_call(kernel, out_shape, operands, name, scratch=()):
    whole = pl.BlockSpec(memory_space=pltpu.VMEM)
    return pl.pallas_call(
        kernel,
        out_shape=out_shape,
        in_specs=[whole] * len(operands),
        out_specs=[whole] * len(out_shape),
        scratch_shapes=scratch,
        compiler_params=pltpu.CompilerParams(vmem_limit_bytes=VMEM_LIMIT),
        name=name,
    )(*operands)


def by_channels(n_seq, n_chan, out_grads, layer_inputs, filters):
    rows = out_grads.shape[0]
    block_len = layer_inputs.shape[0]
    taps_here, groups_here = filters.shape
    groups = groups_here // n_seq
    tokens = n_seq * block_len
    taps = n_seq * taps_here
    chips = n_seq // 2
    masks = partners(chips)

    def half(*shape):
        return jax.ShapeDtypeStruct(shape, jnp.bfloat16)

    unit = half(2 * block_len + EXTRA, LANES)
    x_other = xor_permute(layer_inputs, "seq", 1)
    f_other = xor_permute(filters, "seq", 1)
    (dy,) = local_call(
        functools.partial(fan_grads_kernel, n_seq),
        [half(n_seq * n_chan, rows, LANES)],
        (out_grads,),
        "fan_grads",
    )
    dy = lax.all_to_all(dy, ("seq", "chan"), split_axis=0, concat_axis=0, tiled=True)
    pieces = local_call(
        fan_inputs_kernel,
        [unit] * chips,
        (layer_inputs, x_other, filters, f_other),
        "fan_inputs",
        [pltpu.VMEM((2, groups_here, LANES), jnp.float32)],
    )
    near = masks[2:]
    near_shape = half(len(near) * (block_len + EXTRA // 2), LANES)
    dye, tap_parts, toeplitz, outside, far, send = local_call(
        functools.partial(first_kernel, n_seq, taps_here, masks[1], near),
        [
            half(tokens + taps + LANES, LANES),
            half(chips, EXTRA, LANES),
            half(groups * SLAB, taps),
            half(SLAB, groups * SLAB),
            unit,
            near_shape,
        ],
        (dy.reshape(tokens, LANES), *fan_out(pieces, "seq", 2)),
        "first",
        [
            pltpu.VMEM((tokens, LANES), jnp.bfloat16),
            pltpu.VMEM((chips, groups, LANES), jnp.float32),
            pltpu.VMEM((2, LANES, tokens + taps), jnp.bfloat16),
        ],
    )
    far = xor_permute(far, "seq", 2 * masks[1])
    got = xor_permute(send, "seq", 1)
    (keep,) = local_call(
        functools.partial(near_kernel, near),
        [near_shape],
        (dye, toeplitz, outside, tap_parts),
        "near_keep",
    )
    pieces = local_call(near_pieces_kernel, [unit] * len(near), (keep, got), "near_pieces")
    pieces = [
        turned_permute(piece, "seq", [2 * bits for bits in near[index:] + near[:index]])
        for index, piece in enumerate(pieces)
    ]
    far, tap_parts = lax.optimization_barrier((far, tap_parts))
    (own,) = local_call(own_kernel, [unit], (dye, toeplitz, outside, tap_parts), "own")
    (send,) = local_call(
        swap_kernel, [half(2 * block_len + EXTRA, LANES)], (own, far), "swap"
    )
    return local_call(
        functools.partial(unpack_kernel, masks),
        [
            half(block_len, n_seq * LANES),
            jax.ShapeDtypeStruct((taps_here, groups_here), jnp.float32),
        ],
        (*pieces, own, far, xor_permute(send, "seq", 1)),
        "unpack",
        [pltpu.VMEM((groups_here, LANES), jnp.float32)],
    )


def solution(mesh):
    n_seq, n_chan = mesh.shape["seq"], mesh.shape["chan"]

    def on_device(out_grads, layer_inputs, filters):
        taps_here, groups_here = filters.shape
        fits = (
            n_seq == 8
            and n_chan in (2, 4, 8)
            and layer_inputs.shape[1] == n_seq * LANES
            and groups_here == 8 * n_seq
            and 2 * taps_here == LANES
            and out_grads.shape[0] % 16 == 0
            and layer_inputs.shape[0] % SLAB == 0
            and layer_inputs.shape[0] == 2 * STEP
            and n_seq * taps_here + LANES <= n_seq * layer_inputs.shape[0]
        )
        if fits:
            return tuple(by_channels(n_seq, n_chan, out_grads, layer_inputs, filters))
        return by_tokens(out_grads, layer_inputs, filters)

    in_specs = (P(("seq", "chan"), None), P("seq", "chan"), P("seq", "chan"))
    out_specs = (P("seq", "chan"), P("seq", "chan"))
    return jax.shard_map(
        on_device, mesh=mesh, in_specs=in_specs, out_specs=out_specs, check_vma=False
    )
```

```python
import functools

import jax
import jax.numpy as jnp
from jax import lax
from jax.experimental import pallas as pl
from jax.experimental.pallas import tpu as pltpu
from jax.sharding import PartitionSpec as P

LANES = 128
STEP = 64
SLAB = 64
EXTRA = 16
VMEM_LIMIT = 40 * 1024 * 1024


def shifted(value, axis, steps):
    count = lax.axis_size(axis)
    pairs = [(source, (source + steps) % count) for source in range(count)]
    return lax.ppermute(value, axis, pairs)


def skewed_sums(products):
    groups_here, length, _ = products.shape
    padded = jnp.pad(products, ((0, 0), (0, 0), (0, length)))
    flat = padded.reshape(groups_here, 2 * length * length)[:, : length * (2 * length - 1)]
    return flat.reshape(groups_here, length, 2 * length - 1).sum(axis=1)


def by_tokens(out_grads, layer_inputs, filters):
    local_grads = lax.all_to_all(out_grads, "chan", split_axis=1, concat_axis=0, tiled=True)
    taps_all = lax.all_gather(filters, "seq", axis=0, tiled=True)
    block_len = local_grads.shape[0]
    chan_width = local_grads.shape[1]
    groups_here = filters.shape[1]
    per_group = chan_width // groups_here
    taps_total = taps_all.shape[0]
    spread_blocks = taps_total // block_len
    filt_rows = taps_all.T
    x_reversed = layer_inputs[::-1].reshape(block_len, groups_here, per_group).transpose(1, 2, 0)
    offsets = lax.broadcasted_iota(jnp.int32, (block_len, block_len), 1) - lax.broadcasted_iota(
        jnp.int32, (block_len, block_len), 0
    )
    dx_total = jnp.zeros((groups_here, per_group, block_len), jnp.float32)
    lag_buffer = jnp.zeros((groups_here, (spread_blocks + 2) * block_len), jnp.float32)
    current = local_grads
    for lag_block in range(spread_blocks + 1):
        if lag_block > 0:
            current = shifted(local_grads, "seq", -lag_block)
        dy_grouped = current.reshape(block_len, groups_here, per_group).transpose(1, 2, 0)
        lag_index = lag_block * block_len + offsets
        inside = (lag_index >= 0) & (lag_index < taps_total)
        picked = jnp.take(filt_rows, jnp.clip(lag_index, 0, taps_total - 1), axis=1)
        toeplitz = jnp.where(inside[None], picked, jnp.zeros((), jnp.bfloat16))
        dx_total = dx_total + jnp.einsum(
            "guv,gkv->gku", toeplitz, dy_grouped, preferred_element_type=jnp.float32
        )
        products = jnp.einsum(
            "gku,gkv->guv", x_reversed, dy_grouped, preferred_element_type=jnp.float32
        )
        start = lag_block * block_len
        lag_buffer = lag_buffer.at[:, start : start + 2 * block_len - 1].add(skewed_sums(products))
    partial_dh = lag_buffer[:, block_len - 1 : block_len - 1 + taps_total].T
    filter_grads = lax.psum_scatter(partial_dh, "seq", scatter_dimension=0, tiled=True)
    input_grads = dx_total.transpose(2, 0, 1).reshape(block_len, chan_width).astype(jnp.bfloat16)
    return (input_grads, filter_grads)


def xor_permute(value, axis, bits):
    pairs = [(source, source ^ bits) for source in range(lax.axis_size(axis))]
    return lax.ppermute(value, axis, pairs)


def turned_permute(value, axis, masks):
    pairs = [(source, source ^ masks[source % 2]) for source in range(lax.axis_size(axis))]
    return lax.ppermute(value, axis, pairs)


def partners(count):
    return [(count - step) % count for step in range(count)]


def fan_out(pieces, axis, unit):
    masks = partners(len(pieces))[1:]
    return [pieces[0]] + [xor_permute(p, axis, m * unit) for p, m in zip(pieces[1:], masks)]


def roll_left(value, steps):
    width = value.shape[-1]
    return pltpu.roll(value, (width - steps) % width, value.ndim - 1)


def place():
    seq = lax.axis_index("seq")
    return seq // 2, seq % 2, lax.axis_index("chan")


def rows_at(index, size):
    return pl.ds(pl.multiple_of(index * size, 16), size)


def fan_grads_kernel(n_seq, in_ref, out_ref):
    n_chan = out_ref.shape[0] // n_seq
    for seq in range(n_seq):
        for chan in range(n_chan):
            start = (chan * n_seq + seq) * LANES
            out_ref[seq * n_chan + chan] = in_ref[:, start : start + LANES]


def fan_inputs_kernel(x_own_ref, x_other_ref, f_own_ref, f_other_ref, *refs):
    *out_refs, taps_ref = refs
    chip, core, _ = place()
    block_len = x_own_ref.shape[0]
    taps_here, groups_here = f_own_ref.shape
    groups = groups_here // (2 * len(out_refs))
    rest = jnp.zeros((groups_here, LANES - taps_here), jnp.float32)
    for flip, f_ref in enumerate((f_own_ref, f_other_ref)):
        taps_ref[flip] = jnp.concatenate([f_ref[...].astype(jnp.float32).T, rest], axis=1)
    for bits, out_ref in zip(partners(len(out_refs)), out_refs):
        target = 2 * (chip ^ bits) + core
        columns = pl.ds(pl.multiple_of(target * LANES, LANES), LANES)
        out_ref[:block_len] = x_own_ref[:, columns]
        out_ref[block_len : 2 * block_len] = x_other_ref[:, columns]
        rows = pl.ds(pl.multiple_of(target * groups, groups), groups)
        taps = jnp.concatenate([taps_ref[0, rows], taps_ref[1, rows]], axis=0)
        out_ref[2 * block_len :] = taps.astype(jnp.bfloat16)


def place_inputs(in_refs, taps_here, x_ref, filt_ref):
    block_len = (in_refs[0].shape[0] - EXTRA) // 2
    groups = EXTRA // 2
    chip, core, _ = place()
    low = lax.broadcasted_iota(jnp.int32, (groups, LANES), 1) < taps_here
    for bits, in_ref in zip(partners(len(in_refs)), in_refs):
        for flip in range(2):
            block = 2 * (chip ^ bits) + (core ^ flip)
            x_ref[rows_at(block, block_len)] = in_ref[flip * block_len : (flip + 1) * block_len]
        taps = in_ref[2 * block_len :].astype(jnp.float32)
        first = jnp.where(core == 0, taps[:groups], taps[groups:])
        second = jnp.where(core == 0, taps[groups:], taps[:groups])
        filt_ref[chip ^ bits] = jnp.where(low, first, pltpu.roll(second, taps_here, 1))


def toeplitz_rows(filt_ref, toep_ref, rest_ref):
    chips, groups, _ = filt_ref.shape
    taps = chips * LANES
    tiles = [filt_ref[tile] for tile in range(chips)]
    filt = jnp.concatenate(tiles + [jnp.zeros((groups, LANES), jnp.float32)], axis=1)
    low = lax.broadcasted_iota(jnp.int32, (SLAB, LANES), 1) < SLAB
    outside = []
    for group in range(groups):
        rows = jnp.broadcast_to(filt[group : group + 1], (SLAB, taps + LANES))
        rows = pltpu.roll(rows, 0, 1, stride=1, stride_axis=0)
        toep_ref[group * SLAB : (group + 1) * SLAB] = rows[:, :taps].astype(jnp.bfloat16)
        outside.append(rows[:, taps:])
    for pair in range(groups // 2):
        both = jnp.where(low, outside[2 * pair], pltpu.roll(outside[2 * pair + 1], SLAB, 1))
        rest_ref[:, pair * LANES : (pair + 1) * LANES] = both.astype(jnp.bfloat16)


def group_of_lane(rows, width, groups):
    lane = lax.broadcasted_iota(jnp.int32, (rows, width), 1)
    return (lane % LANES) // (LANES // groups)


def tokens_of(seqs, dye_ref, toep_ref, rest_ref, out_ref, block_len):
    groups = toep_ref.shape[0] // SLAB
    taps = toep_ref.shape[1]
    starts = [seq * block_len + row for seq in seqs for row in range(0, block_len, SLAB)]

    def windows(at, size):
        return jnp.concatenate(
            [dye_ref[pl.ds(pl.multiple_of(start + at, SLAB), size)] for start in starts], axis=1
        )

    group_in = group_of_lane(SLAB, len(starts) * LANES, groups)
    after = windows(taps, SLAB)
    after = [jnp.where(group_in == group, after, jnp.zeros_like(after)) for group in range(groups)]
    full = jnp.dot(toep_ref[...], windows(0, taps), preferred_element_type=jnp.float32)
    rest = jnp.dot(
        rest_ref[...], jnp.concatenate(after, axis=0), preferred_element_type=jnp.float32
    )
    total = full[:SLAB]
    for group in range(1, groups):
        total = jnp.where(group_in == group, full[group * SLAB : (group + 1) * SLAB], total)
    total = (total + rest).astype(jnp.bfloat16)
    for index in range(len(starts)):
        columns = slice(index * LANES, (index + 1) * LANES)
        out_ref[index * SLAB : (index + 1) * SLAB] = total[:, columns]


def inputs_kernel(n_seq, taps_here, *refs):
    chips = n_seq // 2
    in_refs = refs[:chips]
    filt_ref, sides_ref, x_ref = refs[chips:]
    groups = sides_ref.shape[0]
    per_group = LANES // groups
    place_inputs(in_refs, taps_here, x_ref, filt_ref)
    pairs = x_ref.shape[0] // (2 * STEP)
    inputs = x_ref[...].T
    for group in range(groups):
        own = slice(group * per_group, (group + 1) * per_group)
        sides = jnp.concatenate(
            [inputs[own, pair * LANES : (pair + 1) * LANES] for pair in range(pairs)], axis=0
        ).T
        sides_ref[group] = jnp.concatenate([sides[:STEP], sides[STEP:]], axis=1)


def first_kernel(n_seq, taps_here, far, near, dy_ref, filt_ref, sides_ref, *refs):
    chips = n_seq // 2
    dye_ref, taps_ref, toep_ref, rest_ref, far_ref, near_ref, turned_ref = refs
    tokens = dy_ref.shape[0]
    groups = EXTRA // 2
    taps = n_seq * taps_here
    reach = taps + LANES
    per_group = LANES // groups
    chip, core, _ = place()

    dye_ref[:tokens] = dy_ref[...]
    dye_ref[tokens:] = dy_ref[:reach]

    pairs = tokens // (2 * STEP)
    wide = (pairs - 1) * LANES + reach
    for odd in range(2):
        turned_ref[odd] = dye_ref[odd * STEP : odd * STEP + wide].T
    toeplitz_rows(filt_ref, toep_ref, rest_ref)
    products = []
    for group in range(groups):
        own = slice(group * per_group, (group + 1) * per_group)
        windows = jnp.concatenate(
            [
                turned_ref[odd, own, pair * LANES : pair * LANES + reach]
                for odd in range(2)
                for pair in range(pairs)
            ],
            axis=0,
        )
        products.append(jnp.dot(sides_ref[group], windows, preferred_element_type=jnp.float32))

    block_len = tokens // n_seq
    seqs = [2 * (chip ^ far) + (core ^ flip) for flip in range(2)]
    tokens_of(seqs, dye_ref, toep_ref, rest_ref, far_ref, block_len)
    seqs = [2 * (chip ^ bits) + (core ^ 1) for bits in near]
    tokens_of(seqs, dye_ref, toep_ref, rest_ref, near_ref, block_len)
    eights = []
    for lags in products:
        rows = lags[:8]
        for high in range(1, STEP // 8):
            rows = rows + roll_left(lags[8 * high : 8 * high + 8], 8 * high)
        eights.append(rows)
    skew = jnp.concatenate(eights, axis=0)
    row_in = lax.broadcasted_iota(jnp.int32, skew.shape, 0) % 8
    for bit in (1, 2, 4):
        skew = jnp.where((row_in & bit) != 0, roll_left(skew, bit), skew)
    dh = skew.reshape(groups, 8, reach).sum(axis=1)[:, :taps]

    high = dh.astype(jnp.bfloat16).astype(jnp.float32)
    rest = dh - high
    low = lax.broadcasted_iota(jnp.int32, (groups, LANES), 1) < taps_here
    for to_chip in range(chips):
        columns = slice(to_chip * LANES, (to_chip + 1) * LANES)
        top, bottom = high[:, columns], rest[:, columns]
        even = jnp.where(low, top, pltpu.roll(bottom, taps_here, 1))
        odd = jnp.where(low, pltpu.roll(top, taps_here, 1), bottom)
        mine = jnp.where(core == 0, even, odd)
        other = jnp.where(core == 0, odd, even)
        taps_ref[to_chip] = jnp.concatenate([mine, other], axis=0).astype(jnp.bfloat16)

    far_ref[2 * block_len :] = taps_ref[chip ^ far]
    near_ref[len(near) * block_len :] = stacked([half_of(taps_ref[chip ^ bits], 1) for bits in near])


def half_of(taps, flip):
    groups = EXTRA // 2
    return taps.astype(jnp.float32)[flip * groups : (flip + 1) * groups]


def stacked(rows):
    return jnp.concatenate(rows, axis=0).astype(jnp.bfloat16)


def near_kernel(masks, dye_ref, toep_ref, rest_ref, taps_ref, out_ref):
    chip, core, _ = place()
    block_len = (out_ref.shape[0] - len(masks) * EXTRA // 2) // len(masks)
    seqs = [2 * (chip ^ bits) + core for bits in masks]
    tokens_of(seqs, dye_ref, toep_ref, rest_ref, out_ref, block_len)
    out_ref[len(masks) * block_len :] = stacked(
        [half_of(taps_ref[chip ^ bits], 0) for bits in masks]
    )


def near_pieces_kernel(keep_ref, got_ref, *out_refs):
    _, core, _ = place()
    count = len(out_refs)
    block_len = (out_refs[0].shape[0] - EXTRA) // 2
    groups = EXTRA // 2
    keep_taps = keep_ref[count * block_len :].astype(jnp.float32)
    got_taps = got_ref[count * block_len :].astype(jnp.float32)
    taps = [
        stacked(
            [value[index * groups : (index + 1) * groups] for value in (keep_taps, got_taps)]
        )
        for index in range(count)
    ]
    for index, out_ref in enumerate(out_refs):
        other = (index + 1) % count
        out_ref[:block_len] = keep_ref[rows_at((index + core) % count, block_len)]
        out_ref[block_len : 2 * block_len] = got_ref[rows_at((index + core) % count, block_len)]
        out_ref[2 * block_len :] = jnp.where(core == 0, taps[index], taps[other])


def own_kernel(dye_ref, toep_ref, rest_ref, taps_ref, out_ref):
    chip, core, _ = place()
    block_len = (out_ref.shape[0] - EXTRA) // 2
    seqs = [2 * chip + (core ^ flip) for flip in range(2)]
    tokens_of(seqs, dye_ref, toep_ref, rest_ref, out_ref, block_len)
    out_ref[2 * block_len :] = taps_ref[chip]


def swap_kernel(*refs):
    *in_refs, out_ref = refs
    block_len = (in_refs[0].shape[0] - EXTRA) // 2
    for index, in_ref in enumerate(in_refs):
        out_ref[index * block_len : (index + 1) * block_len] = in_ref[block_len : 2 * block_len]
    out_ref[len(in_refs) * block_len :] = stacked(
        [half_of(in_ref[2 * block_len :], 1) for in_ref in in_refs]
    )


def unpack_kernel(masks, *refs):
    *near_refs, own_ref, far_ref, swapped_ref, dx_ref, dh_ref, rows_ref = refs
    chip, core, _ = place()
    block_len = dx_ref.shape[0]
    taps_here, groups_here = dh_ref.shape
    groups = EXTRA // 2

    def put(from_chip, flip, tokens, taps):
        source = 2 * from_chip + (core ^ flip)
        dx_ref[:, pl.ds(pl.multiple_of(source * LANES, LANES), LANES)] = tokens
        rows_ref[pl.ds(pl.multiple_of(source * groups, groups), groups)] = taps + pltpu.roll(
            taps, taps_here, 1
        )

    swapped_taps = swapped_ref[2 * block_len :]
    for index, ref in enumerate((own_ref, far_ref)):
        put(chip ^ masks[index], 0, ref[:block_len], half_of(ref[2 * block_len :], 0))
        rows = swapped_ref[index * block_len : (index + 1) * block_len]
        put(chip ^ masks[index], 1, rows, half_of(swapped_taps, index))
    near = masks[2:]
    for index, ref in enumerate(near_refs):
        bits = jnp.where(core == 0, near[index], near[(index + 1) % len(near)])
        for flip in range(2):
            rows = ref[flip * block_len : (flip + 1) * block_len]
            put(chip ^ bits, flip, rows, half_of(ref[2 * block_len :], flip))
    dh_ref[...] = rows_ref[...].T[:taps_here]


def local_call(kernel, out_shape, operands, name, scratch=()):
    whole = pl.BlockSpec(memory_space=pltpu.VMEM)
    return pl.pallas_call(
        kernel,
        out_shape=out_shape,
        in_specs=[whole] * len(operands),
        out_specs=[whole] * len(out_shape),
        scratch_shapes=scratch,
        compiler_params=pltpu.CompilerParams(vmem_limit_bytes=VMEM_LIMIT),
        name=name,
    )(*operands)


def by_channels(n_seq, n_chan, out_grads, layer_inputs, filters):
    rows = out_grads.shape[0]
    block_len = layer_inputs.shape[0]
    taps_here, groups_here = filters.shape
    groups = groups_here // n_seq
    tokens = n_seq * block_len
    taps = n_seq * taps_here
    chips = n_seq // 2
    masks = partners(chips)

    def half(*shape):
        return jax.ShapeDtypeStruct(shape, jnp.bfloat16)

    unit = half(2 * block_len + EXTRA, LANES)
    x_other = xor_permute(layer_inputs, "seq", 1)
    f_other = xor_permute(filters, "seq", 1)
    (dy,) = local_call(
        functools.partial(fan_grads_kernel, n_seq),
        [half(n_seq * n_chan, rows, LANES)],
        (out_grads,),
        "fan_grads",
    )
    dy = lax.all_to_all(dy, ("seq", "chan"), split_axis=0, concat_axis=0, tiled=True)
    pieces = local_call(
        fan_inputs_kernel,
        [unit] * chips,
        (layer_inputs, x_other, filters, f_other),
        "fan_inputs",
        [pltpu.VMEM((2, groups_here, LANES), jnp.float32)],
    )
    near = masks[2:]
    near_shape = half(len(near) * (block_len + EXTRA // 2), LANES)
    by_chip, sides = local_call(
        functools.partial(inputs_kernel, n_seq, taps_here),
        [
            jax.ShapeDtypeStruct((chips, groups, LANES), jnp.float32),
            half(groups, STEP, tokens * LANES // (groups * STEP)),
        ],
        fan_out(pieces, "seq", 2),
        "inputs",
        [pltpu.VMEM((tokens, LANES), jnp.bfloat16)],
    )
    dye, tap_parts, toeplitz, outside, far, send = local_call(
        functools.partial(first_kernel, n_seq, taps_here, masks[1], near),
        [
            half(tokens + taps + LANES, LANES),
            half(chips, EXTRA, LANES),
            half(groups * SLAB, taps),
            half(SLAB, groups * SLAB),
            unit,
            near_shape,
        ],
        (dy.reshape(tokens, LANES), by_chip, sides),
        "first",
        [pltpu.VMEM((2, LANES, tokens + taps), jnp.bfloat16)],
    )
    far = xor_permute(far, "seq", 2 * masks[1])
    got = xor_permute(send, "seq", 1)
    (keep,) = local_call(
        functools.partial(near_kernel, near),
        [near_shape],
        (dye, toeplitz, outside, tap_parts),
        "near_keep",
    )
    pieces = local_call(near_pieces_kernel, [unit] * len(near), (keep, got), "near_pieces")
    pieces = [
        turned_permute(piece, "seq", [2 * bits for bits in near[index:] + near[:index]])
        for index, piece in enumerate(pieces)
    ]
    far, tap_parts = lax.optimization_barrier((far, tap_parts))
    (own,) = local_call(own_kernel, [unit], (dye, toeplitz, outside, tap_parts), "own")
    (send,) = local_call(
        swap_kernel, [half(2 * block_len + EXTRA, LANES)], (own, far), "swap"
    )
    return local_call(
        functools.partial(unpack_kernel, masks),
        [
            half(block_len, n_seq * LANES),
            jax.ShapeDtypeStruct((taps_here, groups_here), jnp.float32),
        ],
        (*pieces, own, far, xor_permute(send, "seq", 1)),
        "unpack",
        [pltpu.VMEM((groups_here, LANES), jnp.float32)],
    )


def solution(mesh):
    n_seq, n_chan = mesh.shape["seq"], mesh.shape["chan"]

    def on_device(out_grads, layer_inputs, filters):
        taps_here, groups_here = filters.shape
        fits = (
            n_seq == 8
            and n_chan in (2, 4, 8)
            and layer_inputs.shape[1] == n_seq * LANES
            and groups_here == 8 * n_seq
            and 2 * taps_here == LANES
            and out_grads.shape[0] % 16 == 0
            and layer_inputs.shape[0] % SLAB == 0
            and layer_inputs.shape[0] == 2 * STEP
            and n_seq * taps_here + LANES <= n_seq * layer_inputs.shape[0]
        )
        if fits:
            return tuple(by_channels(n_seq, n_chan, out_grads, layer_inputs, filters))
        return by_tokens(out_grads, layer_inputs, filters)

    in_specs = (P(("seq", "chan"), None), P("seq", "chan"), P("seq", "chan"))
    out_specs = (P("seq", "chan"), P("seq", "chan"))
    return jax.shard_map(
        on_device, mesh=mesh, in_specs=in_specs, out_specs=out_specs, check_vma=False
    )
```
